32 devices in a mesh: rep: 4 (over y, x), shard: 8 (over z, core).
Axes of the slice: x: 2, y: 2, z: 4, core: 2. Of those that a mesh axis runs over, the one named last changes fastest.
Arguments:
- x_prompt: bfloat16 [8, 1024, 2048], P('rep', 'shard'), may hold values from -6 to 6
- x_cont: bfloat16 [8192, 2048], P(('rep', 'shard')), may hold values from -6 to 6
- teacher_prompt: bfloat16 [8, 1024, 2048], P('rep', 'shard'), may hold values from -6 to 6
- teacher_cont: bfloat16 [8192, 2048], P(('rep', 'shard')), may hold values from -6 to 6
- valid_mask: int32 [64, 128], P(('rep', 'shard')), may hold values from 0 to 1, as said below
- group_of: int32 [64], P(('rep', 'shard')), may hold values from 0 to 1
- ln1_gain: bfloat16 [2048], P('shard'), may hold values from 0.5 to 1.5
- ln1_bias: bfloat16 [2048], P('shard'), may hold values from -4 to 4
- w_qkv: bfloat16 [2048, 6144], P('shard'), may hold values from -0.125 to 0.125
- q_bias: bfloat16 [2048], P('shard'), may hold values from -4 to 4
- v_bias: bfloat16 [2048], P('shard'), may hold values from -4 to 4
- w_out: bfloat16 [2048, 2048], P('shard'), may hold values from -0.375 to 0.375
- out_bias: bfloat16 [2048], P('shard'), may hold values from -4 to 4
- ln2_gain: bfloat16 [2048], P('shard'), may hold values from 0.5 to 1.5
- ln2_bias: bfloat16 [2048], P('shard'), may hold values from -4 to 4
- w_up: bfloat16 [2048, 8192], P('shard'), may hold values from -0.125 to 0.125
- up_bias: bfloat16 [8192], P('shard'), may hold values from -4 to 4
- w_down: bfloat16 [8192, 2048], P('shard'), may hold values from -0.0625 to 0.0625
- down_bias: bfloat16 [2048], P('shard'), may hold values from -4 to 4
Outputs:
- out_prompt: bfloat16 [8, 1024, 2048], P('rep', 'shard')
- out_cont: bfloat16 [8192, 2048], P(('rep', 'shard'))
- grad_prompt: float32 [8, 1024, 2048], P('rep', 'shard')
- grad_cont: float32 [8192, 2048], P(('rep', 'shard'))
- grad_ln1_gain: float32 [2048], P('shard')
- grad_ln1_bias: float32 [2048], P('shard')
- grad_w_qkv: float32 [2048, 6144], P('shard')
- grad_q_bias: float32 [2048], P('shard')
- grad_v_bias: float32 [2048], P('shard')
- grad_w_out: float32 [2048, 2048], P('shard')
- grad_out_bias: float32 [2048], P('shard')
- grad_ln2_gain: float32 [2048], P('shard')
- grad_ln2_bias: float32 [2048], P('shard')
- grad_w_up: float32 [2048, 8192], P('shard')
- grad_up_bias: float32 [8192], P('shard')
- grad_w_down: float32 [8192, 2048], P('shard')
- grad_down_bias: float32 [2048], P('shard')
The draws below stay inside these ranges and needn't reach their ends.
Inputs may be any that keep to these rules, and one draw needn't show every extreme that they name: Each row of valid_mask holds ones on a prefix of one or more of its 128 positions and zeros after it.
All inputs are finite; a program needn't handle non-finite values.
Results may differ from the reference program's by a relative error of at most 0.011.
Values may be sent and summed in bfloat16 or wider, within the bound.
A program may use at most 512 MiB of HBM per device.

```python
import jax
import jax.numpy as jnp
from jax import lax

D = 2048
FF = 8192
HEADS = 16
HEAD_DIM = 128
P_SIZE = 1024
C = 128
PROMPTS = 2
CONTS = 16
CONTS_ALL = 64
GROUPS_ALL = 8
TOTAL = 16384
N_REP = 4


def draw_valid_mask(key, part):
    key = jax.random.fold_in(key, 3)
    position_ids = jnp.arange(CONTS_ALL, dtype=jnp.int32)
    top_length = C // 4 + (C - C // 4) * position_ids // max(CONTS_ALL - 1, 1)
    least_length = jnp.maximum(top_length // 2, 1)
    length = jax.random.randint(key, (CONTS_ALL,), least_length, top_length + 1)
    return (jnp.arange(C, dtype=jnp.int32)[None, :] < length[:, None]).astype(jnp.int32)


def touch_ends(values, stream_key, smallest, high):
    longest = values.shape.index(max(values.shape))
    spots = []
    for shift in (0, 1):
        where = [jax.random.randint(jax.random.fold_in(stream_key, axis), (), 0, length) for axis, length in enumerate(values.shape)]
        where[longest] = (where[longest] + shift) % values.shape[longest]
        spots.append(tuple(where))
    return values.at[spots[0]].set(smallest).at[spots[1]].set(high)


def level_of(own_key, shape, cuts, least, high):
    loudness, own = 1.0, jax.random.fold_in(own_key, 6)
    for position, parts in cuts:
        heights = jnp.exp(jax.random.uniform(jax.random.fold_in(own, position), (parts,), jnp.float32, least / len(cuts), high / len(cuts)))
        loudness = loudness * jnp.repeat(heights, shape[position] // parts).reshape([-1 if axis == position else 1 for axis in range(len(shape))])
    return loudness


def bell_draw(rng, extent, scale, most, cuts=(), kind=jnp.bfloat16):
    values = jax.random.normal(rng, extent, jnp.float32) * scale
    if len(cuts) > 0:
        values = level_of(rng, extent, cuts, -0.22, 0.18) * values
    return jnp.clip(values, min=-most, max=most).astype(kind)


def setup_inputs(seed: int = 0) -> dict:
    keys = jax.random.split(jax.random.key(seed), 20)
    return {
        "x_prompt": bell_draw(keys[0], (GROUPS_ALL, P_SIZE, D), 1.0, 6.0, ((0, 4), (1, 8))),
        "x_cont": bell_draw(keys[1], (CONTS_ALL * C, D), 1.0, 6.0, ((0, 32),)),
        "teacher_prompt": bell_draw(keys[2], (GROUPS_ALL, P_SIZE, D), 1.0, 6.0, ((0, 4), (1, 8))),
        "teacher_cont": bell_draw(keys[3], (CONTS_ALL * C, D), 1.0, 6.0, ((0, 32),)),
        "valid_mask": draw_valid_mask(jax.random.fold_in(keys[19], 71), 0),
        "group_of": touch_ends(jax.random.randint(keys[5], (CONTS_ALL,), 0, PROMPTS), jax.random.fold_in(keys[5], 1), 0, PROMPTS - 1).astype(jnp.int32),
        "ln1_gain": jnp.clip(1.0 + 0.1 * jax.random.normal(keys[6], (D,), jnp.float32), 0.5, 1.5).astype(jnp.bfloat16),
        "ln1_bias": bell_draw(keys[7], (D,), 0.3, 4.0, ((0, 8),)),
        "w_qkv": bell_draw(keys[8], (D, 3 * D), D ** -0.5, 0.125, ((0, 8),)),
        "q_bias": bell_draw(keys[9], (D,), 0.3, 4.0, ((0, 8),)),
        "v_bias": bell_draw(keys[10], (D,), 0.3, 4.0, ((0, 8),)),
        "w_out": bell_draw(keys[11], (D, D), (D // 8) ** -0.5, 0.375, ((0, 8),)),
        "out_bias": bell_draw(keys[12], (D,), 0.3, 4.0, ((0, 8),)),
        "ln2_gain": jnp.clip(1.0 + 0.1 * jax.random.normal(keys[13], (D,), jnp.float32), 0.5, 1.5).astype(jnp.bfloat16),
        "ln2_bias": bell_draw(keys[14], (D,), 0.3, 4.0, ((0, 8),)),
        "w_up": bell_draw(keys[15], (D, FF), D ** -0.5, 0.125, ((0, 8),)),
        "up_bias": bell_draw(keys[16], (FF,), 0.3, 4.0, ((0, 8),)),
        "w_down": bell_draw(keys[17], (FF, D), FF ** -0.5, 0.0625, ((0, 8),)),
        "down_bias": bell_draw(keys[18], (D,), 0.3, 4.0, ((0, 8),)),
    }


@jax.custom_vjp
def low(v):
    return lax.optimization_barrier(v.astype(jnp.bfloat16)).astype(jnp.float32)

@jax.custom_vjp
def low_back(v):
    return v

def low_keep(v):
    return (low(v), None)

def low_pass(kept, grad):
    return (grad,)

def back_keep(v):
    return (v, None)

def back_low(kept, grad):
    return (low(grad),)
low.defvjp(low_keep, low_pass)
low_back.defvjp(back_keep, back_low)
epsilon = 1e-05
gelu_coef = 0.7978845608028654
highest = lax.Precision.HIGHEST

def gelu_tanh(values):
    return 0.5 * values * (1.0 + jnp.tanh(gelu_coef * (values + 0.044715 * values * values * values)))

def layer_norm(inputs, norm_gain, norm_shift):
    centered = inputs - lax.optimization_barrier(jnp.mean(inputs, axis=-1, keepdims=True))
    variance = lax.optimization_barrier(jnp.mean(centered * centered, axis=-1, keepdims=True))
    return centered * lax.rsqrt(variance + epsilon) * norm_gain + norm_shift

def product(left, right):
    return jnp.dot(left, right, precision=highest, preferred_element_type=jnp.float32)

def attend(queries, key_rows, value_rows, query_pos, key_pos):
    query_heads = queries.reshape(-1, HEADS, HEAD_DIM)
    key_heads = key_rows.reshape(-1, HEADS, HEAD_DIM)
    value_heads = value_rows.reshape(-1, HEADS, HEAD_DIM)
    logits = jnp.einsum('qhe,khe->hqk', query_heads, key_heads, precision=highest) * HEAD_DIM ** (-0.5)
    slopes = 2.0 ** (-8.0 * (jnp.arange(HEADS, dtype=jnp.float32) + 1.0) / HEADS)
    distance = (query_pos[:, None] - key_pos[None, :]).astype(jnp.float32)
    logits = logits - slopes[:, None, None] * distance[None, :, :]
    allowed = key_pos[None, :] <= query_pos[:, None]
    scores = low_back(jnp.where(allowed[None, :, :], logits, -1e+30))
    shifted = scores - lax.optimization_barrier(jnp.max(scores, axis=-1, keepdims=True))
    expo_terms = jnp.exp(shifted)
    soft_weights = low(expo_terms / lax.optimization_barrier(jnp.sum(expo_terms, axis=-1, keepdims=True)))
    mixed_out = jnp.einsum('hqk,khe->qhe', soft_weights, value_heads, precision=highest)
    return mixed_out.reshape(-1, D)

def block_forward(prompt_x, cont_x, chosen_prompts, params):
    gain_one, shift_one, w_qkv, q_bias, v_bias, w_out, out_bias, gain_two, shift_two, w_up, up_bias, w_down, down_bias = params
    prompt_total = PROMPTS * P_SIZE
    inputs = jnp.concatenate([prompt_x.reshape(prompt_total, D), cont_x.reshape(CONTS * C, D)], axis=0)
    normed = low(layer_norm(inputs, gain_one, shift_one))
    joined = product(normed, w_qkv)
    queries = low(low_back(joined[:, :D] + q_bias))
    key_rows = low(low_back(joined[:, D:2 * D]))
    value_rows = low(low_back(joined[:, 2 * D:] + v_bias))
    prompt_q = queries[:prompt_total].reshape(PROMPTS, P_SIZE, D)
    prompt_k = key_rows[:prompt_total].reshape(PROMPTS, P_SIZE, D)
    prompt_v = value_rows[:prompt_total].reshape(PROMPTS, P_SIZE, D)
    cont_q = queries[prompt_total:].reshape(CONTS, C, D)
    cont_k = key_rows[prompt_total:].reshape(CONTS, C, D)
    cont_v = value_rows[prompt_total:].reshape(CONTS, C, D)
    prompt_pos = jnp.arange(P_SIZE, dtype=jnp.int32)
    cont_pos = P_SIZE + jnp.arange(C, dtype=jnp.int32)
    joint_pos = jnp.concatenate([prompt_pos, cont_pos])

    def prompt_block(pieces):
        return attend(pieces[0], pieces[1], pieces[2], prompt_pos, prompt_pos)

    def cont_block(pieces):
        chosen = pieces[3].astype(jnp.int32)
        keys_all = jnp.concatenate([lax.dynamic_index_in_dim(prompt_k, chosen, 0, keepdims=False), pieces[1]], axis=0)
        values_all = jnp.concatenate([lax.dynamic_index_in_dim(prompt_v, chosen, 0, keepdims=False), pieces[2]], axis=0)
        return attend(pieces[0], keys_all, values_all, cont_pos, joint_pos)
    prompt_out = lax.map(jax.checkpoint(prompt_block), (prompt_q, prompt_k, prompt_v))
    cont_out = lax.map(jax.checkpoint(cont_block), (cont_q, cont_k, cont_v, chosen_prompts))
    attended = low(low_back(jnp.concatenate([prompt_out.reshape(prompt_total, D), cont_out.reshape(CONTS * C, D)], axis=0)))
    middle = inputs + low_back(product(attended, w_out) + out_bias)
    normed_two = low(layer_norm(middle, gain_two, shift_two))
    upward = low_back(product(normed_two, w_up) + up_bias)
    active = low(gelu_tanh(upward))
    result = middle + low_back(product(active, w_down) + down_bias)
    return (result[:prompt_total].reshape(PROMPTS, P_SIZE, D), result[prompt_total:].reshape(CONTS, C, D))

def reference(x_prompt, x_cont, teacher_prompt, teacher_cont, valid_mask, group_of, ln1_gain, ln1_bias, w_qkv, q_bias, v_bias, w_out, out_bias, ln2_gain, ln2_bias, w_up, up_bias, w_down, down_bias):
    params = tuple((weight.astype(jnp.float32) for weight in (ln1_gain, ln1_bias, w_qkv, q_bias, v_bias, w_out, out_bias, ln2_gain, ln2_bias, w_up, up_bias, w_down, down_bias)))
    valid_total = jnp.sum(valid_mask.astype(jnp.float32)) + N_REP * PROMPTS * P_SIZE
    loss_scale = TOTAL / valid_total
    prompt_in = x_prompt.astype(jnp.float32).reshape(N_REP, PROMPTS, P_SIZE, D)
    cont_in = x_cont.astype(jnp.float32).reshape(N_REP, CONTS, C, D)
    prompt_goal = teacher_prompt.astype(jnp.float32).reshape(N_REP, PROMPTS, P_SIZE, D)
    cont_goal = teacher_cont.astype(jnp.float32).reshape(N_REP, CONTS, C, D)
    cont_weight = valid_mask.astype(jnp.float32).reshape(N_REP, CONTS, C)
    chosen_all = group_of.astype(jnp.int32).reshape(N_REP, CONTS)

    def replica_step(totals, pieces):
        prompt_x, cont_x, prompt_t, cont_t, cont_w, chosen = pieces

        def loss_of(prompt_arg, cont_arg, param_arg):
            prompt_y, cont_y = block_forward(prompt_arg, cont_arg, chosen, param_arg)
            prompt_err = prompt_y - prompt_t
            cont_err = cont_y - cont_t
            squares = jnp.sum(prompt_err * prompt_err) + jnp.sum(cont_w[:, :, None] * cont_err * cont_err)
            return (0.5 * loss_scale * squares, (prompt_y, cont_y))
        loss_value, backward, outputs = jax.vjp(loss_of, prompt_x, cont_x, params, has_aux=True)
        prompt_grad, cont_grad, param_grads = backward(jnp.ones((), jnp.float32))
        totals = tuple((earlier + added for earlier, added in zip(totals, param_grads)))
        return (totals, (outputs[0].astype(jnp.bfloat16), outputs[1].astype(jnp.bfloat16), prompt_grad, cont_grad))
    initial = tuple((jnp.zeros_like(weight) for weight in params))
    totals, stacked = lax.scan(replica_step, initial, (prompt_in, cont_in, prompt_goal, cont_goal, cont_weight, chosen_all))
    out_prompt = stacked[0].reshape(GROUPS_ALL, P_SIZE, D)
    out_cont = stacked[1].reshape(CONTS_ALL * C, D)
    grad_prompt = stacked[2].reshape(GROUPS_ALL, P_SIZE, D)
    grad_cont = stacked[3].reshape(CONTS_ALL * C, D)
    return (out_prompt, out_cont, grad_prompt, grad_cont, totals[0], totals[1], totals[2], totals[3], totals[4], totals[5], totals[6], totals[7], totals[8], totals[9], totals[10], totals[11], totals[12])
```

```python
import functools

import jax
import jax.numpy as jnp
from jax import lax
from jax.experimental import pallas as pl
from jax.experimental.pallas import tpu as pltpu
from jax.sharding import PartitionSpec as P

HEAD_DIM = 128
AXES = ("rep", "shard")


epsilon = 1e-05
gelu_coef = 0.7978845608028654


def gelu_tanh(values):
    return (
        0.5 * values * (1.0 + jnp.tanh(gelu_coef * (values + 0.044715 * values * values * values)))
    )


def norm_forward(inputs, norm_gain, norm_shift):
    centered = inputs - jnp.mean(inputs, axis=-1, keepdims=True)
    variance = jnp.mean(centered * centered, axis=-1, keepdims=True)
    inverse = lax.rsqrt(variance + epsilon)
    unit_rows = centered * inverse
    return (unit_rows * norm_gain + norm_shift, unit_rows, inverse)


def norm_backward(upstream, unit_rows, inverse, norm_gain):
    scaled = upstream * norm_gain
    centered = (
        scaled
        - jnp.mean(scaled, axis=-1, keepdims=True)
        - unit_rows * jnp.mean(scaled * unit_rows, axis=-1, keepdims=True)
    )
    return (centered * inverse, jnp.sum(upstream * unit_rows, axis=0), jnp.sum(upstream, axis=0))


def cross(left, right):
    return lax.dot_general(
        left, right, (((0,), (0,)), ((), ())), preferred_element_type=jnp.float32
    )


def back_product(left, right):
    return lax.dot_general(
        left, right, (((1,), (1,)), ((), ())), preferred_element_type=jnp.float32
    )


def score_table(query_heads, key_heads, query_pos, key_pos):
    head_count = query_heads.shape[2]
    logits = jnp.einsum(
        "bqhe,bkhe->bhqk", query_heads, key_heads, preferred_element_type=jnp.float32
    ) * query_heads.shape[3] ** (-0.5)
    slopes = 2.0 ** (-8.0 * (jnp.arange(head_count, dtype=jnp.float32) + 1.0) / head_count)
    distance = (query_pos[:, :, None] - key_pos[:, None, :]).astype(jnp.float32)
    logits = logits - slopes[None, :, None, None] * distance[:, None, :, :]
    allowed = (key_pos[:, None, :] <= query_pos[:, :, None])[:, None, :, :]
    return jnp.where(allowed, logits, -1e30)


def attend_forward(query_heads, key_heads, value_heads, query_pos, key_pos):
    logits = score_table(query_heads, key_heads, query_pos, key_pos)
    largest = jnp.max(logits, axis=-1, keepdims=True)
    expo_terms = jnp.exp(logits - largest)
    totals = jnp.sum(expo_terms, axis=-1, keepdims=True)
    soft_weights = (expo_terms / totals).astype(jnp.bfloat16)
    mixed_out = jnp.einsum(
        "bhqk,bkhe->bqhe", soft_weights, value_heads, preferred_element_type=jnp.float32
    )
    return (mixed_out, largest + jnp.log(totals))


def attend_backward(
    query_heads, key_heads, value_heads, query_pos, key_pos, log_totals, mixed_grad
):
    logits = score_table(query_heads, key_heads, query_pos, key_pos)
    soft_weights = jnp.exp(logits - log_totals)
    weight_grad = jnp.einsum(
        "bqhe,bkhe->bhqk", mixed_grad, value_heads, preferred_element_type=jnp.float32
    )
    row_inner = jnp.sum(soft_weights * weight_grad, axis=-1, keepdims=True)
    logit_grad = (soft_weights * (weight_grad - row_inner)).astype(jnp.bfloat16)
    factor = query_heads.shape[3] ** (-0.5)
    query_grad = (
        jnp.einsum("bhqk,bkhe->bqhe", logit_grad, key_heads, preferred_element_type=jnp.float32)
        * factor
    )
    key_grad = (
        jnp.einsum("bhqk,bqhe->bkhe", logit_grad, query_heads, preferred_element_type=jnp.float32)
        * factor
    )
    value_grad = jnp.einsum(
        "bhqk,bqhe->bkhe",
        soft_weights.astype(jnp.bfloat16),
        mixed_grad,
        preferred_element_type=jnp.float32,
    )
    return (query_grad, key_grad, value_grad)


def send(block, target):
    replicas, shards = lax.axis_size("rep"), lax.axis_size("shard")
    pairs = []
    for r in range(replicas):
        for s in range(shards):
            r_to, z_to, c_to = target(r, s // 2, s % 2)
            pairs.append((r * shards + s, r_to * shards + 2 * z_to + c_to))
    return lax.ppermute(block, AXES, pairs)


def ring_next(block):
    levels = lax.axis_size("shard") // 2
    return send(block, lambda r, z, c: (r, (z + 1) % levels, c))


def swap_core(block):
    return send(block, lambda r, z, c: (r, z, 1 - c))


def bit_of(step, core):
    bits = lax.axis_size("rep").bit_length() - 1
    return step if core == 0 else bits - 1 - step


def swap_rep(block, step):
    return send(block, lambda r, z, c: (r ^ (1 << bit_of(step, c)), z, c))


def mask_lists():
    bits = lax.axis_size("rep").bit_length() - 1
    lists = []
    for core in range(2):
        masks = [0]
        for step in range(bits):
            masks += [m ^ (1 << bit_of(step, core)) for m in masks]
        lists.append(masks)
    return lists


def spread_rep(block):
    bits = lax.axis_size("rep").bit_length() - 1
    pieces = [block]
    for step in range(bits):
        pieces += [swap_rep(p, step) for p in pieces]
    return pieces


def rep_positions(core, r):
    lists = mask_lists()
    return [jnp.where(core == 0, a, b) ^ r for a, b in zip(*lists)]


def place_kernel(levels, replicas, own, *refs):
    count = (levels - 1) * replicas
    pieces, out = refs[:count], refs[count]
    local_sem, send_sem, recv_sem = refs[count + 1 :]
    r, s = lax.axis_index("rep"), lax.axis_index("shard")
    core, z = lax.rem(s, 2), lax.div(s, 2)
    other = {"shard": s + 1 - 2 * core}
    barrier = pltpu.get_barrier_semaphore()
    pl.semaphore_signal(barrier, inc=1, device_id=other, device_id_type=pl.DeviceIdType.MESH)
    pl.semaphore_wait(barrier, 1)
    lists = mask_lists()
    places = [(own, out.at[s])]
    for j in range(1, levels):
        owner = 2 * lax.rem(z - j + levels, levels) + core
        for k in range(replicas):
            q = jnp.where(core == 0, r ^ lists[0][k], r ^ lists[1][k])
            places.append((pieces[(j - 1) * replicas + k], out.at[owner, q]))
    copies = []
    for n, (source, target) in enumerate(places):
        copies.append(
            pltpu.make_async_remote_copy(
                src_ref=source,
                dst_ref=target,
                send_sem=send_sem.at[n],
                recv_sem=recv_sem.at[n],
                device_id=other,
                device_id_type=pl.DeviceIdType.MESH,
            )
        )
        copies.append(pltpu.make_async_copy(source, target, local_sem.at[n]))
    for copy in copies:
        copy.start()
    for copy in copies:
        copy.wait()


def gather_rows(local, collective_id):
    replicas, shards = lax.axis_size("rep"), lax.axis_size("shard")
    levels = shards // 2
    rows, columns = local.shape
    part = rows // replicas
    own = local.reshape(replicas, part, columns)
    piece = lax.dynamic_index_in_dim(own, lax.axis_index("rep"), 0, keepdims=False)
    pieces = []
    for _ in range(levels - 1):
        piece = ring_next(piece)
        pieces += spread_rep(piece)
    any_space = pl.BlockSpec(memory_space=pl.ANY)
    count = len(pieces) + 1
    full = pl.pallas_call(
        functools.partial(place_kernel, levels, replicas),
        out_shape=jax.ShapeDtypeStruct((shards, replicas, part, columns), local.dtype),
        in_specs=[any_space] * count,
        out_specs=any_space,
        scratch_shapes=[pltpu.SemaphoreType.DMA((count,))] * 3,
        compiler_params=pltpu.CompilerParams(collective_id=collective_id, has_side_effects=True),
        cost_estimate=pl.CostEstimate(
            flops=0, transcendentals=0, bytes_accessed=2 * shards * rows * columns * 2
        ),
    )(own, *pieces)
    return full.reshape(shards * rows, columns)


def pair_rows(block):
    return jnp.concatenate([block, swap_core(block)], axis=0)


def owned_columns(block):
    shards = lax.axis_size("shard")
    core = lax.rem(lax.axis_index("shard"), 2)
    rows, columns = block.shape
    width = columns // shards
    split = block.reshape(rows, shards // 2, 2, width)
    mine = lax.dynamic_index_in_dim(split, core, 2, keepdims=False)
    others = lax.dynamic_index_in_dim(split, 1 - core, 2, keepdims=False)
    half = (rows, columns // 2)
    return jnp.concatenate([mine.reshape(half), swap_core(others.reshape(half))], axis=0)


def add_low(left, right):
    return (left.astype(jnp.float32) + right.astype(jnp.float32)).astype(jnp.bfloat16)


def weight_gradient(left, right_pair):
    replicas, shards = lax.axis_size("rep"), lax.axis_size("shard")
    levels = shards // 2
    bits = replicas.bit_length() - 1
    r, s = lax.axis_index("rep"), lax.axis_index("shard")
    core, z = lax.rem(s, 2), lax.div(s, 2)
    total = cross(owned_columns(left), right_pair).astype(jnp.bfloat16)
    rows = total.shape[0] // levels
    columns = total.shape[1]
    part = rows // replicas
    total = total.reshape(levels, replicas, part, columns)
    lists = mask_lists()
    reversed_masks = []
    for c in range(2):
        masks = [0]
        for step in reversed(range(bits)):
            masks = masks + [m ^ (1 << bit_of(step, c)) for m in masks]
        reversed_masks.append(masks)
    held = [
        lax.dynamic_slice_in_dim(total, jnp.where(core == 0, a, b) ^ r, 1, 1)
        for a, b in zip(*reversed_masks)
    ]
    for step in range(bits):
        half = len(held) // 2
        held = [add_low(held[n], swap_rep(held[half + n], step)) for n in range(half)]
    plane = held[0].reshape(levels, part, columns)
    travelling = lax.dynamic_index_in_dim(plane, lax.rem(z + levels - 1, levels), 0, keepdims=False)
    for step in range(1, levels):
        arrived = ring_next(travelling)
        own = lax.dynamic_index_in_dim(
            plane, lax.rem(z + 2 * levels - 1 - step, levels), 0, keepdims=False
        )
        travelling = add_low(own, arrived)
    pieces = spread_rep(travelling)
    out = jnp.zeros((replicas, part, columns), jnp.float32)
    for piece, q in zip(pieces, rep_positions(core, r)):
        out = lax.dynamic_update_index_in_dim(out, piece.astype(jnp.float32), q, 0)
    return out.reshape(rows, columns)


def per_device(
    x_prompt,
    x_cont,
    teacher_prompt,
    teacher_cont,
    valid_mask,
    group_of,
    ln1_gain,
    ln1_bias,
    w_qkv,
    q_bias,
    v_bias,
    w_out,
    out_bias,
    ln2_gain,
    ln2_bias,
    w_up,
    up_bias,
    w_down,
    down_bias,
):
    shards = lax.axis_size("shard")
    replicas = lax.axis_size("rep")
    shard_index = lax.axis_index("shard")
    prompt_count, prompt_rows, width = x_prompt.shape
    cont_rows = x_cont.shape[0]
    cont_count, cont_len = valid_mask.shape
    prompt_len = prompt_rows * shards
    prompt_total = prompt_count * prompt_rows
    head_count = width // HEAD_DIM
    all_tokens = replicas * shards * (prompt_total + cont_rows)
    valid_local = jnp.sum(valid_mask.astype(jnp.float32)) + prompt_total
    valid_all = lax.psum(valid_local, ("rep", "shard"))
    loss_scale = all_tokens / valid_all
    qkv_full = gather_rows(w_qkv, 0)
    out_full = gather_rows(w_out, 1)
    up_full = gather_rows(w_up, 2)
    down_full = gather_rows(w_down, 3)
    vectors = (
        ln1_gain,
        ln1_bias,
        q_bias,
        v_bias,
        out_bias,
        ln2_gain,
        ln2_bias,
        up_bias,
        down_bias,
    )
    joint = lax.all_gather(jnp.concatenate(vectors)[None], "shard", axis=0, tiled=True)
    starts = [0]
    for vector in vectors:
        starts.append(starts[-1] + vector.shape[0])
    (
        gain_one,
        shift_one,
        bias_query,
        bias_value,
        bias_out,
        gain_two,
        shift_two,
        bias_up,
        bias_down,
    ) = [
        joint[:, begin:end].reshape(-1).astype(jnp.float32)
        for begin, end in zip(starts[:-1], starts[1:])
    ]
    inputs = jnp.concatenate([x_prompt.reshape(prompt_total, width), x_cont], axis=0).astype(
        jnp.float32
    )
    normed, unit_one, inverse_one = norm_forward(inputs, gain_one, shift_one)
    normed_low = normed.astype(jnp.bfloat16)
    joined = jnp.dot(normed_low, qkv_full, preferred_element_type=jnp.float32)
    queries = (joined[:, :width] + bias_query).astype(jnp.bfloat16)
    key_rows = joined[:, width : 2 * width].astype(jnp.bfloat16)
    value_rows = (joined[:, 2 * width :] + bias_value).astype(jnp.bfloat16)
    local_pairs = jnp.concatenate(
        [key_rows[:prompt_total], value_rows[:prompt_total]], axis=1
    ).reshape(prompt_count, prompt_rows, 2 * width)
    prompt_pairs = lax.all_gather(local_pairs, "shard", axis=1, tiled=True)
    prompt_keys = prompt_pairs[:, :, :width].reshape(prompt_count, prompt_len, head_count, HEAD_DIM)
    prompt_values = prompt_pairs[:, :, width:].reshape(
        prompt_count, prompt_len, head_count, HEAD_DIM
    )
    prompt_queries = queries[:prompt_total].reshape(prompt_count, prompt_rows, head_count, HEAD_DIM)
    prompt_qpos = jnp.broadcast_to(
        shard_index * prompt_rows + jnp.arange(prompt_rows, dtype=jnp.int32),
        (prompt_count, prompt_rows),
    )
    prompt_kpos = jnp.broadcast_to(
        jnp.arange(prompt_len, dtype=jnp.int32), (prompt_count, prompt_len)
    )
    prompt_mixed, prompt_lse = attend_forward(
        prompt_queries, prompt_keys, prompt_values, prompt_qpos, prompt_kpos
    )
    chosen = group_of[:, None, None]
    selected = jnp.broadcast_to(prompt_pairs[0], (cont_count,) + prompt_pairs.shape[1:])
    for prompt in range(1, prompt_count):
        selected = jnp.where(chosen == prompt, prompt_pairs[prompt], selected)
    own_keys = key_rows[prompt_total:].reshape(cont_count, cont_len, width)
    own_values = value_rows[prompt_total:].reshape(cont_count, cont_len, width)
    cont_keys = jnp.concatenate([selected[:, :, :width], own_keys], axis=1).reshape(
        cont_count, prompt_len + cont_len, head_count, HEAD_DIM
    )
    cont_values = jnp.concatenate([selected[:, :, width:], own_values], axis=1).reshape(
        cont_count, prompt_len + cont_len, head_count, HEAD_DIM
    )
    cont_queries = queries[prompt_total:].reshape(cont_count, cont_len, head_count, HEAD_DIM)
    cont_qpos = jnp.broadcast_to(
        prompt_len + jnp.arange(cont_len, dtype=jnp.int32), (cont_count, cont_len)
    )
    cont_kpos = jnp.broadcast_to(
        jnp.arange(prompt_len + cont_len, dtype=jnp.int32), (cont_count, prompt_len + cont_len)
    )
    cont_mixed, cont_lse = attend_forward(
        cont_queries, cont_keys, cont_values, cont_qpos, cont_kpos
    )
    attended = jnp.concatenate(
        [prompt_mixed.reshape(prompt_total, width), cont_mixed.reshape(cont_rows, width)], axis=0
    ).astype(jnp.bfloat16)
    middle = inputs + jnp.dot(attended, out_full, preferred_element_type=jnp.float32) + bias_out
    normed_two, unit_two, inverse_two = norm_forward(middle, gain_two, shift_two)
    normed_two_low = normed_two.astype(jnp.bfloat16)
    upward = jnp.dot(normed_two_low, up_full, preferred_element_type=jnp.float32) + bias_up
    active_low = gelu_tanh(upward).astype(jnp.bfloat16)
    result = middle + jnp.dot(active_low, down_full, preferred_element_type=jnp.float32) + bias_down
    out_prompt = (
        result[:prompt_total].reshape(prompt_count, prompt_rows, width).astype(jnp.bfloat16)
    )
    out_cont = result[prompt_total:].astype(jnp.bfloat16)
    targets = jnp.concatenate(
        [teacher_prompt.reshape(prompt_total, width), teacher_cont], axis=0
    ).astype(jnp.float32)
    weight_rows = jnp.concatenate(
        [jnp.ones((prompt_total,), jnp.float32), valid_mask.reshape(cont_rows).astype(jnp.float32)]
    )
    out_grad = (loss_scale * weight_rows)[:, None] * (result - targets)
    mlp_grad = out_grad.astype(jnp.bfloat16)
    grad_bias_down = jnp.sum(mlp_grad, axis=0, dtype=jnp.float32)
    active_grad = back_product(mlp_grad, down_full)
    unused_value, gelu_pull = jax.vjp(gelu_tanh, upward)
    upward_grad = gelu_pull(active_grad)[0].astype(jnp.bfloat16)
    grad_bias_up = jnp.sum(upward_grad, axis=0, dtype=jnp.float32)
    normed_two_grad = back_product(upward_grad, up_full)
    middle_step, grad_gain_two, grad_shift_two = norm_backward(
        normed_two_grad, unit_two, inverse_two, gain_two
    )
    middle_grad = out_grad + middle_step
    branch_grad = middle_grad.astype(jnp.bfloat16)
    grad_bias_out = jnp.sum(branch_grad, axis=0, dtype=jnp.float32)
    attended_grad = back_product(branch_grad, out_full).astype(jnp.bfloat16)
    prompt_og = attended_grad[:prompt_total].reshape(
        prompt_count, prompt_rows, head_count, HEAD_DIM
    )
    cont_og = attended_grad[prompt_total:].reshape(cont_count, cont_len, head_count, HEAD_DIM)
    prompt_qgrad, prompt_kgrad, prompt_vgrad = attend_backward(
        prompt_queries, prompt_keys, prompt_values, prompt_qpos, prompt_kpos, prompt_lse, prompt_og
    )
    cont_qgrad, cont_kgrad, cont_vgrad = attend_backward(
        cont_queries, cont_keys, cont_values, cont_qpos, cont_kpos, cont_lse, cont_og
    )
    cont_pair_grad = jnp.concatenate(
        [
            cont_kgrad[:, :prompt_len].reshape(cont_count, prompt_len, width),
            cont_vgrad[:, :prompt_len].reshape(cont_count, prompt_len, width),
        ],
        axis=2,
    )
    routed_grad = jnp.stack(
        [
            jnp.sum(jnp.where(chosen == prompt, cont_pair_grad, 0.0), axis=0)
            for prompt in range(prompt_count)
        ]
    )
    pair_grad = (
        jnp.concatenate(
            [
                prompt_kgrad.reshape(prompt_count, prompt_len, width),
                prompt_vgrad.reshape(prompt_count, prompt_len, width),
            ],
            axis=2,
        )
        + routed_grad
    )
    owned_pairs = lax.psum_scatter(
        pair_grad.astype(jnp.bfloat16)
        .reshape(prompt_count, shards, prompt_rows, 2 * width)
        .transpose(1, 0, 2, 3),
        "shard",
        scatter_dimension=0,
    ).astype(jnp.float32)
    query_part = jnp.concatenate(
        [prompt_qgrad.reshape(prompt_total, width), cont_qgrad.reshape(cont_rows, width)], axis=0
    )
    key_part = jnp.concatenate(
        [
            owned_pairs[:, :, :width].reshape(prompt_total, width),
            cont_kgrad[:, prompt_len:].reshape(cont_rows, width),
        ],
        axis=0,
    )
    value_part = jnp.concatenate(
        [
            owned_pairs[:, :, width:].reshape(prompt_total, width),
            cont_vgrad[:, prompt_len:].reshape(cont_rows, width),
        ],
        axis=0,
    )
    joined_grad = jnp.concatenate([query_part, key_part, value_part], axis=1).astype(jnp.bfloat16)
    grad_bias_query = jnp.sum(joined_grad[:, :width], axis=0, dtype=jnp.float32)
    grad_bias_value = jnp.sum(joined_grad[:, 2 * width :], axis=0, dtype=jnp.float32)
    normed_grad = back_product(joined_grad, qkv_full)
    input_step, grad_gain_one, grad_shift_one = norm_backward(
        normed_grad, unit_one, inverse_one, gain_one
    )
    input_grad = middle_grad + input_step
    summed_down = weight_gradient(active_low, pair_rows(mlp_grad))
    summed_up = weight_gradient(normed_two_low, pair_rows(upward_grad))
    summed_out = weight_gradient(attended, pair_rows(branch_grad))
    summed_qkv = weight_gradient(normed_low, pair_rows(joined_grad))
    vector_sums = lax.psum(
        (
            grad_gain_one,
            grad_shift_one,
            grad_bias_query,
            grad_bias_value,
            grad_bias_out,
            grad_gain_two,
            grad_shift_two,
            grad_bias_up,
            grad_bias_down,
        ),
        ("rep", "shard"),
    )
    owned_vectors = [
        lax.dynamic_slice_in_dim(
            vector, shard_index * (vector.shape[0] // shards), vector.shape[0] // shards
        )
        for vector in vector_sums
    ]
    grad_prompt = input_grad[:prompt_total].reshape(prompt_count, prompt_rows, width)
    grad_cont = input_grad[prompt_total:]
    return (
        out_prompt,
        out_cont,
        grad_prompt,
        grad_cont,
        owned_vectors[0],
        owned_vectors[1],
        summed_qkv,
        owned_vectors[2],
        owned_vectors[3],
        summed_out,
        owned_vectors[4],
        owned_vectors[5],
        owned_vectors[6],
        summed_up,
        owned_vectors[7],
        summed_down,
        owned_vectors[8],
    )


def solution(mesh):
    in_specs = (
        P("rep", "shard", None),
        P(("rep", "shard"), None),
        P("rep", "shard", None),
        P(("rep", "shard"), None),
        P(("rep", "shard"), None),
        P(("rep", "shard")),
        P("shard"),
        P("shard"),
        P("shard", None),
        P("shard"),
        P("shard"),
        P("shard", None),
        P("shard"),
        P("shard"),
        P("shard"),
        P("shard", None),
        P("shard"),
        P("shard", None),
        P("shard"),
    )
    out_specs = (
        P("rep", "shard", None),
        P(("rep", "shard"), None),
        P("rep", "shard", None),
        P(("rep", "shard"), None),
        P("shard"),
        P("shard"),
        P("shard", None),
        P("shard"),
        P("shard"),
        P("shard", None),
        P("shard"),
        P("shard"),
        P("shard"),
        P("shard", None),
        P("shard"),
        P("shard", None),
        P("shard"),
    )
    return jax.shard_map(
        per_device, mesh=mesh, in_specs=in_specs, out_specs=out_specs, check_vma=False
    )
```

```python
import functools

import jax
import jax.numpy as jnp
from jax import lax
from jax.experimental import pallas as pl
from jax.experimental.pallas import tpu as pltpu
from jax.sharding import PartitionSpec as P

HEAD_DIM = 128
AXES = ("rep", "shard")


epsilon = 1e-05
gelu_coef = 0.7978845608028654


def gelu_tanh(values):
    return (
        0.5 * values * (1.0 + jnp.tanh(gelu_coef * (values + 0.044715 * values * values * values)))
    )


def norm_forward(inputs, norm_gain, norm_shift):
    centered = inputs - jnp.mean(inputs, axis=-1, keepdims=True)
    variance = jnp.mean(centered * centered, axis=-1, keepdims=True)
    inverse = lax.rsqrt(variance + epsilon)
    unit_rows = centered * inverse
    return (unit_rows * norm_gain + norm_shift, unit_rows, inverse)


def norm_backward(upstream, unit_rows, inverse, norm_gain):
    scaled = upstream * norm_gain
    centered = (
        scaled
        - jnp.mean(scaled, axis=-1, keepdims=True)
        - unit_rows * jnp.mean(scaled * unit_rows, axis=-1, keepdims=True)
    )
    return (centered * inverse, jnp.sum(upstream * unit_rows, axis=0), jnp.sum(upstream, axis=0))


def cross(left, right):
    return lax.dot_general(
        left, right, (((0,), (0,)), ((), ())), preferred_element_type=jnp.float32
    )


def back_product(left, right):
    return lax.dot_general(
        left, right, (((1,), (1,)), ((), ())), preferred_element_type=jnp.float32
    )


def dot_last(left, right):
    return back_product(left, right)


def causal_scores(queries, keys, factor, slope, key_start, query_start, masked):
    scores = dot_last(queries, keys) * factor
    key_pos = key_start + lax.broadcasted_iota(jnp.int32, (1, keys.shape[0]), 1)
    scores = scores + slope * (key_pos - query_start).astype(jnp.float32)
    if masked:
        query_pos = query_start + lax.broadcasted_iota(jnp.int32, (queries.shape[0], 1), 0)
        scores = jnp.where(key_pos <= query_pos, scores, -1e30)
    return scores


def all_rows(ref, prompt):
    return ref[:, prompt].reshape(-1, ref.shape[-1])


def forward_kernel(sizes, places, slopes, q_ref, k_ref, v_ref, own_k_ref, own_v_ref, out_ref, lse_ref):
    prompt_count, prompt_rows, cont_count, cont_len = sizes
    prompt_total = prompt_count * prompt_rows
    prompt_len = k_ref.shape[0] * prompt_rows
    slope = slopes[pl.program_id(0)]
    factor = q_ref.shape[1] ** (-0.5)
    for p in range(prompt_count):
        rows = slice(p * prompt_rows, (p + 1) * prompt_rows)
        scores = causal_scores(q_ref[rows], all_rows(k_ref, p), factor, slope, 0, places[0], True)
        largest = jnp.max(scores, axis=-1, keepdims=True)
        terms = jnp.exp(scores - largest)
        total = jnp.sum(terms, axis=-1, keepdims=True)
        probs = (terms / total).astype(jnp.bfloat16)
        mixed = jnp.dot(probs, all_rows(v_ref, p), preferred_element_type=jnp.float32)
        out_ref[rows] = mixed.astype(out_ref.dtype)
        lse_ref[0, rows] = largest + jnp.log(total)
    for c in range(cont_count):
        own = slice(c * cont_len, (c + 1) * cont_len)
        rows = slice(prompt_total + c * cont_len, prompt_total + (c + 1) * cont_len)
        group = places[1 + c]
        far = causal_scores(q_ref[rows], all_rows(k_ref, group), factor, slope, 0, prompt_len, False)
        near = causal_scores(q_ref[rows], own_k_ref[own], factor, slope, prompt_len, prompt_len, True)
        largest = jnp.maximum(
            jnp.max(far, axis=-1, keepdims=True), jnp.max(near, axis=-1, keepdims=True)
        )
        far, near = jnp.exp(far - largest), jnp.exp(near - largest)
        total = jnp.sum(far, axis=-1, keepdims=True) + jnp.sum(near, axis=-1, keepdims=True)
        mixed = jnp.dot(
            (far / total).astype(jnp.bfloat16), all_rows(v_ref, group), preferred_element_type=jnp.float32
        ) + jnp.dot(
            (near / total).astype(jnp.bfloat16), own_v_ref[own], preferred_element_type=jnp.float32
        )
        out_ref[rows] = mixed.astype(out_ref.dtype)
        lse_ref[0, rows] = largest + jnp.log(total)


def backward_kernel(
    sizes, places, slopes, q_ref, k_ref, v_ref, own_k_ref, own_v_ref, lse_ref, grad_ref,
    q_grad_ref, pair_grad_ref, own_k_grad_ref, own_v_grad_ref, k_sum, v_sum,
):
    prompt_count, prompt_rows, cont_count, cont_len = sizes
    prompt_total = prompt_count * prompt_rows
    prompt_len = k_ref.shape[0] * prompt_rows
    slope = slopes[pl.program_id(0)]
    factor = q_ref.shape[1] ** (-0.5)
    for p in range(prompt_count):
        rows = slice(p * prompt_rows, (p + 1) * prompt_rows)
        queries, grads = q_ref[rows], grad_ref[rows]
        scores = causal_scores(queries, all_rows(k_ref, p), factor, slope, 0, places[0], True)
        probs = jnp.exp(scores - lse_ref[0, rows])
        prob_grad = dot_last(grads, all_rows(v_ref, p))
        inner = jnp.sum(probs * prob_grad, axis=-1, keepdims=True)
        score_grad = (probs * (prob_grad - inner)).astype(jnp.bfloat16)
        q_grad = jnp.dot(score_grad, all_rows(k_ref, p), preferred_element_type=jnp.float32) * factor
        q_grad_ref[rows] = q_grad.astype(q_grad_ref.dtype)
        k_sum[p] = cross(score_grad, queries) * factor
        v_sum[p] = cross(probs.astype(jnp.bfloat16), grads)
    for c in range(cont_count):
        own = slice(c * cont_len, (c + 1) * cont_len)
        rows = slice(prompt_total + c * cont_len, prompt_total + (c + 1) * cont_len)
        group = places[1 + c]
        queries, grads = q_ref[rows], grad_ref[rows]
        far_keys, near_keys = all_rows(k_ref, group), own_k_ref[own]
        far = causal_scores(queries, far_keys, factor, slope, 0, prompt_len, False)
        near = causal_scores(queries, near_keys, factor, slope, prompt_len, prompt_len, True)
        far, near = jnp.exp(far - lse_ref[0, rows]), jnp.exp(near - lse_ref[0, rows])
        far_grad, near_grad = dot_last(grads, all_rows(v_ref, group)), dot_last(grads, own_v_ref[own])
        inner = jnp.sum(far * far_grad, axis=-1, keepdims=True)
        inner = inner + jnp.sum(near * near_grad, axis=-1, keepdims=True)
        far_grad = (far * (far_grad - inner)).astype(jnp.bfloat16)
        near_grad = (near * (near_grad - inner)).astype(jnp.bfloat16)
        q_grad = jnp.dot(far_grad, far_keys, preferred_element_type=jnp.float32)
        q_grad = q_grad + jnp.dot(near_grad, near_keys, preferred_element_type=jnp.float32)
        q_grad_ref[rows] = (q_grad * factor).astype(q_grad_ref.dtype)
        k_sum[group] = k_sum[group] + cross(far_grad, queries) * factor
        v_sum[group] = v_sum[group] + cross(far.astype(jnp.bfloat16), grads)
        own_k_grad_ref[own] = (cross(near_grad, queries) * factor).astype(own_k_grad_ref.dtype)
        own_v_grad_ref[own] = cross(near.astype(jnp.bfloat16), grads).astype(own_v_grad_ref.dtype)
    for p in range(prompt_count):
        for piece in range(prompt_len // prompt_rows):
            rows = slice(piece * prompt_rows, (piece + 1) * prompt_rows)
            pair_grad_ref[piece, 0, p] = k_sum[p, rows].astype(pair_grad_ref.dtype)
            pair_grad_ref[piece, 1, p] = v_sum[p, rows].astype(pair_grad_ref.dtype)


def attention_call(sizes, joined_rows, pairs, places, more=None):
    prompt_count, prompt_rows, cont_count, cont_len = sizes
    tokens, width = joined_rows[0].shape
    prompt_len = pairs.shape[0] * prompt_rows
    heads = width // HEAD_DIM
    cont_rows = cont_count * cont_len
    slopes = 2.0 ** (-8.0 * (jnp.arange(heads, dtype=jnp.float32) + 1.0) / heads)
    by_head = pl.BlockSpec((tokens, HEAD_DIM), lambda h, *_: (0, h))
    own_head = pl.BlockSpec((cont_rows, HEAD_DIM), lambda h, *_: (0, h))
    pair_block = pairs.shape[:3] + (HEAD_DIM,)
    keys = pl.BlockSpec(pair_block, lambda h, *_: (0, 0, 0, h))
    values = pl.BlockSpec(pair_block, lambda h, *_: (0, 0, 0, heads + h))
    stats = pl.BlockSpec((1, tokens, 1), lambda h, *_: (h, 0, 0))
    stats_shape = jax.ShapeDtypeStruct((heads, tokens, 1), jnp.float32)
    rows_shape = jax.ShapeDtypeStruct((tokens, width), jnp.bfloat16)
    own_shape = jax.ShapeDtypeStruct((cont_rows, width), jnp.bfloat16)
    queries, own_keys, own_values = joined_rows
    inputs = (queries, pairs, pairs, own_keys, own_values)
    in_specs = [by_head, keys, values, own_head, own_head]
    pieces = prompt_len // prompt_rows
    scores = tokens * (prompt_len + cont_len) * heads
    if more is None:
        kernel, scratch, products = forward_kernel, [], 2
        out_shape, out_specs = (rows_shape, stats_shape), (by_head, stats)
    else:
        kernel, products = backward_kernel, 5
        scratch = [pltpu.VMEM((prompt_count, prompt_len, HEAD_DIM), jnp.float32)] * 2
        inputs += more
        in_specs += [stats, by_head]
        piece_shape = jax.ShapeDtypeStruct(
            (pieces, 2, prompt_count, prompt_rows, width), jnp.bfloat16
        )
        piece = pl.BlockSpec(
            (pieces, 2, prompt_count, prompt_rows, HEAD_DIM), lambda h, *_: (0, 0, 0, 0, h)
        )
        out_shape = (rows_shape, piece_shape, own_shape, own_shape)
        out_specs = (by_head, piece, own_head, own_head)
    return pl.pallas_call(
        functools.partial(kernel, sizes),
        out_shape=out_shape,
        grid_spec=pltpu.PrefetchScalarGridSpec(
            num_scalar_prefetch=2,
            grid=(heads,),
            in_specs=in_specs,
            out_specs=out_specs,
            scratch_shapes=scratch,
        ),
        compiler_params=pltpu.CompilerParams(vmem_limit_bytes=40 << 20),
        cost_estimate=pl.CostEstimate(
            flops=2 * products * scores * HEAD_DIM,
            transcendentals=scores,
            bytes_accessed=8 * prompt_count * prompt_len * width,
        ),
    )(places, slopes, *inputs)


def send(block, target):
    replicas, shards = lax.axis_size("rep"), lax.axis_size("shard")
    pairs = []
    for r in range(replicas):
        for s in range(shards):
            r_to, z_to, c_to = target(r, s // 2, s % 2)
            pairs.append((r * shards + s, r_to * shards + 2 * z_to + c_to))
    return lax.ppermute(block, AXES, pairs)


def ring_next(block):
    levels = lax.axis_size("shard") // 2
    return send(block, lambda r, z, c: (r, (z + 1) % levels, c))


def swap_core(block):
    return send(block, lambda r, z, c: (r, z, 1 - c))


def bit_of(step, core):
    bits = lax.axis_size("rep").bit_length() - 1
    return step if core == 0 else bits - 1 - step


def swap_rep(block, step):
    return send(block, lambda r, z, c: (r ^ (1 << bit_of(step, c)), z, c))


def mask_lists():
    bits = lax.axis_size("rep").bit_length() - 1
    lists = []
    for core in range(2):
        masks = [0]
        for step in range(bits):
            masks += [m ^ (1 << bit_of(step, core)) for m in masks]
        lists.append(masks)
    return lists


def spread_rep(block):
    bits = lax.axis_size("rep").bit_length() - 1
    pieces = [block]
    for step in range(bits):
        pieces += [swap_rep(p, step) for p in pieces]
    return pieces


def rep_positions(core, r):
    lists = mask_lists()
    return [jnp.where(core == 0, a, b) ^ r for a, b in zip(*lists)]


MESH_ID = pl.DeviceIdType.MESH


def gather_kernel(levels, replicas, spread, units, *refs):
    count = len(spread)
    owns, fulls = refs[:count], refs[count : 2 * count]
    staged = refs[2 * count : 3 * count]
    own_sem, ring_send, ring_recv, rep_send, rep_recv, core_send, core_recv = refs[3 * count :]
    bits = replicas.bit_length() - 1
    r, s = lax.axis_index("rep"), lax.axis_index("shard")
    core, z = lax.rem(s, 2), lax.div(s, 2)
    other = {"shard": s + 1 - 2 * core}
    ring_to = {"shard": lax.rem(s + 2, 2 * levels)}
    ring_from = {"shard": lax.rem(s + 2 * levels - 2, 2 * levels)}
    rep_to = [{"rep": r ^ jnp.where(core == 0, 1 << bit_of(n, 0), 1 << bit_of(n, 1))} for n in range(bits)]
    barrier = pltpu.get_barrier_semaphore()
    partners = [ring_to, ring_from, other] + rep_to
    for partner in partners:
        pl.semaphore_signal(barrier, inc=1, device_id=partner, device_id_type=MESH_ID)
    pl.semaphore_wait(barrier, len(partners))
    lists = mask_lists()
    place = [jnp.where(core == 0, a, b) ^ r for a, b in zip(*lists)]

    def piece_of(m, j, n):
        block = fulls[m].at[2 * lax.rem(z - j + levels, levels) + core]
        return block.at[place[n]] if spread[m] else block

    def remote(source, target, sends, recvs, n, device):
        return pltpu.make_async_remote_copy(
            src_ref=source,
            dst_ref=target,
            send_sem=sends.at[n],
            recv_sem=recvs.at[n],
            device_id=device,
            device_id_type=MESH_ID,
        )

    def ring_copy(t):
        m, j = units[t]
        target = piece_of(m, j - 1, 0)
        own = owns[m].at[r] if spread[m] else owns[m]
        return remote(own if j == 1 else target, target, ring_send, ring_recv, t, ring_to)

    def rep_copy(t, step, n):
        piece = piece_of(*units[t], n)
        return remote(piece, piece, rep_send, rep_recv, t * replicas + (1 << step) + n, rep_to[step])

    def core_copy(t, n):
        piece = piece_of(*units[t], n)
        return remote(piece, piece, core_send, core_recv, t * replicas + n, other)

    last = len(units)
    ready = {}
    for t, (m, j) in enumerate(units):
        earlier = units.index((m, j - 1)) if j > 1 else -1
        ready.setdefault(max(earlier, t - 2), []).append(t)
    started = []

    def start(copy):
        copy.start()
        started.append(copy)

    rings = [ring_copy(t) for t in range(last)]
    reps = {}
    for early in (-2, -1):
        for t in ready.get(early, []):
            start(rings[t])
    own_ins, own_outs, own_cores = [], [], []
    for m in range(count):
        own_ins.append(pltpu.make_async_copy(owns[m], staged[m], own_sem.at[2 * m]))
        own_outs.append(pltpu.make_async_copy(staged[m], fulls[m].at[s], own_sem.at[2 * m + 1]))
        own_cores.append(
            remote(staged[m], fulls[m].at[s], core_send, core_recv, last * replicas + m, other)
        )
        own_ins[m].start()
    for m in range(count):
        own_ins[m].wait()
        own_outs[m].start()
        start(own_cores[m])
    for tick in range(last + bits):
        t = tick
        if t < last:
            rings[t].wait_recv()
            for later in ready.get(t, []):
                start(rings[later])
            if spread[units[t][0]]:
                for step in range(bits):
                    reps[t, step, 0] = rep_copy(t, step, 0)
                    start(reps[t, step, 0])
            start(core_copy(t, 0))
        for lag in range(1, bits + 1):
            t = tick - lag
            if not 0 <= t < last or not spread[units[t][0]]:
                continue
            got = lag - 1
            for n in range(1 << got):
                reps[t, got, n].wait_recv()
                arrived = (1 << got) + n
                for step in range(got + 1, bits):
                    reps[t, step, arrived] = rep_copy(t, step, arrived)
                    start(reps[t, step, arrived])
                start(core_copy(t, arrived))
    for copy in started:
        copy.wait_send()
    for t in range(last):
        for n in range(replicas if spread[units[t][0]] else 1):
            core_copy(t, n).wait_recv()
    for m in range(count):
        own_outs[m].wait()
        own_cores[m].wait_recv()


def gather_rows(arrays, spread, order, collective_id):
    replicas, shards = lax.axis_size("rep"), lax.axis_size("shard")
    levels = shards // 2
    count = len(arrays)
    owns = [
        w.reshape((replicas, w.shape[0] // replicas) + w.shape[1:]) if wide else w
        for w, wide in zip(arrays, spread)
    ]
    units = [(m, j) for j in range(1, levels) for m in order]
    slots = len(units) * replicas
    any_space = pl.BlockSpec(memory_space=pl.ANY)
    dma = pltpu.SemaphoreType.DMA
    size = sum(w.size * 2 for w in arrays)
    return pl.pallas_call(
        functools.partial(gather_kernel, levels, replicas, spread, units),
        out_shape=[jax.ShapeDtypeStruct((shards,) + w.shape, w.dtype) for w in owns],
        in_specs=[any_space] * count,
        out_specs=[any_space] * count,
        scratch_shapes=[pltpu.VMEM(w.shape, w.dtype) for w in owns]
        + [
            dma((2 * count,)),
            dma((len(units),)),
            dma((len(units),)),
            dma((slots,)),
            dma((slots,)),
            dma((slots + count,)),
            dma((slots + count,)),
        ],
        compiler_params=pltpu.CompilerParams(
            collective_id=collective_id, has_side_effects=True, vmem_limit_bytes=size + (1 << 20)
        ),
        cost_estimate=pl.CostEstimate(flops=0, transcendentals=0, bytes_accessed=30 * size),
    )(*owns)


def plain(full):
    return full.reshape(-1, full.shape[-1])


def behind(numbers, top, *arrays):
    for array in arrays:
        first = lax.slice(array, (0,) * array.ndim, (1,) * array.ndim).reshape(())
        numbers = numbers + (first != first).astype(jnp.int32)
    return jnp.clip(numbers, 0, top)


def gradient_kernel(places, left, left_far, right, right_far, out):
    total = cross(left[...], right[...]) + cross(left_far[...], right_far[...])
    parts, part = out.shape[0], out.shape[2]
    for q in range(parts):
        out[q, 0] = total[q * part : (q + 1) * part].astype(out.dtype)


def chip_gradient(left, right, *first):
    replicas, shards = lax.axis_size("rep"), lax.axis_size("shard")
    levels = shards // 2
    core = lax.rem(lax.axis_index("shard"), 2)
    tokens, height = left.shape
    columns = right.shape[1]
    rows = height // shards
    part = rows // replicas
    even, odd = [
        jnp.concatenate(
            [left[:, (2 * z + c) * rows : (2 * z + c + 1) * rows] for z in range(levels)], axis=1
        )
        for c in range(2)
    ]
    left_far = swap_core(jnp.where(core == 0, odd, even))
    right_far = swap_core(right)
    wide = min(columns, (1 << 18) // rows)
    return pl.pallas_call(
        gradient_kernel,
        out_shape=jax.ShapeDtypeStruct((replicas, levels, part, columns), jnp.bfloat16),
        grid_spec=pltpu.PrefetchScalarGridSpec(
            num_scalar_prefetch=1,
            grid=(columns // wide, levels),
            in_specs=[
                pl.BlockSpec((tokens, rows), lambda n, z, places: (0, 2 * z + places[0])),
                pl.BlockSpec((tokens, rows), lambda n, z, places: (0, z)),
                pl.BlockSpec((tokens, wide), lambda n, z, places: (0, n)),
                pl.BlockSpec((tokens, wide), lambda n, z, places: (0, n)),
            ],
            out_specs=pl.BlockSpec((replicas, 1, part, wide), lambda n, z, places: (0, z, 0, n)),
        ),
        compiler_params=pltpu.CompilerParams(vmem_limit_bytes=40 << 20),
        cost_estimate=pl.CostEstimate(
            flops=2 * tokens * height * columns,
            transcendentals=0,
            bytes_accessed=2 * (2 * tokens + height // 2) * columns + 2 * tokens * height,
        ),
    )(behind(core[None], 1, *first), left, left_far, right, right_far)


def add_low(left, right):
    return (left.astype(jnp.float32) + right.astype(jnp.float32)).astype(jnp.bfloat16)


def halve_rep(total):
    replicas = lax.axis_size("rep")
    bits = replicas.bit_length() - 1
    r = lax.axis_index("rep")
    core = lax.rem(lax.axis_index("shard"), 2)
    offsets = []
    for c in range(2):
        masks = [0]
        for step in reversed(range(bits)):
            masks = masks + [m ^ (1 << bit_of(step, c)) for m in masks]
        offsets.append(masks)
    held = [
        lax.dynamic_index_in_dim(total, jnp.where(core == 0, a, b) ^ r, 0, keepdims=False)
        for a, b in zip(*offsets)
    ]
    steps = []
    for step in range(bits):
        half = len(held) // 2
        arrived = [swap_rep(held[half + n], step) for n in range(half)]
        steps.append(arrived[-1])
        held = [add_low(held[n], arrived[n]) for n in range(half)]
    return steps, held[0]


def ring_sum(plane):
    levels = plane.shape[0]
    z = lax.div(lax.axis_index("shard"), 2)
    travelling = lax.dynamic_index_in_dim(plane, lax.rem(z + levels - 1, levels), 0, keepdims=False)
    for step in range(1, levels):
        arrived = ring_next(travelling)
        own = lax.dynamic_index_in_dim(
            plane, lax.rem(z + 2 * levels - 1 - step, levels), 0, keepdims=False
        )
        travelling = add_low(own, arrived)
    return travelling


def owned_rows(block):
    replicas = lax.axis_size("rep")
    r = lax.axis_index("rep")
    core = lax.rem(lax.axis_index("shard"), 2)
    part, columns = block.shape
    out = jnp.zeros((replicas, part, columns), jnp.float32)
    for piece, q in zip(spread_rep(block), rep_positions(core, r)):
        out = lax.dynamic_update_index_in_dim(out, piece.astype(jnp.float32), q, 0)
    return out.reshape(replicas * part, columns)


def sum_everywhere(block):
    replicas, shards = lax.axis_size("rep"), lax.axis_size("shard")
    step = 1
    while step < shards:
        block = block + lax.ppermute(block, "shard", [(s, s ^ step) for s in range(shards)])
        step *= 2
    step = 1
    while step < replicas:
        block = block + lax.ppermute(block, "rep", [(r, r ^ step) for r in range(replicas)])
        step *= 2
    return block


def owned_sums(vectors):
    shards = lax.axis_size("shard")
    shard_index = lax.axis_index("shard")
    joint = jnp.concatenate([vector.reshape(shards, -1) for vector in vectors], axis=1)
    total = sum_everywhere(joint)
    mine = lax.dynamic_index_in_dim(total, shard_index, 0, keepdims=False)
    parts, begin = [], 0
    for vector in vectors:
        size = vector.shape[0] // shards
        parts.append(mine[begin : begin + size])
        begin += size
    return parts


def per_device(
    x_prompt,
    x_cont,
    teacher_prompt,
    teacher_cont,
    valid_mask,
    group_of,
    ln1_gain,
    ln1_bias,
    w_qkv,
    q_bias,
    v_bias,
    w_out,
    out_bias,
    ln2_gain,
    ln2_bias,
    w_up,
    up_bias,
    w_down,
    down_bias,
):
    shards = lax.axis_size("shard")
    replicas = lax.axis_size("rep")
    shard_index = lax.axis_index("shard")
    prompt_count, prompt_rows, width = x_prompt.shape
    cont_rows = x_cont.shape[0]
    cont_count, cont_len = valid_mask.shape
    prompt_len = prompt_rows * shards
    prompt_total = prompt_count * prompt_rows
    head_count = width // HEAD_DIM
    all_tokens = replicas * shards * (prompt_total + cont_rows)
    valid_local = jnp.sum(valid_mask.astype(jnp.float32)) + prompt_total
    valid_all = sum_everywhere(jnp.full((8, 128), valid_local, jnp.float32))[0, 0]
    loss_scale = all_tokens / valid_all
    (qkv_full,) = gather_rows([w_qkv], (True,), (0,), 0)
    qkv_full = plain(qkv_full)
    vectors = (
        ln1_gain,
        ln1_bias,
        q_bias,
        v_bias,
        out_bias,
        ln2_gain,
        ln2_bias,
        up_bias,
        down_bias,
    )
    joint = lax.all_gather(jnp.concatenate(vectors)[None], "shard", axis=0, tiled=True)
    starts = [0]
    for vector in vectors:
        starts.append(starts[-1] + vector.shape[0])
    (
        gain_one,
        shift_one,
        bias_query,
        bias_value,
        bias_out,
        gain_two,
        shift_two,
        bias_up,
        bias_down,
    ) = [
        joint[:, begin:end].reshape(-1).astype(jnp.float32)
        for begin, end in zip(starts[:-1], starts[1:])
    ]
    inputs = jnp.concatenate([x_prompt.reshape(prompt_total, width), x_cont], axis=0).astype(
        jnp.float32
    )
    normed, unit_one, inverse_one = norm_forward(inputs, gain_one, shift_one)
    normed_low = normed.astype(jnp.bfloat16)
    joined = jnp.dot(normed_low, qkv_full, preferred_element_type=jnp.float32)
    queries = (joined[:, :width] + bias_query).astype(jnp.bfloat16)
    key_rows = joined[:, width : 2 * width].astype(jnp.bfloat16)
    value_rows = (joined[:, 2 * width :] + bias_value).astype(jnp.bfloat16)
    local_pairs = jnp.concatenate(
        [key_rows[:prompt_total], value_rows[:prompt_total]], axis=1
    ).reshape(prompt_count, prompt_rows, 2 * width)
    prompt_pairs, out_full, up_full, down_full = gather_rows(
        [local_pairs, w_out, w_up, w_down], (False, True, True, True), (1, 2, 0, 3), 1
    )
    out_full, up_full, down_full = plain(out_full), plain(up_full), plain(down_full)
    sizes = (prompt_count, prompt_rows, cont_count, cont_len)
    places = jnp.concatenate([(shard_index * prompt_rows)[None], group_of]).astype(jnp.int32)
    joined_rows = (queries, key_rows[prompt_total:], value_rows[prompt_total:])
    attended, log_totals = attention_call(sizes, joined_rows, prompt_pairs, places)
    middle = inputs + jnp.dot(attended, out_full, preferred_element_type=jnp.float32) + bias_out
    normed_two, unit_two, inverse_two = norm_forward(middle, gain_two, shift_two)
    normed_two_low = normed_two.astype(jnp.bfloat16)
    upward = jnp.dot(normed_two_low, up_full, preferred_element_type=jnp.float32) + bias_up
    active_low = gelu_tanh(upward).astype(jnp.bfloat16)
    result = middle + jnp.dot(active_low, down_full, preferred_element_type=jnp.float32) + bias_down
    out_prompt = (
        result[:prompt_total].reshape(prompt_count, prompt_rows, width).astype(jnp.bfloat16)
    )
    out_cont = result[prompt_total:].astype(jnp.bfloat16)
    targets = jnp.concatenate(
        [teacher_prompt.reshape(prompt_total, width), teacher_cont], axis=0
    ).astype(jnp.float32)
    weight_rows = jnp.concatenate(
        [jnp.ones((prompt_total,), jnp.float32), valid_mask.reshape(cont_rows).astype(jnp.float32)]
    )
    out_grad = (loss_scale * weight_rows)[:, None] * (result - targets)
    mlp_grad = out_grad.astype(jnp.bfloat16)
    grad_bias_down = jnp.sum(mlp_grad, axis=0, dtype=jnp.float32)
    down_steps, down_plane = halve_rep(chip_gradient(active_low, mlp_grad))
    active_grad = back_product(mlp_grad, down_full)
    unused_value, gelu_pull = jax.vjp(gelu_tanh, upward)
    upward_grad = gelu_pull(active_grad)[0].astype(jnp.bfloat16)
    grad_bias_up = jnp.sum(upward_grad, axis=0, dtype=jnp.float32)
    up_steps, up_plane = halve_rep(chip_gradient(normed_two_low, upward_grad))
    normed_two_grad = back_product(upward_grad, up_full)
    middle_step, grad_gain_two, grad_shift_two = norm_backward(
        normed_two_grad, unit_two, inverse_two, gain_two
    )
    middle_grad = out_grad + middle_step
    branch_grad = middle_grad.astype(jnp.bfloat16)
    grad_bias_out = jnp.sum(branch_grad, axis=0, dtype=jnp.float32)
    attended_grad = back_product(branch_grad, out_full).astype(jnp.bfloat16)
    later_places = behind(places, prompt_rows * shards, down_steps[0])
    query_part, pair_grad, own_key_grad, own_value_grad = attention_call(
        sizes, joined_rows, prompt_pairs, later_places, (log_totals, attended_grad)
    )
    out_steps, out_plane = halve_rep(chip_gradient(attended, branch_grad, down_plane))
    summed_down = owned_rows(ring_sum(down_plane))
    owned_keys, owned_values = lax.psum_scatter(pair_grad, "shard", scatter_dimension=0)
    key_part = jnp.concatenate([owned_keys.reshape(prompt_total, width), own_key_grad], axis=0)
    value_part = jnp.concatenate(
        [owned_values.reshape(prompt_total, width), own_value_grad], axis=0
    )
    joined_grad = jnp.concatenate([query_part, key_part, value_part], axis=1)
    grad_bias_query = jnp.sum(joined_grad[:, :width], axis=0, dtype=jnp.float32)
    grad_bias_value = jnp.sum(joined_grad[:, 2 * width :], axis=0, dtype=jnp.float32)
    normed_grad = back_product(joined_grad, qkv_full)
    input_step, grad_gain_one, grad_shift_one = norm_backward(
        normed_grad, unit_one, inverse_one, gain_one
    )
    input_grad = middle_grad + input_step
    qkv_steps, qkv_plane = halve_rep(chip_gradient(normed_low, joined_grad, up_steps[0]))
    summed_up = owned_rows(ring_sum(up_plane))
    summed_out = owned_rows(ring_sum(out_plane))
    summed_qkv = owned_rows(ring_sum(qkv_plane))
    early_sums = (grad_bias_out, grad_gain_two, grad_shift_two, grad_bias_up, grad_bias_down)
    late_sums = (grad_gain_one, grad_shift_one, grad_bias_query, grad_bias_value)
    owned_vectors = owned_sums(late_sums) + owned_sums(early_sums)
    grad_prompt = input_grad[:prompt_total].reshape(prompt_count, prompt_rows, width)
    grad_cont = input_grad[prompt_total:]
    return (
        out_prompt,
        out_cont,
        grad_prompt,
        grad_cont,
        owned_vectors[0],
        owned_vectors[1],
        summed_qkv,
        owned_vectors[2],
        owned_vectors[3],
        summed_out,
        owned_vectors[4],
        owned_vectors[5],
        owned_vectors[6],
        summed_up,
        owned_vectors[7],
        summed_down,
        owned_vectors[8],
    )


def solution(mesh):
    in_specs = (
        P("rep", "shard", None),
        P(("rep", "shard"), None),
        P("rep", "shard", None),
        P(("rep", "shard"), None),
        P(("rep", "shard"), None),
        P(("rep", "shard")),
        P("shard"),
        P("shard"),
        P("shard", None),
        P("shard"),
        P("shard"),
        P("shard", None),
        P("shard"),
        P("shard"),
        P("shard"),
        P("shard", None),
        P("shard"),
        P("shard", None),
        P("shard"),
    )
    out_specs = (
        P("rep", "shard", None),
        P(("rep", "shard"), None),
        P("rep", "shard", None),
        P(("rep", "shard"), None),
        P("shard"),
        P("shard"),
        P("shard", None),
        P("shard"),
        P("shard"),
        P("shard", None),
        P("shard"),
        P("shard"),
        P("shard"),
        P("shard", None),
        P("shard"),
        P("shard", None),
        P("shard"),
    )
    return jax.shard_map(
        per_device, mesh=mesh, in_specs=in_specs, out_specs=out_specs, check_vma=False
    )
```

```python
import functools

import jax
import jax.numpy as jnp
from jax import lax
from jax.experimental import pallas as pl
from jax.experimental.pallas import tpu as pltpu
from jax.sharding import PartitionSpec as P

HEAD_DIM = 128
AXES = ("rep", "shard")


epsilon = 1e-05
gelu_coef = 0.7978845608028654


def gelu_tanh(values):
    return (
        0.5 * values * (1.0 + jnp.tanh(gelu_coef * (values + 0.044715 * values * values * values)))
    )


def norm_forward(inputs, norm_gain, norm_shift):
    centered = inputs - jnp.mean(inputs, axis=-1, keepdims=True)
    variance = jnp.mean(centered * centered, axis=-1, keepdims=True)
    inverse = lax.rsqrt(variance + epsilon)
    unit_rows = centered * inverse
    return (unit_rows * norm_gain + norm_shift, unit_rows, inverse)


def norm_backward(upstream, unit_rows, inverse, norm_gain):
    scaled = upstream * norm_gain
    centered = (
        scaled
        - jnp.mean(scaled, axis=-1, keepdims=True)
        - unit_rows * jnp.mean(scaled * unit_rows, axis=-1, keepdims=True)
    )
    return (centered * inverse, jnp.sum(upstream * unit_rows, axis=0), jnp.sum(upstream, axis=0))


def cross(left, right):
    return lax.dot_general(
        left, right, (((0,), (0,)), ((), ())), preferred_element_type=jnp.float32
    )


def back_product(left, right):
    return lax.dot_general(
        left, right, (((1,), (1,)), ((), ())), preferred_element_type=jnp.float32
    )


def dot_last(left, right):
    return back_product(left, right)


def causal_scores(queries, keys, factor, slope, key_start, query_start, masked):
    scores = dot_last(queries, keys) * factor
    key_pos = key_start + lax.broadcasted_iota(jnp.int32, (1, keys.shape[0]), 1)
    scores = scores + slope * (key_pos - query_start).astype(jnp.float32)
    if masked:
        query_pos = query_start + lax.broadcasted_iota(jnp.int32, (queries.shape[0], 1), 0)
        scores = jnp.where(key_pos <= query_pos, scores, -1e30)
    return scores


def all_rows(ref, prompt):
    return ref[:, prompt].reshape(-1, ref.shape[-1])


def forward_kernel(sizes, places, slopes, q_ref, k_ref, v_ref, own_k_ref, own_v_ref, out_ref, lse_ref):
    prompt_count, prompt_rows, cont_count, cont_len = sizes
    prompt_total = prompt_count * prompt_rows
    prompt_len = k_ref.shape[0] * prompt_rows
    slope = slopes[pl.program_id(0)]
    factor = q_ref.shape[1] ** (-0.5)
    for p in range(prompt_count):
        rows = slice(p * prompt_rows, (p + 1) * prompt_rows)
        scores = causal_scores(q_ref[rows], all_rows(k_ref, p), factor, slope, 0, places[0], True)
        largest = jnp.max(scores, axis=-1, keepdims=True)
        terms = jnp.exp(scores - largest)
        total = jnp.sum(terms, axis=-1, keepdims=True)
        probs = (terms / total).astype(jnp.bfloat16)
        mixed = jnp.dot(probs, all_rows(v_ref, p), preferred_element_type=jnp.float32)
        out_ref[rows] = mixed.astype(out_ref.dtype)
        lse_ref[0, rows] = largest + jnp.log(total)
    for c in range(cont_count):
        own = slice(c * cont_len, (c + 1) * cont_len)
        rows = slice(prompt_total + c * cont_len, prompt_total + (c + 1) * cont_len)
        group = places[1 + c]
        far = causal_scores(q_ref[rows], all_rows(k_ref, group), factor, slope, 0, prompt_len, False)
        near = causal_scores(q_ref[rows], own_k_ref[own], factor, slope, prompt_len, prompt_len, True)
        largest = jnp.maximum(
            jnp.max(far, axis=-1, keepdims=True), jnp.max(near, axis=-1, keepdims=True)
        )
        far, near = jnp.exp(far - largest), jnp.exp(near - largest)
        total = jnp.sum(far, axis=-1, keepdims=True) + jnp.sum(near, axis=-1, keepdims=True)
        mixed = jnp.dot(
            (far / total).astype(jnp.bfloat16), all_rows(v_ref, group), preferred_element_type=jnp.float32
        ) + jnp.dot(
            (near / total).astype(jnp.bfloat16), own_v_ref[own], preferred_element_type=jnp.float32
        )
        out_ref[rows] = mixed.astype(out_ref.dtype)
        lse_ref[0, rows] = largest + jnp.log(total)


def backward_kernel(
    sizes, places, slopes, q_ref, k_ref, v_ref, own_k_ref, own_v_ref, lse_ref, grad_ref,
    q_grad_ref, pair_grad_ref, own_k_grad_ref, own_v_grad_ref, k_sum, v_sum,
):
    prompt_count, prompt_rows, cont_count, cont_len = sizes
    prompt_total = prompt_count * prompt_rows
    prompt_len = k_ref.shape[0] * prompt_rows
    slope = slopes[pl.program_id(0)]
    factor = q_ref.shape[1] ** (-0.5)
    for p in range(prompt_count):
        rows = slice(p * prompt_rows, (p + 1) * prompt_rows)
        queries, grads = q_ref[rows], grad_ref[rows]
        scores = causal_scores(queries, all_rows(k_ref, p), factor, slope, 0, places[0], True)
        probs = jnp.exp(scores - lse_ref[0, rows])
        prob_grad = dot_last(grads, all_rows(v_ref, p))
        inner = jnp.sum(probs * prob_grad, axis=-1, keepdims=True)
        score_grad = (probs * (prob_grad - inner)).astype(jnp.bfloat16)
        q_grad = jnp.dot(score_grad, all_rows(k_ref, p), preferred_element_type=jnp.float32) * factor
        q_grad_ref[rows] = q_grad.astype(q_grad_ref.dtype)
        k_sum[p] = cross(score_grad, queries) * factor
        v_sum[p] = cross(probs.astype(jnp.bfloat16), grads)
    for c in range(cont_count):
        own = slice(c * cont_len, (c + 1) * cont_len)
        rows = slice(prompt_total + c * cont_len, prompt_total + (c + 1) * cont_len)
        group = places[1 + c]
        queries, grads = q_ref[rows], grad_ref[rows]
        far_keys, near_keys = all_rows(k_ref, group), own_k_ref[own]
        far = causal_scores(queries, far_keys, factor, slope, 0, prompt_len, False)
        near = causal_scores(queries, near_keys, factor, slope, prompt_len, prompt_len, True)
        far, near = jnp.exp(far - lse_ref[0, rows]), jnp.exp(near - lse_ref[0, rows])
        far_grad, near_grad = dot_last(grads, all_rows(v_ref, group)), dot_last(grads, own_v_ref[own])
        inner = jnp.sum(far * far_grad, axis=-1, keepdims=True)
        inner = inner + jnp.sum(near * near_grad, axis=-1, keepdims=True)
        far_grad = (far * (far_grad - inner)).astype(jnp.bfloat16)
        near_grad = (near * (near_grad - inner)).astype(jnp.bfloat16)
        q_grad = jnp.dot(far_grad, far_keys, preferred_element_type=jnp.float32)
        q_grad = q_grad + jnp.dot(near_grad, near_keys, preferred_element_type=jnp.float32)
        q_grad_ref[rows] = (q_grad * factor).astype(q_grad_ref.dtype)
        k_sum[group] = k_sum[group] + cross(far_grad, queries) * factor
        v_sum[group] = v_sum[group] + cross(far.astype(jnp.bfloat16), grads)
        own_k_grad_ref[own] = (cross(near_grad, queries) * factor).astype(own_k_grad_ref.dtype)
        own_v_grad_ref[own] = cross(near.astype(jnp.bfloat16), grads).astype(own_v_grad_ref.dtype)
    for p in range(prompt_count):
        for piece in range(prompt_len // prompt_rows):
            rows = slice(piece * prompt_rows, (piece + 1) * prompt_rows)
            pair_grad_ref[piece, 0, p] = k_sum[p, rows].astype(pair_grad_ref.dtype)
            pair_grad_ref[piece, 1, p] = v_sum[p, rows].astype(pair_grad_ref.dtype)


def attention_call(sizes, joined_rows, pairs, places, more=None):
    prompt_count, prompt_rows, cont_count, cont_len = sizes
    tokens, width = joined_rows[0].shape
    prompt_len = pairs.shape[0] * prompt_rows
    heads = width // HEAD_DIM
    cont_rows = cont_count * cont_len
    slopes = 2.0 ** (-8.0 * (jnp.arange(heads, dtype=jnp.float32) + 1.0) / heads)
    by_head = pl.BlockSpec((tokens, HEAD_DIM), lambda h, *_: (0, h))
    own_head = pl.BlockSpec((cont_rows, HEAD_DIM), lambda h, *_: (0, h))
    pair_block = pairs.shape[:3] + (HEAD_DIM,)
    keys = pl.BlockSpec(pair_block, lambda h, *_: (0, 0, 0, h))
    values = pl.BlockSpec(pair_block, lambda h, *_: (0, 0, 0, heads + h))
    stats = pl.BlockSpec((1, tokens, 1), lambda h, *_: (h, 0, 0))
    stats_shape = jax.ShapeDtypeStruct((heads, tokens, 1), jnp.float32)
    rows_shape = jax.ShapeDtypeStruct((tokens, width), jnp.bfloat16)
    own_shape = jax.ShapeDtypeStruct((cont_rows, width), jnp.bfloat16)
    queries, own_pairs = joined_rows
    own_values = pl.BlockSpec((cont_rows, HEAD_DIM), lambda h, *_: (0, heads + h))
    inputs = (queries, pairs, pairs, own_pairs, own_pairs)
    in_specs = [by_head, keys, values, own_head, own_values]
    pieces = prompt_len // prompt_rows
    scores = tokens * (prompt_len + cont_len) * heads
    if more is None:
        kernel, scratch, products = forward_kernel, [], 2
        out_shape, out_specs = (rows_shape, stats_shape), (by_head, stats)
    else:
        kernel, products = backward_kernel, 5
        scratch = [pltpu.VMEM((prompt_count, prompt_len, HEAD_DIM), jnp.float32)] * 2
        inputs += more
        in_specs += [stats, by_head]
        piece_shape = jax.ShapeDtypeStruct(
            (pieces, 2, prompt_count, prompt_rows, width), jnp.bfloat16
        )
        piece = pl.BlockSpec(
            (pieces, 2, prompt_count, prompt_rows, HEAD_DIM), lambda h, *_: (0, 0, 0, 0, h)
        )
        out_shape = (rows_shape, piece_shape, own_shape, own_shape)
        out_specs = (by_head, piece, own_head, own_head)
    return pl.pallas_call(
        functools.partial(kernel, sizes),
        out_shape=out_shape,
        grid_spec=pltpu.PrefetchScalarGridSpec(
            num_scalar_prefetch=2,
            grid=(heads,),
            in_specs=in_specs,
            out_specs=out_specs,
            scratch_shapes=scratch,
        ),
        compiler_params=pltpu.CompilerParams(vmem_limit_bytes=40 << 20),
        cost_estimate=pl.CostEstimate(
            flops=2 * products * scores * HEAD_DIM,
            transcendentals=scores,
            bytes_accessed=8 * prompt_count * prompt_len * width,
        ),
    )(places, slopes, *inputs)


def send(block, target):
    replicas, shards = lax.axis_size("rep"), lax.axis_size("shard")
    pairs = []
    for r in range(replicas):
        for s in range(shards):
            r_to, z_to, c_to = target(r, s // 2, s % 2)
            pairs.append((r * shards + s, r_to * shards + 2 * z_to + c_to))
    return lax.ppermute(block, AXES, pairs)


def ring_next(block):
    levels = lax.axis_size("shard") // 2
    return send(block, lambda r, z, c: (r, (z + 1) % levels, c))


def swap_core(block):
    return send(block, lambda r, z, c: (r, z, 1 - c))


def bit_of(step, core):
    bits = lax.axis_size("rep").bit_length() - 1
    return step if core == 0 else bits - 1 - step


def swap_rep(block, step):
    return send(block, lambda r, z, c: (r ^ (1 << bit_of(step, c)), z, c))


def mask_lists():
    bits = lax.axis_size("rep").bit_length() - 1
    lists = []
    for core in range(2):
        masks = [0]
        for step in range(bits):
            masks += [m ^ (1 << bit_of(step, core)) for m in masks]
        lists.append(masks)
    return lists


def spread_rep(block):
    bits = lax.axis_size("rep").bit_length() - 1
    pieces = [block]
    for step in range(bits):
        pieces += [swap_rep(p, step) for p in pieces]
    return pieces


def rep_positions(core, r):
    lists = mask_lists()
    return [jnp.where(core == 0, a, b) ^ r for a, b in zip(*lists)]


MESH_ID = pl.DeviceIdType.MESH


def gather_kernel(levels, replicas, spread, placed, begun, units, *refs):
    count = len(spread)
    owns, fulls = refs[:count], refs[count + begun : 2 * count + begun]
    staged = refs[2 * count + begun : 3 * count + begun]
    own_sem, ring_send, ring_recv, rep_send, rep_recv, core_send, core_recv = refs[3 * count + begun :]
    bits = replicas.bit_length() - 1
    r, s = lax.axis_index("rep"), lax.axis_index("shard")
    core, z = lax.rem(s, 2), lax.div(s, 2)
    other = {"shard": s + 1 - 2 * core}
    ring_to = {"shard": lax.rem(s + 2, 2 * levels)}
    ring_from = {"shard": lax.rem(s + 2 * levels - 2, 2 * levels)}
    rep_to = [{"rep": r ^ jnp.where(core == 0, 1 << bit_of(n, 0), 1 << bit_of(n, 1))} for n in range(bits)]
    barrier = pltpu.get_barrier_semaphore()
    partners = [ring_to, ring_from, other] + rep_to
    for partner in partners:
        pl.semaphore_signal(barrier, inc=1, device_id=partner, device_id_type=MESH_ID)
    pl.semaphore_wait(barrier, len(partners))
    lists = mask_lists()
    place = [jnp.where(core == 0, a, b) ^ r for a, b in zip(*lists)]

    def piece_of(m, j, n):
        block = fulls[m].at[2 * lax.rem(z - j + levels, levels) + core]
        return block.at[place[n]] if spread[m] else block

    def remote(source, target, sends, recvs, n, device):
        return pltpu.make_async_remote_copy(
            src_ref=source,
            dst_ref=target,
            send_sem=sends.at[n],
            recv_sem=recvs.at[n],
            device_id=device,
            device_id_type=MESH_ID,
        )

    def ring_copy(t):
        m, j = units[t][:2]
        target = piece_of(m, j - 1, 0)
        own = owns[m].at[r] if spread[m] else owns[m]
        return remote(own if j == 1 else target, target, ring_send, ring_recv, t, ring_to)

    def rep_copy(t, step, n):
        piece = piece_of(*units[t][:2], n)
        return remote(piece, piece, rep_send, rep_recv, t * replicas + (1 << step) + n, rep_to[step])

    def core_copy(t, n):
        piece = piece_of(*units[t][:2], n)
        return remote(piece, piece, core_send, core_recv, t * replicas + n, other)

    last = len(units)
    goes = [t for t in range(last) if units[t][2]]
    ready = {}
    for n, t in enumerate(goes):
        m, j = units[t][:2]
        needs = [goes[n - 2]] if n >= 2 else []
        needs += [e for e in goes[:n] if units[e][:2] == (m, j - 1)]
        ready.setdefault(max(needs, default=-1), []).append(t)
    started = []

    def start(copy):
        copy.start()
        started.append(copy)

    rings = {t: ring_copy(t) for t in goes}
    reps = {}
    for t in ready.get(-1, []):
        start(rings[t])
    own_ins, own_outs, own_cores = {}, {}, {}
    for m in range(count):
        if placed[m]:
            own_ins[m] = pltpu.make_async_copy(owns[m], staged[m], own_sem.at[2 * m])
            own_outs[m] = pltpu.make_async_copy(staged[m], fulls[m].at[s], own_sem.at[2 * m + 1])
            own_cores[m] = remote(
                staged[m], fulls[m].at[s], core_send, core_recv, last * replicas + m, other
            )
            own_ins[m].start()
    for m in own_ins:
        own_ins[m].wait()
        own_outs[m].start()
        start(own_cores[m])
    for tick in range(last + bits):
        t = tick
        if t < last:
            if units[t][2]:
                rings[t].wait_recv()
                for later in ready.get(t, []):
                    start(rings[later])
            if units[t][3]:
                if spread[units[t][0]]:
                    for step in range(bits):
                        reps[t, step, 0] = rep_copy(t, step, 0)
                        start(reps[t, step, 0])
                start(core_copy(t, 0))
        for lag in range(1, bits + 1):
            t = tick - lag
            if not 0 <= t < last or not units[t][3] or not spread[units[t][0]]:
                continue
            got = lag - 1
            for n in range(1 << got):
                reps[t, got, n].wait_recv()
                arrived = (1 << got) + n
                for step in range(got + 1, bits):
                    reps[t, step, arrived] = rep_copy(t, step, arrived)
                    start(reps[t, step, arrived])
                start(core_copy(t, arrived))
    for copy in started:
        copy.wait_send()
    for t in range(last):
        if units[t][3]:
            for n in range(replicas if spread[units[t][0]] else 1):
                core_copy(t, n).wait_recv()
    for m in own_outs:
        own_outs[m].wait()
        own_cores[m].wait_recv()


def gather_rows(arrays, spread, placed, units, collective_id, begun=None):
    begun = begun or {}
    replicas, shards = lax.axis_size("rep"), lax.axis_size("shard")
    levels = shards // 2
    count = len(arrays)
    owns = [
        w.reshape((replicas, w.shape[0] // replicas) + w.shape[1:]) if wide else w
        for w, wide in zip(arrays, spread)
    ]
    slots = len(units) * replicas
    any_space = pl.BlockSpec(memory_space=pl.ANY)
    dma = pltpu.SemaphoreType.DMA
    size = sum(w.size * w.dtype.itemsize for w in arrays)
    staging = [
        pltpu.VMEM(w.shape if put else (8, 128), w.dtype if put else jnp.float32)
        for w, put in zip(owns, placed)
    ]
    return pl.pallas_call(
        functools.partial(gather_kernel, levels, replicas, spread, placed, len(begun), tuple(units)),
        out_shape=[jax.ShapeDtypeStruct((shards,) + w.shape, w.dtype) for w in owns],
        in_specs=[any_space] * (count + len(begun)),
        out_specs=[any_space] * count,
        scratch_shapes=staging
        + [
            dma((2 * count,)),
            dma((len(units),)),
            dma((len(units),)),
            dma((slots,)),
            dma((slots,)),
            dma((slots + count,)),
            dma((slots + count,)),
        ],
        input_output_aliases={count + n: m for n, m in enumerate(begun)},
        compiler_params=pltpu.CompilerParams(
            collective_id=collective_id, has_side_effects=True, vmem_limit_bytes=size + (1 << 20)
        ),
        cost_estimate=pl.CostEstimate(flops=0, transcendentals=0, bytes_accessed=30 * size),
    )(*owns, *begun.values())


def kept_behind(block, array):
    first = lax.slice(array, (0,) * array.ndim, (1,) * array.ndim).reshape(())
    return jnp.where(first == first, block, jnp.zeros_like(block))


def plain(full):
    return full.reshape(-1, full.shape[-1])


def behind(numbers, top, *arrays):
    for array in arrays:
        first = lax.slice(array, (0,) * array.ndim, (1,) * array.ndim).reshape(())
        numbers = numbers + (first != first).astype(jnp.int32)
    return jnp.clip(numbers, 0, top)


def gradient_kernel(places, left, left_far, right, right_far, keep, leave, total):
    sums = cross(left[...], right[...]) + cross(left_far[...], right_far[...])
    parts, part = total.shape[0], total.shape[1]
    for q in range(parts):
        total[q] = sums[q * part : (q + 1) * part].astype(total.dtype)
    half = parts // 2
    for slot in range(half):
        keep[slot, 0] = total[places[1 + slot]]
        leave[slot, 0] = total[places[1 + half + slot]]


def slot_parts():
    bits = lax.axis_size("rep").bit_length() - 1
    r = lax.axis_index("rep")
    core = lax.rem(lax.axis_index("shard"), 2)
    lists = []
    for c in range(2):
        masks = [0]
        for step in reversed(range(bits)):
            masks = masks + [m ^ (1 << bit_of(step, c)) for m in masks]
        lists.append(masks)
    return [jnp.where(core == 0, a, b) ^ r for a, b in zip(*lists)]


def chip_gradient(left, right, *first):
    replicas, shards = lax.axis_size("rep"), lax.axis_size("shard")
    levels = shards // 2
    core = lax.rem(lax.axis_index("shard"), 2)
    tokens, height = left.shape
    columns = right.shape[1]
    rows = height // shards
    part = rows // replicas
    even, odd = [
        jnp.concatenate(
            [left[:, (2 * z + c) * rows : (2 * z + c + 1) * rows] for z in range(levels)], axis=1
        )
        for c in range(2)
    ]
    left_far = swap_core(jnp.where(core == 0, odd, even))
    right_far = swap_core(right)
    wide = min(columns, (1 << 18) // rows)
    places = jnp.stack([core] + slot_parts()).astype(jnp.int32)
    half = (replicas // 2, levels, part, columns)
    half_spec = pl.BlockSpec((replicas // 2, 1, part, wide), lambda n, z, places: (0, z, 0, n))
    return pl.pallas_call(
        gradient_kernel,
        out_shape=[jax.ShapeDtypeStruct(half, jnp.bfloat16)] * 2,
        grid_spec=pltpu.PrefetchScalarGridSpec(
            num_scalar_prefetch=1,
            grid=(columns // wide, levels),
            in_specs=[
                pl.BlockSpec((tokens, rows), lambda n, z, places: (0, 2 * z + places[0])),
                pl.BlockSpec((tokens, rows), lambda n, z, places: (0, z)),
                pl.BlockSpec((tokens, wide), lambda n, z, places: (0, n)),
                pl.BlockSpec((tokens, wide), lambda n, z, places: (0, n)),
            ],
            out_specs=[half_spec] * 2,
            scratch_shapes=[pltpu.VMEM((replicas, part, wide), jnp.bfloat16)],
        ),
        compiler_params=pltpu.CompilerParams(vmem_limit_bytes=40 << 20),
        cost_estimate=pl.CostEstimate(
            flops=2 * tokens * height * columns,
            transcendentals=0,
            bytes_accessed=2 * (2 * tokens + height // 2) * columns + 2 * tokens * height,
        ),
    )(behind(places, replicas - 1, *first), left, left_far, right, right_far)


def add_low(*terms):
    return sum(term.astype(jnp.float32) for term in terms).astype(jnp.bfloat16)


def halve_rep(total):
    keep, leave = total
    bits = lax.axis_size("rep").bit_length() - 1
    first = swap_rep(leave, 0)
    terms = [keep, first]
    for step in range(1, bits):
        half = terms[0].shape[0] // 2
        arrived = swap_rep(add_low(*[term[half : 2 * half] for term in terms]), step)
        terms = [term[:half] for term in terms] + [arrived]
    return first, add_low(*[term[0] for term in terms])


def ring_sum(plane):
    levels = plane.shape[0]
    z = lax.div(lax.axis_index("shard"), 2)
    travelling = lax.dynamic_index_in_dim(plane, lax.rem(z + levels - 1, levels), 0, keepdims=False)
    for step in range(1, levels):
        arrived = ring_next(travelling)
        own = lax.dynamic_index_in_dim(
            plane, lax.rem(z + 2 * levels - 1 - step, levels), 0, keepdims=False
        )
        travelling = add_low(own, arrived)
    return travelling


def owned_kernel(tiles, places, *refs):
    pieces, out = refs[:-1], refs[-1]
    replicas = out.shape[0]
    begin = 0
    for n, size in enumerate(tiles):
        own = pieces[n * replicas : (n + 1) * replicas]

        @pl.when((pl.program_id(0) >= begin) & (pl.program_id(0) < begin + size))
        def _(own=own):
            for k in range(replicas):
                out[places[k]] = own[k][...].astype(out.dtype)

        begin += size


def owned_rows(blocks):
    replicas = lax.axis_size("rep")
    r = lax.axis_index("rep")
    core = lax.rem(lax.axis_index("shard"), 2)
    part = blocks[0].shape[0]
    wide = min(1024, min(block.shape[1] for block in blocks))
    tiles = [block.shape[1] // wide for block in blocks]
    in_specs, pieces, begin = [], [], 0
    for block, size in zip(blocks, tiles):
        spec = pl.BlockSpec(
            (part, wide),
            lambda n, places, begin=begin, size=size: (0, jnp.clip(n - begin, 0, size - 1)),
        )
        in_specs += [spec] * replicas
        pieces += spread_rep(block)
        begin += size
    places = jnp.stack(rep_positions(core, r)).astype(jnp.int32)
    out = pl.pallas_call(
        functools.partial(owned_kernel, tiles),
        out_shape=jax.ShapeDtypeStruct((replicas, part, begin * wide), jnp.float32),
        grid_spec=pltpu.PrefetchScalarGridSpec(
            num_scalar_prefetch=1,
            grid=(begin,),
            in_specs=in_specs,
            out_specs=pl.BlockSpec((replicas, part, wide), lambda n, places: (0, 0, n)),
        ),
        compiler_params=pltpu.CompilerParams(vmem_limit_bytes=40 << 20),
        cost_estimate=pl.CostEstimate(
            flops=0, transcendentals=0, bytes_accessed=6 * replicas * part * begin * wide
        ),
    )(places, *pieces)
    return out.reshape(replicas * part, begin * wide)


def sum_along(block, axis):
    size = lax.axis_size(axis)
    step = 1
    while step < size:
        block = block + lax.ppermute(block, axis, [(n, n ^ step) for n in range(size)])
        step *= 2
    return block


def sum_everywhere(block):
    return sum_along(sum_along(block, "shard"), "rep")


def owned_sums(vectors, summed):
    shards = lax.axis_size("shard")
    shard_index = lax.axis_index("shard")
    joint = jnp.concatenate([vector.reshape(shards, -1) for vector in vectors], axis=1)
    total = summed(joint)
    mine = lax.dynamic_index_in_dim(total, shard_index, 0, keepdims=False)
    parts, begin = [], 0
    for vector in vectors:
        size = vector.shape[0] // shards
        parts.append(mine[begin : begin + size])
        begin += size
    return parts


def per_device(
    x_prompt,
    x_cont,
    teacher_prompt,
    teacher_cont,
    valid_mask,
    group_of,
    ln1_gain,
    ln1_bias,
    w_qkv,
    q_bias,
    v_bias,
    w_out,
    out_bias,
    ln2_gain,
    ln2_bias,
    w_up,
    up_bias,
    w_down,
    down_bias,
):
    shards = lax.axis_size("shard")
    replicas = lax.axis_size("rep")
    shard_index = lax.axis_index("shard")
    prompt_count, prompt_rows, width = x_prompt.shape
    cont_rows = x_cont.shape[0]
    cont_count, cont_len = valid_mask.shape
    prompt_len = prompt_rows * shards
    prompt_total = prompt_count * prompt_rows
    head_count = width // HEAD_DIM
    all_tokens = replicas * shards * (prompt_total + cont_rows)
    valid_local = jnp.sum(valid_mask.astype(jnp.float32)) + prompt_total
    vectors = (
        ln1_gain,
        ln1_bias,
        q_bias,
        v_bias,
        out_bias,
        ln2_gain,
        ln2_bias,
        up_bias,
        down_bias,
    )
    starts = [0]
    for vector in vectors:
        starts.append(starts[-1] + vector.shape[0])
    filled = -(starts[-1] + 1) % 1024
    joint = jnp.concatenate(
        [vector.astype(jnp.float32) for vector in vectors]
        + [valid_local[None], jnp.zeros((filled,), jnp.float32)]
    ).reshape(8, -1)
    levels = shards // 2
    steps = range(1, levels)
    ahead = (levels - 1) * 2 // 3
    first_units = [(m, j, True, True) for j in steps for m in (2, 0, 1)]
    first_units += [(3, j, True, False) for j in steps if j <= ahead]
    q_full, kv_full, joint, up_begun = gather_rows(
        [w_qkv[:, :width], w_qkv[:, width:], joint, w_up],
        (True, True, False, True),
        (True, True, True, False),
        first_units,
        0,
    )
    q_full, kv_full = plain(q_full), plain(kv_full)
    joint = joint.reshape(shards, -1)
    (
        gain_one,
        shift_one,
        bias_query,
        bias_value,
        bias_out,
        gain_two,
        shift_two,
        bias_up,
        bias_down,
    ) = [joint[:, begin:end].reshape(-1) for begin, end in zip(starts[:-1], starts[1:])]
    valid_group = jnp.broadcast_to(jnp.sum(joint[:, starts[-1]]), (8, 128))
    valid_all = sum_along(valid_group, "rep")[0, 0]
    loss_scale = all_tokens / valid_all
    inputs = jnp.concatenate([x_prompt.reshape(prompt_total, width), x_cont], axis=0).astype(
        jnp.float32
    )
    normed, unit_one, inverse_one = norm_forward(inputs, gain_one, shift_one)
    normed_low = normed.astype(jnp.bfloat16)
    queries = jnp.dot(normed_low, q_full, preferred_element_type=jnp.float32)
    queries = (queries + bias_query).astype(jnp.bfloat16)
    pair_bias = jnp.concatenate([jnp.zeros_like(bias_value), bias_value])
    pair_rows = jnp.dot(normed_low, kv_full, preferred_element_type=jnp.float32)
    pair_rows = (pair_rows + pair_bias).astype(jnp.bfloat16)
    local_pairs = pair_rows[:prompt_total].reshape(prompt_count, prompt_rows, 2 * width)
    own_pairs = pair_rows[prompt_total:]
    second_units = [(2, j, False, True) for j in steps if j <= ahead]
    for j in steps:
        second_units += [(1, j, True, True), (0, j, True, True), (3, j, True, True)]
        if j > ahead:
            second_units.append((2, j, True, True))
    prompt_pairs, out_full, up_full, down_full = gather_rows(
        [local_pairs, w_out, w_up, w_down],
        (False, True, True, True),
        (True, True, True, True),
        second_units,
        1,
        {2: up_begun},
    )
    out_full, up_full, down_full = plain(out_full), plain(up_full), plain(down_full)
    sizes = (prompt_count, prompt_rows, cont_count, cont_len)
    places = jnp.concatenate([(shard_index * prompt_rows)[None], group_of]).astype(jnp.int32)
    joined_rows = (queries, own_pairs)
    attended, log_totals = attention_call(sizes, joined_rows, prompt_pairs, places)
    middle = inputs + jnp.dot(attended, out_full, preferred_element_type=jnp.float32) + bias_out
    normed_two, unit_two, inverse_two = norm_forward(middle, gain_two, shift_two)
    normed_two_low = normed_two.astype(jnp.bfloat16)
    upward = jnp.dot(normed_two_low, up_full, preferred_element_type=jnp.float32) + bias_up
    active_low = gelu_tanh(upward).astype(jnp.bfloat16)
    result = middle + jnp.dot(active_low, down_full, preferred_element_type=jnp.float32) + bias_down
    out_prompt = (
        result[:prompt_total].reshape(prompt_count, prompt_rows, width).astype(jnp.bfloat16)
    )
    out_cont = result[prompt_total:].astype(jnp.bfloat16)
    targets = jnp.concatenate(
        [teacher_prompt.reshape(prompt_total, width), teacher_cont], axis=0
    ).astype(jnp.float32)
    weight_rows = jnp.concatenate(
        [jnp.ones((prompt_total,), jnp.float32), valid_mask.reshape(cont_rows).astype(jnp.float32)]
    )
    out_grad = (loss_scale * weight_rows)[:, None] * (result - targets)
    mlp_grad = out_grad.astype(jnp.bfloat16)
    grad_bias_down = jnp.sum(mlp_grad, axis=0, dtype=jnp.float32)
    down_total = chip_gradient(active_low, mlp_grad)
    down_first, down_plane = halve_rep(down_total)
    active_grad = back_product(kept_behind(mlp_grad, down_total[0]), down_full)
    unused_value, gelu_pull = jax.vjp(gelu_tanh, upward)
    upward_grad = gelu_pull(active_grad)[0].astype(jnp.bfloat16)
    grad_bias_up = jnp.sum(upward_grad, axis=0, dtype=jnp.float32)
    up_total = chip_gradient(normed_two_low, upward_grad)
    up_first, up_plane = halve_rep(up_total)
    normed_two_grad = back_product(kept_behind(upward_grad, up_total[0]), up_full)
    middle_step, grad_gain_two, grad_shift_two = norm_backward(
        normed_two_grad, unit_two, inverse_two, gain_two
    )
    middle_grad = out_grad + middle_step
    branch_grad = middle_grad.astype(jnp.bfloat16)
    grad_bias_out = jnp.sum(branch_grad, axis=0, dtype=jnp.float32)
    attended_grad = back_product(branch_grad, out_full).astype(jnp.bfloat16)
    later_places = behind(places, prompt_rows * shards, up_total[0], down_first)
    query_part, pair_grad, own_key_grad, own_value_grad = attention_call(
        sizes, joined_rows, prompt_pairs, later_places, (log_totals, attended_grad)
    )
    out_first, out_plane = halve_rep(chip_gradient(attended, branch_grad))
    q_first, q_plane = halve_rep(chip_gradient(normed_low, query_part))
    down_owned = ring_sum(down_plane)
    owned_keys, owned_values = lax.psum_scatter(pair_grad, "shard", scatter_dimension=0)
    pair_part = jnp.concatenate(
        [
            jnp.concatenate([owned_keys, owned_values], axis=2).reshape(prompt_total, 2 * width),
            jnp.concatenate([own_key_grad, own_value_grad], axis=1),
        ],
        axis=0,
    )
    grad_bias_query = jnp.sum(query_part, axis=0, dtype=jnp.float32)
    grad_bias_value = jnp.sum(pair_part[:, width:], axis=0, dtype=jnp.float32)
    normed_grad = back_product(query_part, q_full) + back_product(pair_part, kv_full)
    input_step, grad_gain_one, grad_shift_one = norm_backward(
        normed_grad, unit_one, inverse_one, gain_one
    )
    input_grad = middle_grad + input_step
    pair_first, pair_plane = halve_rep(
        chip_gradient(normed_low, pair_part, up_first, down_plane)
    )
    summed_down = owned_rows([down_owned])
    summed_up = owned_rows([ring_sum(up_plane)])
    summed_out = owned_rows([ring_sum(out_plane)])
    summed_qkv = owned_rows([ring_sum(q_plane), ring_sum(pair_plane)])
    early_sums = (grad_bias_out, grad_gain_two, grad_shift_two, grad_bias_up, grad_bias_down)
    late_sums = (grad_gain_one, grad_shift_one, grad_bias_query, grad_bias_value)
    owned_vectors = owned_sums(late_sums, sum_everywhere)
    owned_vectors += owned_sums(early_sums, lambda block: lax.psum(block, AXES))
    grad_prompt = input_grad[:prompt_total].reshape(prompt_count, prompt_rows, width)
    grad_cont = input_grad[prompt_total:]
    return (
        out_prompt,
        out_cont,
        grad_prompt,
        grad_cont,
        owned_vectors[0],
        owned_vectors[1],
        summed_qkv,
        owned_vectors[2],
        owned_vectors[3],
        summed_out,
        owned_vectors[4],
        owned_vectors[5],
        owned_vectors[6],
        summed_up,
        owned_vectors[7],
        summed_down,
        owned_vectors[8],
    )


def solution(mesh):
    in_specs = (
        P("rep", "shard", None),
        P(("rep", "shard"), None),
        P("rep", "shard", None),
        P(("rep", "shard"), None),
        P(("rep", "shard"), None),
        P(("rep", "shard")),
        P("shard"),
        P("shard"),
        P("shard", None),
        P("shard"),
        P("shard"),
        P("shard", None),
        P("shard"),
        P("shard"),
        P("shard"),
        P("shard", None),
        P("shard"),
        P("shard", None),
        P("shard"),
    )
    out_specs = (
        P("rep", "shard", None),
        P(("rep", "shard"), None),
        P("rep", "shard", None),
        P(("rep", "shard"), None),
        P("shard"),
        P("shard"),
        P("shard", None),
        P("shard"),
        P("shard"),
        P("shard", None),
        P("shard"),
        P("shard"),
        P("shard"),
        P("shard", None),
        P("shard"),
        P("shard", None),
        P("shard"),
    )
    return jax.shard_map(
        per_device, mesh=mesh, in_specs=in_specs, out_specs=out_specs, check_vma=False
    )
```

```python
import functools

import jax
import jax.numpy as jnp
from jax import lax
from jax.experimental import pallas as pl
from jax.experimental.pallas import tpu as pltpu
from jax.sharding import PartitionSpec as P

HEAD_DIM = 128
AXES = ("rep", "shard")


epsilon = 1e-05
gelu_coef = 0.7978845608028654


def gelu_tanh(values):
    return (
        0.5 * values * (1.0 + jnp.tanh(gelu_coef * (values + 0.044715 * values * values * values)))
    )


def norm_forward(inputs, norm_gain, norm_shift):
    centered = inputs - jnp.mean(inputs, axis=-1, keepdims=True)
    variance = jnp.mean(centered * centered, axis=-1, keepdims=True)
    inverse = lax.rsqrt(variance + epsilon)
    unit_rows = centered * inverse
    return (unit_rows * norm_gain + norm_shift, unit_rows, inverse)


def norm_backward(upstream, unit_rows, inverse, norm_gain):
    scaled = upstream * norm_gain
    centered = (
        scaled
        - jnp.mean(scaled, axis=-1, keepdims=True)
        - unit_rows * jnp.mean(scaled * unit_rows, axis=-1, keepdims=True)
    )
    return (centered * inverse, jnp.sum(upstream * unit_rows, axis=0), jnp.sum(upstream, axis=0))


def cross(left, right):
    return lax.dot_general(
        left, right, (((0,), (0,)), ((), ())), preferred_element_type=jnp.float32
    )


def back_product(left, right):
    return lax.dot_general(
        left, right, (((1,), (1,)), ((), ())), preferred_element_type=jnp.float32
    )


def dot_last(left, right):
    return back_product(left, right)


def causal_scores(queries, keys, factor, slope, key_start, query_start, masked):
    scores = dot_last(queries, keys) * factor
    key_pos = key_start + lax.broadcasted_iota(jnp.int32, (1, keys.shape[0]), 1)
    scores = scores + slope * (key_pos - query_start).astype(jnp.float32)
    if masked:
        query_pos = query_start + lax.broadcasted_iota(jnp.int32, (queries.shape[0], 1), 0)
        scores = jnp.where(key_pos <= query_pos, scores, -1e30)
    return scores


def all_rows(ref, prompt):
    return ref[:, prompt].reshape(-1, ref.shape[-1])


def forward_kernel(sizes, places, slopes, q_ref, k_ref, v_ref, own_k_ref, own_v_ref, out_ref, lse_ref):
    prompt_count, prompt_rows, cont_count, cont_len = sizes
    prompt_total = prompt_count * prompt_rows
    prompt_len = k_ref.shape[0] * prompt_rows
    slope = slopes[pl.program_id(0)]
    factor = q_ref.shape[1] ** (-0.5)
    for p in range(prompt_count):
        rows = slice(p * prompt_rows, (p + 1) * prompt_rows)
        scores = causal_scores(q_ref[rows], all_rows(k_ref, p), factor, slope, 0, places[0], True)
        largest = jnp.max(scores, axis=-1, keepdims=True)
        terms = jnp.exp(scores - largest)
        total = jnp.sum(terms, axis=-1, keepdims=True)
        probs = (terms / total).astype(jnp.bfloat16)
        mixed = jnp.dot(probs, all_rows(v_ref, p), preferred_element_type=jnp.float32)
        out_ref[rows] = mixed.astype(out_ref.dtype)
        lse_ref[0, rows] = largest + jnp.log(total)
    for c in range(cont_count):
        own = slice(c * cont_len, (c + 1) * cont_len)
        rows = slice(prompt_total + c * cont_len, prompt_total + (c + 1) * cont_len)
        group = places[1 + c]
        far = causal_scores(q_ref[rows], all_rows(k_ref, group), factor, slope, 0, prompt_len, False)
        near = causal_scores(q_ref[rows], own_k_ref[own], factor, slope, prompt_len, prompt_len, True)
        largest = jnp.maximum(
            jnp.max(far, axis=-1, keepdims=True), jnp.max(near, axis=-1, keepdims=True)
        )
        far, near = jnp.exp(far - largest), jnp.exp(near - largest)
        total = jnp.sum(far, axis=-1, keepdims=True) + jnp.sum(near, axis=-1, keepdims=True)
        mixed = jnp.dot(
            (far / total).astype(jnp.bfloat16), all_rows(v_ref, group), preferred_element_type=jnp.float32
        ) + jnp.dot(
            (near / total).astype(jnp.bfloat16), own_v_ref[own], preferred_element_type=jnp.float32
        )
        out_ref[rows] = mixed.astype(out_ref.dtype)
        lse_ref[0, rows] = largest + jnp.log(total)


def backward_kernel(
    sizes, places, slopes, q_ref, k_ref, v_ref, own_k_ref, own_v_ref, lse_ref, grad_ref,
    q_grad_ref, pair_grad_ref, own_grad_ref, k_sum, v_sum,
):
    prompt_count, prompt_rows, cont_count, cont_len = sizes
    prompt_total = prompt_count * prompt_rows
    prompt_len = k_ref.shape[0] * prompt_rows
    slope = slopes[pl.program_id(0)]
    factor = q_ref.shape[1] ** (-0.5)
    for p in range(prompt_count):
        rows = slice(p * prompt_rows, (p + 1) * prompt_rows)
        queries, grads = q_ref[rows], grad_ref[rows]
        scores = causal_scores(queries, all_rows(k_ref, p), factor, slope, 0, places[0], True)
        probs = jnp.exp(scores - lse_ref[0, rows])
        prob_grad = dot_last(grads, all_rows(v_ref, p))
        inner = jnp.sum(probs * prob_grad, axis=-1, keepdims=True)
        score_grad = (probs * (prob_grad - inner)).astype(jnp.bfloat16)
        q_grad = jnp.dot(score_grad, all_rows(k_ref, p), preferred_element_type=jnp.float32) * factor
        q_grad_ref[rows] = q_grad.astype(q_grad_ref.dtype)
        k_sum[p] = cross(score_grad, queries) * factor
        v_sum[p] = cross(probs.astype(jnp.bfloat16), grads)
    for c in range(cont_count):
        own = slice(c * cont_len, (c + 1) * cont_len)
        rows = slice(prompt_total + c * cont_len, prompt_total + (c + 1) * cont_len)
        group = places[1 + c]
        queries, grads = q_ref[rows], grad_ref[rows]
        far_keys, near_keys = all_rows(k_ref, group), own_k_ref[own]
        far = causal_scores(queries, far_keys, factor, slope, 0, prompt_len, False)
        near = causal_scores(queries, near_keys, factor, slope, prompt_len, prompt_len, True)
        far, near = jnp.exp(far - lse_ref[0, rows]), jnp.exp(near - lse_ref[0, rows])
        far_grad, near_grad = dot_last(grads, all_rows(v_ref, group)), dot_last(grads, own_v_ref[own])
        inner = jnp.sum(far * far_grad, axis=-1, keepdims=True)
        inner = inner + jnp.sum(near * near_grad, axis=-1, keepdims=True)
        far_grad = (far * (far_grad - inner)).astype(jnp.bfloat16)
        near_grad = (near * (near_grad - inner)).astype(jnp.bfloat16)
        q_grad = jnp.dot(far_grad, far_keys, preferred_element_type=jnp.float32)
        q_grad = q_grad + jnp.dot(near_grad, near_keys, preferred_element_type=jnp.float32)
        q_grad_ref[rows] = (q_grad * factor).astype(q_grad_ref.dtype)
        k_sum[group] = k_sum[group] + cross(far_grad, queries) * factor
        v_sum[group] = v_sum[group] + cross(far.astype(jnp.bfloat16), grads)
        own_grad_ref[0, own] = (cross(near_grad, queries) * factor).astype(own_grad_ref.dtype)
        own_grad_ref[1, own] = cross(near.astype(jnp.bfloat16), grads).astype(own_grad_ref.dtype)
    for p in range(prompt_count):
        for piece in range(prompt_len // prompt_rows):
            rows = slice(piece * prompt_rows, (piece + 1) * prompt_rows)
            pair_grad_ref[piece, 0, p] = k_sum[p, rows].astype(pair_grad_ref.dtype)
            pair_grad_ref[piece, 1, p] = v_sum[p, rows].astype(pair_grad_ref.dtype)


def attention_call(sizes, joined_rows, pairs, places, more=None):
    prompt_count, prompt_rows, cont_count, cont_len = sizes
    tokens, width = joined_rows[0].shape
    prompt_len = pairs.shape[0] * prompt_rows
    heads = width // HEAD_DIM
    cont_rows = cont_count * cont_len
    slopes = 2.0 ** (-8.0 * (jnp.arange(heads, dtype=jnp.float32) + 1.0) / heads)
    by_head = pl.BlockSpec((tokens, HEAD_DIM), lambda h, *_: (0, h))
    own_head = pl.BlockSpec((cont_rows, HEAD_DIM), lambda h, *_: (0, h))
    pair_block = pairs.shape[:3] + (HEAD_DIM,)
    keys = pl.BlockSpec(pair_block, lambda h, *_: (0, 0, 0, h))
    values = pl.BlockSpec(pair_block, lambda h, *_: (0, 0, 0, heads + h))
    stats = pl.BlockSpec((1, tokens, 1), lambda h, *_: (h, 0, 0))
    stats_shape = jax.ShapeDtypeStruct((heads, tokens, 1), jnp.float32)
    rows_shape = jax.ShapeDtypeStruct((tokens, width), jnp.bfloat16)
    own_shape = jax.ShapeDtypeStruct((2, cont_rows, width), jnp.bfloat16)
    queries, own_pairs = joined_rows
    own_values = pl.BlockSpec((cont_rows, HEAD_DIM), lambda h, *_: (0, heads + h))
    inputs = (queries, pairs, pairs, own_pairs, own_pairs)
    in_specs = [by_head, keys, values, own_head, own_values]
    pieces = prompt_len // prompt_rows
    scores = tokens * (prompt_len + cont_len) * heads
    if more is None:
        kernel, scratch, products = forward_kernel, [], 2
        out_shape, out_specs = (rows_shape, stats_shape), (by_head, stats)
    else:
        kernel, products = backward_kernel, 5
        scratch = [pltpu.VMEM((prompt_count, prompt_len, HEAD_DIM), jnp.float32)] * 2
        inputs += more
        in_specs += [stats, by_head]
        piece_shape = jax.ShapeDtypeStruct(
            (pieces, 2, prompt_count, prompt_rows, width), jnp.bfloat16
        )
        piece = pl.BlockSpec(
            (pieces, 2, prompt_count, prompt_rows, HEAD_DIM), lambda h, *_: (0, 0, 0, 0, h)
        )
        own_grad = pl.BlockSpec((2, cont_rows, HEAD_DIM), lambda h, *_: (0, 0, h))
        out_shape = (rows_shape, piece_shape, own_shape)
        out_specs = (by_head, piece, own_grad)
    return pl.pallas_call(
        functools.partial(kernel, sizes),
        out_shape=out_shape,
        grid_spec=pltpu.PrefetchScalarGridSpec(
            num_scalar_prefetch=2,
            grid=(heads,),
            in_specs=in_specs,
            out_specs=out_specs,
            scratch_shapes=scratch,
        ),
        compiler_params=pltpu.CompilerParams(vmem_limit_bytes=40 << 20),
        cost_estimate=pl.CostEstimate(
            flops=2 * products * scores * HEAD_DIM,
            transcendentals=scores,
            bytes_accessed=8 * prompt_count * prompt_len * width,
        ),
    )(places, slopes, *inputs)


def send(block, target):
    replicas, shards = lax.axis_size("rep"), lax.axis_size("shard")
    pairs = []
    for r in range(replicas):
        for s in range(shards):
            r_to, z_to, c_to = target(r, s // 2, s % 2)
            pairs.append((r * shards + s, r_to * shards + 2 * z_to + c_to))
    return lax.ppermute(block, AXES, pairs)


def swap_core(block):
    return send(block, lambda r, z, c: (r, z, 1 - c))


def bit_of(step, core):
    bits = lax.axis_size("rep").bit_length() - 1
    return step if core == 0 else bits - 1 - step


def mask_lists():
    bits = lax.axis_size("rep").bit_length() - 1
    lists = []
    for core in range(2):
        masks = [0]
        for step in range(bits):
            masks += [m ^ (1 << bit_of(step, core)) for m in masks]
        lists.append(masks)
    return lists


MESH_ID = pl.DeviceIdType.MESH


def gather_kernel(levels, replicas, spread, placed, begun, units, *refs):
    count = len(spread)
    owns, fulls = refs[:count], refs[count + begun : 2 * count + begun]
    staged = refs[2 * count + begun : 3 * count + begun]
    own_sem, ring_send, ring_recv, rep_send, rep_recv, core_send, core_recv = refs[3 * count + begun :]
    bits = replicas.bit_length() - 1
    r, s = lax.axis_index("rep"), lax.axis_index("shard")
    core, z = lax.rem(s, 2), lax.div(s, 2)
    other = {"shard": s + 1 - 2 * core}
    ring_to = {"shard": lax.rem(s + 2, 2 * levels)}
    ring_from = {"shard": lax.rem(s + 2 * levels - 2, 2 * levels)}
    rep_to = [{"rep": r ^ jnp.where(core == 0, 1 << bit_of(n, 0), 1 << bit_of(n, 1))} for n in range(bits)]
    barrier = pltpu.get_barrier_semaphore()
    partners = [ring_to, ring_from, other] + rep_to
    for partner in partners:
        pl.semaphore_signal(barrier, inc=1, device_id=partner, device_id_type=MESH_ID)
    pl.semaphore_wait(barrier, len(partners))
    lists = mask_lists()
    place = [jnp.where(core == 0, a, b) ^ r for a, b in zip(*lists)]

    def piece_of(m, j, n):
        block = fulls[m].at[2 * lax.rem(z - j + levels, levels) + core]
        return block.at[place[n]] if spread[m] else block

    def remote(source, target, sends, recvs, n, device):
        return pltpu.make_async_remote_copy(
            src_ref=source,
            dst_ref=target,
            send_sem=sends.at[n],
            recv_sem=recvs.at[n],
            device_id=device,
            device_id_type=MESH_ID,
        )

    def ring_copy(t):
        m, j = units[t][:2]
        target = piece_of(m, j - 1, 0)
        own = owns[m].at[r] if spread[m] else owns[m]
        return remote(own if j == 1 else target, target, ring_send, ring_recv, t, ring_to)

    def rep_copy(t, step, n):
        piece = piece_of(*units[t][:2], n)
        return remote(piece, piece, rep_send, rep_recv, t * replicas + (1 << step) + n, rep_to[step])

    def core_copy(t, n):
        piece = piece_of(*units[t][:2], n)
        return remote(piece, piece, core_send, core_recv, t * replicas + n, other)

    last = len(units)
    goes = [t for t in range(last) if units[t][2]]
    ready = {}
    for n, t in enumerate(goes):
        m, j = units[t][:2]
        needs = [goes[n - 3]] if n >= 3 else []
        needs += [e for e in goes[:n] if units[e][:2] == (m, j - 1)]
        ready.setdefault(max(needs, default=-1), []).append(t)
    started = []

    def start(copy):
        copy.start()
        started.append(copy)

    rings = {t: ring_copy(t) for t in goes}
    reps = {}
    for t in ready.get(-1, []):
        start(rings[t])
    own_ins, own_outs, own_cores = {}, {}, {}
    for m in range(count):
        if placed[m]:
            own_ins[m] = pltpu.make_async_copy(owns[m], staged[m], own_sem.at[2 * m])
            own_outs[m] = pltpu.make_async_copy(staged[m], fulls[m].at[s], own_sem.at[2 * m + 1])
            own_cores[m] = remote(
                staged[m], fulls[m].at[s], core_send, core_recv, last * replicas + m, other
            )
            own_ins[m].start()
    for m in own_ins:
        own_ins[m].wait()
        own_outs[m].start()
        start(own_cores[m])
    for tick in range(last + bits):
        t = tick
        if t < last:
            if units[t][2]:
                rings[t].wait_recv()
                for later in ready.get(t, []):
                    start(rings[later])
            if units[t][3]:
                if spread[units[t][0]]:
                    for step in range(bits):
                        reps[t, step, 0] = rep_copy(t, step, 0)
                        start(reps[t, step, 0])
                start(core_copy(t, 0))
        for lag in range(1, bits + 1):
            t = tick - lag
            if not 0 <= t < last or not units[t][3] or not spread[units[t][0]]:
                continue
            got = lag - 1
            for n in range(1 << got):
                reps[t, got, n].wait_recv()
                arrived = (1 << got) + n
                for step in range(got + 1, bits):
                    reps[t, step, arrived] = rep_copy(t, step, arrived)
                    start(reps[t, step, arrived])
                start(core_copy(t, arrived))
    for copy in started:
        copy.wait_send()
    for t in range(last):
        if units[t][3]:
            for n in range(replicas if spread[units[t][0]] else 1):
                core_copy(t, n).wait_recv()
    for m in own_outs:
        own_outs[m].wait()
        own_cores[m].wait_recv()


def gather_rows(arrays, spread, placed, units, collective_id, begun=None):
    begun = begun or {}
    replicas, shards = lax.axis_size("rep"), lax.axis_size("shard")
    levels = shards // 2
    count = len(arrays)
    owns = [
        w.reshape((replicas, w.shape[0] // replicas) + w.shape[1:]) if wide else w
        for w, wide in zip(arrays, spread)
    ]
    slots = len(units) * replicas
    any_space = pl.BlockSpec(memory_space=pl.ANY)
    dma = pltpu.SemaphoreType.DMA
    size = sum(w.size * w.dtype.itemsize for w in arrays)
    staging = [
        pltpu.VMEM(w.shape if put else (8, 128), w.dtype if put else jnp.float32)
        for w, put in zip(owns, placed)
    ]
    return pl.pallas_call(
        functools.partial(gather_kernel, levels, replicas, spread, placed, len(begun), tuple(units)),
        out_shape=[jax.ShapeDtypeStruct((shards,) + w.shape, w.dtype) for w in owns],
        in_specs=[any_space] * (count + len(begun)),
        out_specs=[any_space] * count,
        scratch_shapes=staging
        + [
            dma((2 * count,)),
            dma((len(units),)),
            dma((len(units),)),
            dma((slots,)),
            dma((slots,)),
            dma((slots + count,)),
            dma((slots + count,)),
        ],
        input_output_aliases={count + n: m for n, m in enumerate(begun)},
        compiler_params=pltpu.CompilerParams(
            collective_id=collective_id, has_side_effects=True, vmem_limit_bytes=size + (1 << 20)
        ),
        cost_estimate=pl.CostEstimate(flops=0, transcendentals=0, bytes_accessed=30 * size),
    )(*owns, *begun.values())


def kept_behind(block, array):
    first = lax.slice(array, (0,) * array.ndim, (1,) * array.ndim).reshape(())
    return jnp.where(first == first, block, jnp.zeros_like(block))


def plain(full):
    return full.reshape(-1, full.shape[-1])


def behind(numbers, top, *arrays):
    for array in arrays:
        first = lax.slice(array, (0,) * array.ndim, (1,) * array.ndim).reshape(())
        numbers = numbers + (first != first).astype(jnp.int32)
    return jnp.clip(numbers, 0, top)


def token_products(left, left_far, rights):
    sums, half = None, len(rights) // 2
    for source, blocks in ((left, rights[:half]), (left_far, rights[half:])):
        begin = 0
        for block in blocks:
            rows = block.shape[1]
            term = cross(source[begin : begin + rows], block[0])
            sums = term if sums is None else sums + term
            begin += rows
    return sums


def gradient_kernel(count, places, left, left_far, *refs):
    rights, (keep, leave, total) = refs[:count], refs[count:]
    sums = token_products(left, left_far, rights)
    parts, part = total.shape[0], total.shape[1]
    for q in range(parts):
        total[q] = sums[q * part : (q + 1) * part].astype(total.dtype)
    half = parts // 2
    for slot in range(half):
        keep[slot, 0] = total[places[1 + slot]]
        leave[slot, 0] = total[places[1 + half + slot]]


def whole_kernel(count, places, left, left_far, *refs):
    rights, out = refs[:count], refs[count]
    sums = token_products(left, left_far, rights)
    part = out.shape[2]
    for q in range(out.shape[0]):
        out[q, 0] = sums[q * part : (q + 1) * part].astype(out.dtype)


def slot_parts():
    bits = lax.axis_size("rep").bit_length() - 1
    r = lax.axis_index("rep")
    core = lax.rem(lax.axis_index("shard"), 2)
    lists = []
    for c in range(2):
        masks = [0]
        for step in reversed(range(bits)):
            masks = masks + [m ^ (1 << bit_of(step, c)) for m in masks]
        lists.append(masks)
    return [jnp.where(core == 0, a, b) ^ r for a, b in zip(*lists)]


def chip_gradient(left, rights, halves=True, after=()):
    replicas, shards = lax.axis_size("rep"), lax.axis_size("shard")
    levels = shards // 2
    core = lax.rem(lax.axis_index("shard"), 2)
    tokens, height = left.shape
    blocks, _, width = rights[0].shape
    columns = blocks * width
    rows = height // shards
    part = rows // replicas
    even, odd = [
        jnp.concatenate(
            [left[:, (2 * z + c) * rows : (2 * z + c + 1) * rows] for z in range(levels)], axis=1
        )
        for c in range(2)
    ]
    left_far = swap_core(jnp.where(core == 0, odd, even))
    rights = list(rights) + [swap_core(right) for right in rights]
    wide = min(width, (1 << 18) // rows)
    each = width // wide
    places = jnp.stack([core] + slot_parts()).astype(jnp.int32)
    slots = replicas // 2 if halves else replicas
    out_shape = jax.ShapeDtypeStruct((slots, levels, part, columns), jnp.bfloat16)
    out_spec = pl.BlockSpec((slots, 1, part, wide), lambda n, z, places: (0, z, 0, n))
    kernel = gradient_kernel if halves else whole_kernel
    return pl.pallas_call(
        functools.partial(kernel, len(rights)),
        out_shape=[out_shape] * 2 if halves else out_shape,
        grid_spec=pltpu.PrefetchScalarGridSpec(
            num_scalar_prefetch=1,
            grid=(columns // wide, levels),
            in_specs=[
                pl.BlockSpec((tokens, rows), lambda n, z, places: (0, 2 * z + places[0])),
                pl.BlockSpec((tokens, rows), lambda n, z, places: (0, z)),
            ]
            + [
                pl.BlockSpec((1, right.shape[1], wide), lambda n, z, places: (n // each, 0, n % each))
                for right in rights
            ],
            out_specs=[out_spec] * 2 if halves else out_spec,
            scratch_shapes=[pltpu.VMEM((replicas, part, wide), jnp.bfloat16)] if halves else [],
        ),
        compiler_params=pltpu.CompilerParams(vmem_limit_bytes=40 << 20),
        cost_estimate=pl.CostEstimate(
            flops=2 * tokens * height * columns,
            transcendentals=0,
            bytes_accessed=2 * (2 * tokens + height // 2) * columns + 2 * tokens * height,
        ),
    )(behind(places, replicas - 1, *after), left, left_far, *rights)


def sum_plane(total):
    return lax.psum_scatter(total, "rep", scatter_dimension=0)


def sum_levels(plane):
    shards = lax.axis_size("shard")
    pairs = [list(range(core, shards, 2)) for core in range(2)]
    return lax.psum_scatter(plane, "shard", scatter_dimension=0, axis_index_groups=pairs)


def tie_kernel(block, other, out):
    del block, other, out


def tied(block, other):
    any_space = pl.BlockSpec(memory_space=pl.ANY)
    return pl.pallas_call(
        tie_kernel,
        out_shape=jax.ShapeDtypeStruct(block.shape, block.dtype),
        in_specs=[any_space] * 2,
        out_specs=any_space,
        input_output_aliases={0: 0},
        compiler_params=pltpu.CompilerParams(has_side_effects=True),
    )(block, other)


def add_slabs(target, *terms):
    rows = target.shape[0]
    slab = min(32, rows)

    @pl.loop(0, rows // slab)
    def _(n):
        at = pl.ds(pl.multiple_of(n * slab, slab), slab)
        target[at] = sum(term[at].astype(jnp.float32) for term in terms).astype(target.dtype)


def sum_kernel(levels, replicas, kinds, counts, *refs):
    bits = replicas.bit_length() - 1
    r, s = lax.axis_index("rep"), lax.axis_index("shard")
    core, z = lax.rem(s, 2), lax.div(s, 2)
    other = {"shard": s + 1 - 2 * core}
    ring_to = {"shard": lax.rem(s + 2, 2 * levels)}
    ring_from = {"shard": lax.rem(s + 2 * levels - 2, 2 * levels)}
    rep_to = [{"rep": r ^ jnp.where(core == 0, 1 << bit_of(n, 0), 1 << bit_of(n, 1))} for n in range(bits)]
    lists = mask_lists()
    place = [jnp.where(core == 0, a, b) ^ r for a, b in zip(*lists)]
    ins, outs, scratch = [], [], []
    at = 0
    for kind in kinds:
        size = 2 if kind == "full" else 1
        ins.append(refs[at : at + size])
        at += size
    outs = refs[at : at + len(kinds)]
    at += len(kinds)
    for count in counts:
        scratch.append(refs[at : at + count])
        at += count
    crowd = []
    if "vectors" in kinds:
        crowd = [{"shard": s ^ (1 << n)} for n in range((2 * levels).bit_length() - 1)]
        crowd += [{"rep": r ^ (1 << n)} for n in range(bits)]
    barrier = pltpu.get_barrier_semaphore()
    partners = [ring_to, ring_from, other] + rep_to + crowd
    for partner in partners:
        pl.semaphore_signal(barrier, inc=1, device_id=partner, device_id_type=MESH_ID)
    pl.semaphore_wait(barrier, len(partners))

    level = [lax.rem(z + 2 * levels - 1 - i, levels) for i in range(levels)]
    sent = []

    def remote(source, target, sends, recvs, n, device):
        return pltpu.make_async_remote_copy(
            src_ref=source,
            dst_ref=target,
            send_sem=sends.at[n],
            recv_sem=recvs.at[n],
            device_id=device,
            device_id_type=MESH_ID,
        )

    def start(copy):
        copy.start()
        sent.append(copy)

    def offset(step):
        return replicas - (replicas >> step)

    class Job:
        def __init__(self, kind, ins, out, scratch):
            self.kind, self.ins, self.out = kind, ins, out
            self.held, self.came, self.ring = scratch[:3]
            self.load_sem, self.send_sem, self.recv_sem = scratch[3:6]
            self.ring_send, self.ring_recv, self.rep_send, self.rep_recv, self.own_sem = scratch[6:]

        def load(self, i, k=0):
            if self.kind == "pairs":
                source = self.ins[0].at[2 * level[i] + core]
            elif self.kind == "full":
                source = self.ins[0].at[k, level[i]]
            elif self.kind == "plane":
                source = self.ins[0].at[level[i]]
            else:
                source = self.ins[0].at[0]
            slots = self.held.shape[1]
            return pltpu.make_async_copy(source, self.held.at[i, k], self.load_sem.at[i * slots + k])

        def loads(self):
            return [(i, k) for i in range(self.held.shape[0]) for k in range(self.held.shape[1])]

        def exchange(self, i, step, k):
            n = i * self.came.shape[1] + offset(step) + k
            target = self.came.at[i, offset(step) + k]
            if self.kind == "pairs":
                source, device = self.ins[0].at[2 * level[i] + 1 - core], other
            else:
                device = rep_to[step]
                source = self.ins[1].at[k, level[i]] if step == 0 else self.held.at[i, (replicas >> (step + 1)) + k]
            return remote(source, target, self.send_sem, self.recv_sem, n, device)

        def ring_copy(self, i):
            return remote(self.held.at[i, 0], self.ring.at[i], self.ring_send, self.ring_recv, i, ring_to)

        def rep_copy(self, step, n):
            piece = self.out.at[place[n]]
            source = self.held.at[self.held.shape[0] - 1, 0] if n == 0 else piece
            return remote(source, piece, self.rep_send, self.rep_recv, (1 << step) + n, rep_to[step])

        def begin(self):
            for i, k in self.loads():
                self.load(i, k).start()
            if self.kind in ("pairs", "full"):
                slots = 1 if self.kind == "pairs" else replicas // 2
                for i in range(levels):
                    for k in range(slots):
                        start(self.exchange(i, 0, k))

        def halve(self, i, step):
            if self.kind != "full":
                return
            half = replicas >> (step + 1)
            if step == 0:
                for k in range(replicas // 2):
                    self.load(i, k).wait()
            for k in range(half):
                self.exchange(i, step, k).wait_recv()
            if step + 1 < bits:
                for k in range(half // 2, half):
                    held = self.held.at[i, k]
                    add_slabs(held, held, *[self.came.at[i, offset(n) + k] for n in range(step + 1)])
                    start(self.exchange(i, step + 1, k - half // 2))

        def forward(self, i):
            held = self.held.at[i, 0]
            terms = [held]
            if self.kind == "full":
                terms += [self.came.at[i, offset(n)] for n in range(bits)]
            else:
                self.load(i).wait()
            if self.kind == "pairs":
                self.exchange(i, 0, 0).wait_recv()
                terms.append(self.came.at[i, 0])
            if i > 0:
                self.ring_copy(i - 1).wait_recv()
                terms.append(self.ring.at[i - 1])
            if len(terms) > 1:
                add_slabs(held, *terms)
            if i < levels - 1:
                start(self.ring_copy(i))
            else:
                self.finish()

        def own_out(self):
            target = self.out if self.kind == "pairs" else self.out.at[r]
            final = self.held.at[self.held.shape[0] - 1, 0]
            return pltpu.make_async_copy(final, target, self.own_sem.at[0])

        def finish(self):
            self.own_out().start()
            if self.kind != "pairs":
                for step in range(bits):
                    start(self.rep_copy(step, 0))

        def spread(self, got):
            if self.kind == "pairs":
                return
            for n in range(1 << got):
                self.rep_copy(got, n).wait_recv()
                for step in range(got + 1, bits):
                    start(self.rep_copy(step, (1 << got) + n))

    class Vectors:
        def __init__(self, kind, ins, out, scratch):
            self.kind, self.out = kind, out
            self.held, self.came, self.load_sem, self.send_sem, self.recv_sem, own_sem = scratch
            self.first = pltpu.make_async_copy(ins[0], self.held.at[0], self.load_sem.at[0])
            self.final = pltpu.make_async_copy(self.held.at[len(crowd)], out, own_sem.at[0])
            self.done = 0

        def begin(self):
            self.first.start()

        def exchange(self, n):
            return remote(
                self.held.at[n], self.came.at[n], self.send_sem, self.recv_sem, n, crowd[n]
            )

        def go_on(self):
            n = self.done
            if n > len(crowd):
                return
            if n == 0:
                self.first.wait()
            else:
                self.exchange(n - 1).wait_recv()
                self.held[n] = self.held[n - 1] + self.came[n - 1]
            if n < len(crowd):
                start(self.exchange(n))
            else:
                self.final.start()
            self.done += 1

        def own_out(self):
            return self.final

    jobs = [
        (Vectors if parts[0] == "vectors" else Job)(*parts)
        for parts in zip(kinds, ins, outs, scratch)
    ]
    for job in jobs:
        job.begin()
    plain_jobs = [job for job in jobs if job.kind in ("pairs", "plane")]
    full_jobs = [job for job in jobs if job.kind == "full"]
    vector_jobs = [job for job in jobs if job.kind == "vectors"]
    spread_jobs = [job for job in jobs if job.kind == "spread"]
    for job in plain_jobs:
        job.forward(0)
    for job in spread_jobs:
        job.load(0).wait()
        job.finish()
    for i in range(levels):
        for job in vector_jobs:
            job.go_on()
        if i + 1 < levels:
            for job in plain_jobs:
                job.forward(i + 1)
        for job in full_jobs:
            job.halve(i, 0)
        if i > 0 and i <= bits:
            for job in spread_jobs:
                job.spread(i - 1)
        for step in range(1, bits):
            for job in full_jobs:
                job.halve(i, step)
        for job in full_jobs:
            job.forward(i)
    for got in range(bits):
        late = [job for job in spread_jobs if got >= levels - 1]
        for job in plain_jobs + full_jobs + late:
            job.spread(got)
        for job in vector_jobs:
            job.go_on()
    for job in vector_jobs:
        while job.done <= len(crowd):
            job.go_on()
    for copy in sent:
        copy.wait_send()
    for job in jobs:
        job.own_out().wait()


def sum_arrays(jobs, collective_id):
    replicas, shards = lax.axis_size("rep"), lax.axis_size("shard")
    levels = shards // 2
    dma = pltpu.SemaphoreType.DMA
    any_space = pl.BlockSpec(memory_space=pl.ANY)
    scratch, counts, out_shape, size, total = [], [], [], 0, 0
    exchanges = (shards * replicas).bit_length() - 1
    for kind, arrays in jobs:
        block = arrays[0].shape[-2:]
        dtype = arrays[0].dtype
        total += sum(array.size for array in arrays)
        if kind == "vectors":
            own = [
                pltpu.VMEM((exchanges + 1,) + block, dtype),
                pltpu.VMEM((exchanges,) + block, dtype),
                dma((1,)),
                dma((exchanges,)),
                dma((exchanges,)),
                dma((1,)),
            ]
            scratch += own
            counts.append(len(own))
            size += 4 * block[0] * block[1] * (2 * exchanges + 1)
            out_shape.append(jax.ShapeDtypeStruct(block, dtype))
            continue
        slots = replicas // 2 if kind == "full" else 1
        chunks = 1 if kind == "spread" else levels
        came = {"pairs": 1, "full": replicas - 1}.get(kind, 0)
        own = [
            pltpu.VMEM((chunks, slots) + block, dtype),
            pltpu.VMEM((levels, came) + block if came else (16, 128), dtype),
            pltpu.VMEM((levels - 1,) + block if kind != "spread" else (16, 128), dtype),
            dma((levels * slots,)),
            dma((levels * max(came, 1),)),
            dma((levels * max(came, 1),)),
            dma((levels,)),
            dma((levels,)),
            dma((replicas,)),
            dma((replicas,)),
            dma((1,)),
        ]
        scratch += own
        counts.append(len(own))
        size += 2 * block[0] * block[1] * (chunks * (slots + came) + chunks - 1)
        out_shape.append(jax.ShapeDtypeStruct(block if kind == "pairs" else (replicas,) + block, dtype))
    kinds = tuple(kind for kind, _ in jobs)
    operands = [array for _, arrays in jobs for array in arrays]
    return pl.pallas_call(
        functools.partial(sum_kernel, levels, replicas, kinds, tuple(counts)),
        out_shape=out_shape,
        in_specs=[any_space] * len(operands),
        out_specs=[any_space] * len(jobs),
        scratch_shapes=scratch,
        compiler_params=pltpu.CompilerParams(
            collective_id=collective_id, has_side_effects=True, vmem_limit_bytes=size + (4 << 20)
        ),
        cost_estimate=pl.CostEstimate(flops=total, transcendentals=0, bytes_accessed=20 * total),
    )(*operands)


def sum_along(block, axis):
    size = lax.axis_size(axis)
    step = 1
    while step < size:
        block = block + lax.ppermute(block, axis, [(n, n ^ step) for n in range(size)])
        step *= 2
    return block


def per_device(
    x_prompt,
    x_cont,
    teacher_prompt,
    teacher_cont,
    valid_mask,
    group_of,
    ln1_gain,
    ln1_bias,
    w_qkv,
    q_bias,
    v_bias,
    w_out,
    out_bias,
    ln2_gain,
    ln2_bias,
    w_up,
    up_bias,
    w_down,
    down_bias,
):
    shards = lax.axis_size("shard")
    replicas = lax.axis_size("rep")
    shard_index = lax.axis_index("shard")
    prompt_count, prompt_rows, width = x_prompt.shape
    cont_rows = x_cont.shape[0]
    cont_count, cont_len = valid_mask.shape
    prompt_len = prompt_rows * shards
    prompt_total = prompt_count * prompt_rows
    head_count = width // HEAD_DIM
    all_tokens = replicas * shards * (prompt_total + cont_rows)
    valid_local = jnp.sum(valid_mask.astype(jnp.float32)) + prompt_total
    vectors = (
        ln1_gain,
        ln1_bias,
        q_bias,
        v_bias,
        out_bias,
        ln2_gain,
        ln2_bias,
        up_bias,
        down_bias,
    )
    starts = [0]
    for vector in vectors:
        starts.append(starts[-1] + vector.shape[0])
    filled = -(starts[-1] + 1) % 1024
    joint = jnp.concatenate(
        [vector.astype(jnp.float32) for vector in vectors]
        + [valid_local[None], jnp.zeros((filled,), jnp.float32)]
    ).reshape(8, -1)
    levels = shards // 2
    steps = range(1, levels)
    ahead = (levels - 1) * 2 // 3
    first_units = [(m, j, True, True) for j in steps for m in (2, 0, 1)]
    first_units += [(3, j, True, False) for j in steps if j <= ahead]
    q_full, kv_full, joint, up_begun = gather_rows(
        [w_qkv[:, :width], w_qkv[:, width:], joint, w_up],
        (True, True, False, True),
        (True, True, True, False),
        first_units,
        0,
    )
    q_full, kv_full = plain(q_full), plain(kv_full)
    joint = joint.reshape(shards, -1)
    (
        gain_one,
        shift_one,
        bias_query,
        bias_value,
        bias_out,
        gain_two,
        shift_two,
        bias_up,
        bias_down,
    ) = [joint[:, begin:end].reshape(-1) for begin, end in zip(starts[:-1], starts[1:])]
    valid_group = jnp.broadcast_to(jnp.sum(joint[:, starts[-1]]), (8, 128))
    valid_all = sum_along(valid_group, "rep")[0, 0]
    loss_scale = all_tokens / valid_all
    inputs = jnp.concatenate([x_prompt.reshape(prompt_total, width), x_cont], axis=0).astype(
        jnp.float32
    )
    normed, unit_one, inverse_one = norm_forward(inputs, gain_one, shift_one)
    normed_low = normed.astype(jnp.bfloat16)
    queries = jnp.dot(normed_low, q_full, preferred_element_type=jnp.float32)
    queries = (queries + bias_query).astype(jnp.bfloat16)
    pair_bias = jnp.concatenate([jnp.zeros_like(bias_value), bias_value])
    pair_rows = jnp.dot(normed_low, kv_full, preferred_element_type=jnp.float32)
    pair_rows = (pair_rows + pair_bias).astype(jnp.bfloat16)
    local_pairs = pair_rows[:prompt_total].reshape(prompt_count, prompt_rows, 2 * width)
    own_pairs = pair_rows[prompt_total:]
    second_units = [(2, j, False, True) for j in steps if j <= ahead]
    for j in steps:
        second_units += [(1, j, True, True), (3, j, True, True)]
        if j > ahead:
            second_units.append((2, j, True, True))
        second_units.append((0, j, True, True))
    prompt_pairs, out_full, up_full, down_full = gather_rows(
        [local_pairs, w_out, w_up, w_down],
        (False, True, True, True),
        (True, True, True, True),
        second_units,
        1,
        {2: up_begun},
    )
    out_full, up_full, down_full = plain(out_full), plain(up_full), plain(down_full)
    sizes = (prompt_count, prompt_rows, cont_count, cont_len)
    places = jnp.concatenate([(shard_index * prompt_rows)[None], group_of]).astype(jnp.int32)
    joined_rows = (queries, own_pairs)
    attended, log_totals = attention_call(sizes, joined_rows, prompt_pairs, places)
    middle = inputs + jnp.dot(attended, out_full, preferred_element_type=jnp.float32) + bias_out
    normed_two, unit_two, inverse_two = norm_forward(middle, gain_two, shift_two)
    normed_two_low = normed_two.astype(jnp.bfloat16)
    upward = jnp.dot(normed_two_low, up_full, preferred_element_type=jnp.float32) + bias_up
    active_low = gelu_tanh(upward).astype(jnp.bfloat16)
    result = middle + jnp.dot(active_low, down_full, preferred_element_type=jnp.float32) + bias_down
    out_prompt = (
        result[:prompt_total].reshape(prompt_count, prompt_rows, width).astype(jnp.bfloat16)
    )
    out_cont = result[prompt_total:].astype(jnp.bfloat16)
    targets = jnp.concatenate(
        [teacher_prompt.reshape(prompt_total, width), teacher_cont], axis=0
    ).astype(jnp.float32)
    weight_rows = jnp.concatenate(
        [jnp.ones((prompt_total,), jnp.float32), valid_mask.reshape(cont_rows).astype(jnp.float32)]
    )
    out_grad = (loss_scale * weight_rows)[:, None] * (result - targets)
    mlp_grad = out_grad.astype(jnp.bfloat16)
    grad_bias_down = jnp.sum(mlp_grad, axis=0, dtype=jnp.float32)
    down_total = chip_gradient(active_low, [mlp_grad[None]], halves=False)
    down_plane = sum_plane(down_total)
    active_grad = back_product(kept_behind(mlp_grad, down_total), down_full)
    unused_value, gelu_pull = jax.vjp(gelu_tanh, upward)
    upward_grad = gelu_pull(active_grad)[0].astype(jnp.bfloat16)
    grad_bias_up = jnp.sum(upward_grad, axis=0, dtype=jnp.float32)
    up_total = chip_gradient(normed_two_low, [upward_grad[None]], halves=False)
    up_plane = sum_plane(up_total)
    normed_two_grad = back_product(upward_grad, up_full)
    middle_step, grad_gain_two, grad_shift_two = norm_backward(
        normed_two_grad, unit_two, inverse_two, gain_two
    )
    middle_grad = out_grad + middle_step
    branch_grad = middle_grad.astype(jnp.bfloat16)
    grad_bias_out = jnp.sum(branch_grad, axis=0, dtype=jnp.float32)
    attended_grad = back_product(branch_grad, out_full).astype(jnp.bfloat16)
    later_places = places
    query_part, pair_grad, own_grad = attention_call(
        sizes, joined_rows, prompt_pairs, later_places, (log_totals, attended_grad)
    )
    down_owned = sum_levels(tied(down_plane, query_part))
    out_total = chip_gradient(attended, [branch_grad[None]])
    q_total = chip_gradient(normed_low, [query_part[None]], after=[up_total])
    owned_pairs, out_parts, q_parts = sum_arrays(
        [
            ("pairs", [pair_grad.reshape(shards, -1, width)]),
            ("full", out_total),
            ("full", q_total),
        ],
        2,
    )
    owned_grad = owned_pairs.reshape(2, prompt_total, width)
    pair_total = chip_gradient(normed_low, [owned_grad, own_grad])
    grad_bias_query = jnp.sum(query_part, axis=0, dtype=jnp.float32)
    grad_bias_value = jnp.sum(owned_grad[1], axis=0, dtype=jnp.float32)
    grad_bias_value = grad_bias_value + jnp.sum(own_grad[1], axis=0, dtype=jnp.float32)
    key_part, value_part = [
        jnp.concatenate([owned_grad[n], own_grad[n]], axis=0) for n in range(2)
    ]
    normed_grad = (
        back_product(query_part, q_full)
        + back_product(key_part, kv_full[:, :width])
        + back_product(value_part, kv_full[:, width:])
    )
    input_step, grad_gain_one, grad_shift_one = norm_backward(
        normed_grad, unit_one, inverse_one, gain_one
    )
    input_grad = middle_grad + input_step
    vector_grads = (
        grad_gain_one,
        grad_shift_one,
        grad_bias_query,
        grad_bias_value,
        grad_bias_out,
        grad_gain_two,
        grad_shift_two,
        grad_bias_up,
        grad_bias_down,
    )
    joint_grads = jnp.concatenate([vector.reshape(shards, -1) for vector in vector_grads], axis=1)
    pair_parts, down_parts, up_parts, joint_sums = sum_arrays(
        [
            ("full", pair_total),
            ("spread", [down_owned[None]]),
            ("plane", [up_plane]),
            ("vectors", [joint_grads]),
        ],
        3,
    )
    summed_down, summed_up, summed_out = [
        plain(parts).astype(jnp.float32) for parts in (down_parts, up_parts, out_parts)
    ]
    summed_qkv = jnp.concatenate([plain(q_parts), plain(pair_parts)], axis=1).astype(jnp.float32)
    own_sums = lax.dynamic_index_in_dim(joint_sums, shard_index, 0, keepdims=False)
    owned_vectors = [own_sums[begin:end] for begin, end in zip(starts[:-1], starts[1:])]
    grad_prompt = input_grad[:prompt_total].reshape(prompt_count, prompt_rows, width)
    grad_cont = input_grad[prompt_total:]
    return (
        out_prompt,
        out_cont,
        grad_prompt,
        grad_cont,
        owned_vectors[0],
        owned_vectors[1],
        summed_qkv,
        owned_vectors[2],
        owned_vectors[3],
        summed_out,
        owned_vectors[4],
        owned_vectors[5],
        owned_vectors[6],
        summed_up,
        owned_vectors[7],
        summed_down,
        owned_vectors[8],
    )


def solution(mesh):
    in_specs = (
        P("rep", "shard", None),
        P(("rep", "shard"), None),
        P("rep", "shard", None),
        P(("rep", "shard"), None),
        P(("rep", "shard"), None),
        P(("rep", "shard")),
        P("shard"),
        P("shard"),
        P("shard", None),
        P("shard"),
        P("shard"),
        P("shard", None),
        P("shard"),
        P("shard"),
        P("shard"),
        P("shard", None),
        P("shard"),
        P("shard", None),
        P("shard"),
    )
    out_specs = (
        P("rep", "shard", None),
        P(("rep", "shard"), None),
        P("rep", "shard", None),
        P(("rep", "shard"), None),
        P("shard"),
        P("shard"),
        P("shard", None),
        P("shard"),
        P("shard"),
        P("shard", None),
        P("shard"),
        P("shard"),
        P("shard"),
        P("shard", None),
        P("shard"),
        P("shard", None),
        P("shard"),
    )
    return jax.shard_map(
        per_device, mesh=mesh, in_specs=in_specs, out_specs=out_specs, check_vma=False
    )
```

```python
import functools

import jax
import jax.numpy as jnp
from jax import lax
from jax.experimental import pallas as pl
from jax.experimental.pallas import tpu as pltpu
from jax.sharding import PartitionSpec as P

HEAD_DIM = 128
AXES = ("rep", "shard")


epsilon = 1e-05
gelu_coef = 0.7978845608028654


def norm_forward(inputs, norm_gain, norm_shift):
    centered = inputs - jnp.mean(inputs, axis=-1, keepdims=True)
    variance = jnp.mean(centered * centered, axis=-1, keepdims=True)
    inverse = lax.rsqrt(variance + epsilon)
    unit_rows = centered * inverse
    return (unit_rows * norm_gain + norm_shift, unit_rows, inverse)


def norm_backward(upstream, unit_rows, inverse, norm_gain):
    scaled = upstream * norm_gain
    centered = (
        scaled
        - jnp.mean(scaled, axis=-1, keepdims=True)
        - unit_rows * jnp.mean(scaled * unit_rows, axis=-1, keepdims=True)
    )
    return (centered * inverse, jnp.sum(upstream * unit_rows, axis=0), jnp.sum(upstream, axis=0))


def cross(left, right):
    return lax.dot_general(
        left, right, (((0,), (0,)), ((), ())), preferred_element_type=jnp.float32
    )


def back_product(left, right):
    return lax.dot_general(
        left, right, (((1,), (1,)), ((), ())), preferred_element_type=jnp.float32
    )


def dot_last(left, right):
    return back_product(left, right)


def causal_scores(queries, keys, factor, slope, key_start, query_start, masked):
    scores = dot_last(queries, keys) * factor
    key_pos = key_start + lax.broadcasted_iota(jnp.int32, (1, keys.shape[0]), 1)
    scores = scores + slope * (key_pos - query_start).astype(jnp.float32)
    if masked:
        query_pos = query_start + lax.broadcasted_iota(jnp.int32, (queries.shape[0], 1), 0)
        scores = jnp.where(key_pos <= query_pos, scores, -1e30)
    return scores


def all_rows(ref, prompt):
    return ref[:, prompt].reshape(-1, ref.shape[-1])


def forward_kernel(sizes, places, slopes, q_ref, k_ref, v_ref, own_k_ref, own_v_ref, out_ref, lse_ref):
    prompt_count, prompt_rows, cont_count, cont_len = sizes
    prompt_total = prompt_count * prompt_rows
    prompt_len = k_ref.shape[0] * prompt_rows
    slope = slopes[pl.program_id(0)]
    factor = q_ref.shape[1] ** (-0.5)
    for p in range(prompt_count):
        rows = slice(p * prompt_rows, (p + 1) * prompt_rows)
        scores = causal_scores(q_ref[rows], all_rows(k_ref, p), factor, slope, 0, places[0], True)
        largest = jnp.max(scores, axis=-1, keepdims=True)
        terms = jnp.exp(scores - largest)
        total = jnp.sum(terms, axis=-1, keepdims=True)
        probs = (terms / total).astype(jnp.bfloat16)
        mixed = jnp.dot(probs, all_rows(v_ref, p), preferred_element_type=jnp.float32)
        out_ref[rows] = mixed.astype(out_ref.dtype)
        lse_ref[0, rows] = largest + jnp.log(total)
    for c in range(cont_count):
        own = slice(c * cont_len, (c + 1) * cont_len)
        rows = slice(prompt_total + c * cont_len, prompt_total + (c + 1) * cont_len)
        group = places[1 + c]
        far = causal_scores(q_ref[rows], all_rows(k_ref, group), factor, slope, 0, prompt_len, False)
        near = causal_scores(q_ref[rows], own_k_ref[own], factor, slope, prompt_len, prompt_len, True)
        largest = jnp.maximum(
            jnp.max(far, axis=-1, keepdims=True), jnp.max(near, axis=-1, keepdims=True)
        )
        far, near = jnp.exp(far - largest), jnp.exp(near - largest)
        total = jnp.sum(far, axis=-1, keepdims=True) + jnp.sum(near, axis=-1, keepdims=True)
        mixed = jnp.dot(
            (far / total).astype(jnp.bfloat16), all_rows(v_ref, group), preferred_element_type=jnp.float32
        ) + jnp.dot(
            (near / total).astype(jnp.bfloat16), own_v_ref[own], preferred_element_type=jnp.float32
        )
        out_ref[rows] = mixed.astype(out_ref.dtype)
        lse_ref[0, rows] = largest + jnp.log(total)


def backward_kernel(
    sizes, places, slopes, q_ref, k_ref, v_ref, own_k_ref, own_v_ref, lse_ref, grad_ref,
    q_grad_ref, pair_grad_ref, own_grad_ref, k_sum, v_sum,
):
    prompt_count, prompt_rows, cont_count, cont_len = sizes
    prompt_total = prompt_count * prompt_rows
    prompt_len = k_ref.shape[0] * prompt_rows
    slope = slopes[pl.program_id(0)]
    factor = q_ref.shape[1] ** (-0.5)
    for p in range(prompt_count):
        rows = slice(p * prompt_rows, (p + 1) * prompt_rows)
        queries, grads = q_ref[rows], grad_ref[rows]
        scores = causal_scores(queries, all_rows(k_ref, p), factor, slope, 0, places[0], True)
        probs = jnp.exp(scores - lse_ref[0, rows])
        prob_grad = dot_last(grads, all_rows(v_ref, p))
        inner = jnp.sum(probs * prob_grad, axis=-1, keepdims=True)
        score_grad = (probs * (prob_grad - inner)).astype(jnp.bfloat16)
        q_grad = jnp.dot(score_grad, all_rows(k_ref, p), preferred_element_type=jnp.float32) * factor
        q_grad_ref[rows] = q_grad.astype(q_grad_ref.dtype)
        k_sum[p] = cross(score_grad, queries) * factor
        v_sum[p] = cross(probs.astype(jnp.bfloat16), grads)
    for c in range(cont_count):
        own = slice(c * cont_len, (c + 1) * cont_len)
        rows = slice(prompt_total + c * cont_len, prompt_total + (c + 1) * cont_len)
        group = places[1 + c]
        queries, grads = q_ref[rows], grad_ref[rows]
        far_keys, near_keys = all_rows(k_ref, group), own_k_ref[own]
        far = causal_scores(queries, far_keys, factor, slope, 0, prompt_len, False)
        near = causal_scores(queries, near_keys, factor, slope, prompt_len, prompt_len, True)
        far, near = jnp.exp(far - lse_ref[0, rows]), jnp.exp(near - lse_ref[0, rows])
        far_grad, near_grad = dot_last(grads, all_rows(v_ref, group)), dot_last(grads, own_v_ref[own])
        inner = jnp.sum(far * far_grad, axis=-1, keepdims=True)
        inner = inner + jnp.sum(near * near_grad, axis=-1, keepdims=True)
        far_grad = (far * (far_grad - inner)).astype(jnp.bfloat16)
        near_grad = (near * (near_grad - inner)).astype(jnp.bfloat16)
        q_grad = jnp.dot(far_grad, far_keys, preferred_element_type=jnp.float32)
        q_grad = q_grad + jnp.dot(near_grad, near_keys, preferred_element_type=jnp.float32)
        q_grad_ref[rows] = (q_grad * factor).astype(q_grad_ref.dtype)
        k_sum[group] = k_sum[group] + cross(far_grad, queries) * factor
        v_sum[group] = v_sum[group] + cross(far.astype(jnp.bfloat16), grads)
        own_grad_ref[0, own] = (cross(near_grad, queries) * factor).astype(own_grad_ref.dtype)
        own_grad_ref[1, own] = cross(near.astype(jnp.bfloat16), grads).astype(own_grad_ref.dtype)
    for p in range(prompt_count):
        for piece in range(prompt_len // prompt_rows):
            rows = slice(piece * prompt_rows, (piece + 1) * prompt_rows)
            pair_grad_ref[piece, 0, p] = k_sum[p, rows].astype(pair_grad_ref.dtype)
            pair_grad_ref[piece, 1, p] = v_sum[p, rows].astype(pair_grad_ref.dtype)


def attention_call(sizes, joined_rows, pairs, places, more=None):
    prompt_count, prompt_rows, cont_count, cont_len = sizes
    tokens, width = joined_rows[0].shape
    prompt_len = pairs.shape[0] * prompt_rows
    heads = width // HEAD_DIM
    cont_rows = cont_count * cont_len
    slopes = 2.0 ** (-8.0 * (jnp.arange(heads, dtype=jnp.float32) + 1.0) / heads)
    by_head = pl.BlockSpec((tokens, HEAD_DIM), lambda h, *_: (0, h))
    own_head = pl.BlockSpec((cont_rows, HEAD_DIM), lambda h, *_: (0, h))
    pair_block = pairs.shape[:3] + (HEAD_DIM,)
    keys = pl.BlockSpec(pair_block, lambda h, *_: (0, 0, 0, h))
    values = pl.BlockSpec(pair_block, lambda h, *_: (0, 0, 0, heads + h))
    stats = pl.BlockSpec((1, tokens, 1), lambda h, *_: (h, 0, 0))
    stats_shape = jax.ShapeDtypeStruct((heads, tokens, 1), jnp.float32)
    rows_shape = jax.ShapeDtypeStruct((tokens, width), jnp.bfloat16)
    own_shape = jax.ShapeDtypeStruct((2, cont_rows, width), jnp.bfloat16)
    queries, own_pairs = joined_rows
    own_values = pl.BlockSpec((cont_rows, HEAD_DIM), lambda h, *_: (0, heads + h))
    inputs = (queries, pairs, pairs, own_pairs, own_pairs)
    in_specs = [by_head, keys, values, own_head, own_values]
    pieces = prompt_len // prompt_rows
    scores = tokens * (prompt_len + cont_len) * heads
    if more is None:
        kernel, scratch, products = forward_kernel, [], 2
        out_shape, out_specs = (rows_shape, stats_shape), (by_head, stats)
    else:
        kernel, products = backward_kernel, 5
        scratch = [pltpu.VMEM((prompt_count, prompt_len, HEAD_DIM), jnp.float32)] * 2
        inputs += more
        in_specs += [stats, by_head]
        piece_shape = jax.ShapeDtypeStruct(
            (pieces, 2, prompt_count, prompt_rows, width), jnp.bfloat16
        )
        piece = pl.BlockSpec(
            (pieces, 2, prompt_count, prompt_rows, HEAD_DIM), lambda h, *_: (0, 0, 0, 0, h)
        )
        own_grad = pl.BlockSpec((2, cont_rows, HEAD_DIM), lambda h, *_: (0, 0, h))
        out_shape = (rows_shape, piece_shape, own_shape)
        out_specs = (by_head, piece, own_grad)
    return pl.pallas_call(
        functools.partial(kernel, sizes),
        out_shape=out_shape,
        grid_spec=pltpu.PrefetchScalarGridSpec(
            num_scalar_prefetch=2,
            grid=(heads,),
            in_specs=in_specs,
            out_specs=out_specs,
            scratch_shapes=scratch,
        ),
        compiler_params=pltpu.CompilerParams(vmem_limit_bytes=40 << 20),
        cost_estimate=pl.CostEstimate(
            flops=2 * products * scores * HEAD_DIM,
            transcendentals=scores,
            bytes_accessed=8 * prompt_count * prompt_len * width,
        ),
    )(places, slopes, *inputs)


def send(block, target):
    replicas, shards = lax.axis_size("rep"), lax.axis_size("shard")
    pairs = []
    for r in range(replicas):
        for s in range(shards):
            r_to, z_to, c_to = target(r, s // 2, s % 2)
            pairs.append((r * shards + s, r_to * shards + 2 * z_to + c_to))
    return lax.ppermute(block, AXES, pairs)


def swap_core(block):
    return send(block, lambda r, z, c: (r, z, 1 - c))


def bit_of(step, core):
    bits = lax.axis_size("rep").bit_length() - 1
    return step if core == 0 else bits - 1 - step


def mask_lists():
    bits = lax.axis_size("rep").bit_length() - 1
    lists = []
    for core in range(2):
        masks = [0]
        for step in range(bits):
            masks += [m ^ (1 << bit_of(step, core)) for m in masks]
        lists.append(masks)
    return lists


MESH_ID = pl.DeviceIdType.MESH


def gather_kernel(levels, replicas, spread, placed, begun, units, *refs):
    count = len(spread)
    owns, fulls = refs[:count], refs[count + begun : 2 * count + begun]
    staged = refs[2 * count + begun : 3 * count + begun]
    own_sem, ring_send, ring_recv, rep_send, rep_recv, core_send, core_recv = refs[3 * count + begun :]
    bits = replicas.bit_length() - 1
    r, s = lax.axis_index("rep"), lax.axis_index("shard")
    core, z = lax.rem(s, 2), lax.div(s, 2)
    other = {"shard": s + 1 - 2 * core}
    ring_to = {"shard": lax.rem(s + 2, 2 * levels)}
    ring_from = {"shard": lax.rem(s + 2 * levels - 2, 2 * levels)}
    rep_to = [{"rep": r ^ jnp.where(core == 0, 1 << bit_of(n, 0), 1 << bit_of(n, 1))} for n in range(bits)]
    barrier = pltpu.get_barrier_semaphore()
    partners = [ring_to, ring_from, other] + rep_to
    for partner in partners:
        pl.semaphore_signal(barrier, inc=1, device_id=partner, device_id_type=MESH_ID)
    pl.semaphore_wait(barrier, len(partners))
    lists = mask_lists()
    place = [jnp.where(core == 0, a, b) ^ r for a, b in zip(*lists)]

    def piece_of(m, j, n):
        block = fulls[m].at[2 * lax.rem(z - j + levels, levels) + core]
        return block.at[place[n]] if spread[m] else block

    def remote(source, target, sends, recvs, n, device):
        return pltpu.make_async_remote_copy(
            src_ref=source,
            dst_ref=target,
            send_sem=sends.at[n],
            recv_sem=recvs.at[n],
            device_id=device,
            device_id_type=MESH_ID,
        )

    def ring_copy(t):
        m, j = units[t][:2]
        target = piece_of(m, j - 1, 0)
        own = owns[m].at[r] if spread[m] else owns[m]
        return remote(own if j == 1 else target, target, ring_send, ring_recv, t, ring_to)

    def rep_copy(t, step, n):
        piece = piece_of(*units[t][:2], n)
        return remote(piece, piece, rep_send, rep_recv, t * replicas + (1 << step) + n, rep_to[step])

    def core_copy(t, n):
        piece = piece_of(*units[t][:2], n)
        return remote(piece, piece, core_send, core_recv, t * replicas + n, other)

    last = len(units)
    goes = [t for t in range(last) if units[t][2]]
    ready = {}
    for n, t in enumerate(goes):
        m, j = units[t][:2]
        needs = [goes[n - 3]] if n >= 3 else []
        needs += [e for e in goes[:n] if units[e][:2] == (m, j - 1)]
        ready.setdefault(max(needs, default=-1), []).append(t)
    started = []

    def start(copy):
        copy.start()
        started.append(copy)

    rings = {t: ring_copy(t) for t in goes}
    reps = {}
    for t in ready.get(-1, []):
        start(rings[t])
    own_ins, own_outs, own_cores = {}, {}, {}
    for m in range(count):
        if placed[m]:
            own_ins[m] = pltpu.make_async_copy(owns[m], staged[m], own_sem.at[2 * m])
            own_outs[m] = pltpu.make_async_copy(staged[m], fulls[m].at[s], own_sem.at[2 * m + 1])
            own_cores[m] = remote(
                staged[m], fulls[m].at[s], core_send, core_recv, last * replicas + m, other
            )
            own_ins[m].start()
    for m in own_ins:
        own_ins[m].wait()
        own_outs[m].start()
        start(own_cores[m])
    for tick in range(last + bits):
        t = tick
        if t < last:
            if units[t][2]:
                rings[t].wait_recv()
                for later in ready.get(t, []):
                    start(rings[later])
            if units[t][3]:
                if spread[units[t][0]]:
                    for step in range(bits):
                        reps[t, step, 0] = rep_copy(t, step, 0)
                        start(reps[t, step, 0])
                start(core_copy(t, 0))
        for lag in range(1, bits + 1):
            t = tick - lag
            if not 0 <= t < last or not units[t][3] or not spread[units[t][0]]:
                continue
            got = lag - 1
            for n in range(1 << got):
                reps[t, got, n].wait_recv()
                arrived = (1 << got) + n
                for step in range(got + 1, bits):
                    reps[t, step, arrived] = rep_copy(t, step, arrived)
                    start(reps[t, step, arrived])
                start(core_copy(t, arrived))
    for copy in started:
        copy.wait_send()
    for t in range(last):
        if units[t][3]:
            for n in range(replicas if spread[units[t][0]] else 1):
                core_copy(t, n).wait_recv()
    for m in own_outs:
        own_outs[m].wait()
        own_cores[m].wait_recv()


def gather_rows(arrays, spread, placed, units, collective_id, begun=None):
    begun = begun or {}
    replicas, shards = lax.axis_size("rep"), lax.axis_size("shard")
    levels = shards // 2
    count = len(arrays)
    owns = [
        w.reshape((replicas, w.shape[0] // replicas) + w.shape[1:]) if wide else w
        for w, wide in zip(arrays, spread)
    ]
    slots = len(units) * replicas
    any_space = pl.BlockSpec(memory_space=pl.ANY)
    dma = pltpu.SemaphoreType.DMA
    size = sum(w.size * w.dtype.itemsize for w in arrays)
    staging = [
        pltpu.VMEM(w.shape if put else (8, 128), w.dtype if put else jnp.float32)
        for w, put in zip(owns, placed)
    ]
    return pl.pallas_call(
        functools.partial(gather_kernel, levels, replicas, spread, placed, len(begun), tuple(units)),
        out_shape=[jax.ShapeDtypeStruct((shards,) + w.shape, w.dtype) for w in owns],
        in_specs=[any_space] * (count + len(begun)),
        out_specs=[any_space] * count,
        scratch_shapes=staging
        + [
            dma((2 * count,)),
            dma((len(units),)),
            dma((len(units),)),
            dma((slots,)),
            dma((slots,)),
            dma((slots + count,)),
            dma((slots + count,)),
        ],
        input_output_aliases={count + n: m for n, m in enumerate(begun)},
        compiler_params=pltpu.CompilerParams(
            collective_id=collective_id, has_side_effects=True, vmem_limit_bytes=size + (1 << 20)
        ),
        cost_estimate=pl.CostEstimate(flops=0, transcendentals=0, bytes_accessed=30 * size),
    )(*owns, *begun.values())


def kept_behind(block, array):
    first = lax.slice(array, (0,) * array.ndim, (1,) * array.ndim).reshape(())
    return jnp.where(first == first, block, jnp.zeros_like(block))


def plain(full):
    return full.reshape(-1, full.shape[-1])


def behind(numbers, top, *arrays):
    for array in arrays:
        first = lax.slice(array, (0,) * array.ndim, (1,) * array.ndim).reshape(())
        numbers = numbers + (first != first).astype(jnp.int32)
    return jnp.clip(numbers, 0, top)


def token_products(left, left_far, rights):
    sums, half = None, len(rights) // 2
    for source, blocks in ((left, rights[:half]), (left_far, rights[half:])):
        begin = 0
        for block in blocks:
            rows = block.shape[1]
            term = cross(source[begin : begin + rows], block[0])
            sums = term if sums is None else sums + term
            begin += rows
    return sums


def gradient_kernel(count, places, left, left_far, *refs):
    rights, (keep, leave, total) = refs[:count], refs[count:]
    sums = token_products(left, left_far, rights)
    parts, part = total.shape[0], total.shape[1]
    for q in range(parts):
        total[q] = sums[q * part : (q + 1) * part].astype(total.dtype)
    half = parts // 2
    for slot in range(half):
        keep[slot, 0] = total[places[1 + slot]]
        leave[slot, 0] = total[places[1 + half + slot]]


def whole_kernel(count, places, left, left_far, *refs):
    rights, out = refs[:count], refs[count]
    sums = token_products(left, left_far, rights)
    part = out.shape[2]
    for q in range(out.shape[0]):
        out[q, 0] = sums[q * part : (q + 1) * part].astype(out.dtype)


def slot_parts():
    bits = lax.axis_size("rep").bit_length() - 1
    r = lax.axis_index("rep")
    core = lax.rem(lax.axis_index("shard"), 2)
    lists = []
    for c in range(2):
        masks = [0]
        for step in reversed(range(bits)):
            masks = masks + [m ^ (1 << bit_of(step, c)) for m in masks]
        lists.append(masks)
    return [jnp.where(core == 0, a, b) ^ r for a, b in zip(*lists)]


def chip_gradient(left, rights, halves=True, after=()):
    replicas, shards = lax.axis_size("rep"), lax.axis_size("shard")
    levels = shards // 2
    core = lax.rem(lax.axis_index("shard"), 2)
    tokens, height = left.shape
    blocks, _, width = rights[0].shape
    columns = blocks * width
    rows = height // shards
    part = rows // replicas
    even, odd = [
        jnp.concatenate(
            [left[:, (2 * z + c) * rows : (2 * z + c + 1) * rows] for z in range(levels)], axis=1
        )
        for c in range(2)
    ]
    left_far = swap_core(jnp.where(core == 0, odd, even))
    rights = list(rights) + [swap_core(right) for right in rights]
    wide = min(width, (1 << 18) // rows)
    each = width // wide
    places = jnp.stack([core] + slot_parts()).astype(jnp.int32)
    slots = replicas // 2 if halves else replicas
    out_shape = jax.ShapeDtypeStruct((slots, levels, part, columns), jnp.bfloat16)
    out_spec = pl.BlockSpec((slots, 1, part, wide), lambda n, z, places: (0, z, 0, n))
    kernel = gradient_kernel if halves else whole_kernel
    return pl.pallas_call(
        functools.partial(kernel, len(rights)),
        out_shape=[out_shape] * 2 if halves else out_shape,
        grid_spec=pltpu.PrefetchScalarGridSpec(
            num_scalar_prefetch=1,
            grid=(columns // wide, levels),
            in_specs=[
                pl.BlockSpec((tokens, rows), lambda n, z, places: (0, 2 * z + places[0])),
                pl.BlockSpec((tokens, rows), lambda n, z, places: (0, z)),
            ]
            + [
                pl.BlockSpec((1, right.shape[1], wide), lambda n, z, places: (n // each, 0, n % each))
                for right in rights
            ],
            out_specs=[out_spec] * 2 if halves else out_spec,
            scratch_shapes=[pltpu.VMEM((replicas, part, wide), jnp.bfloat16)] if halves else [],
        ),
        compiler_params=pltpu.CompilerParams(vmem_limit_bytes=40 << 20),
        cost_estimate=pl.CostEstimate(
            flops=2 * tokens * height * columns,
            transcendentals=0,
            bytes_accessed=2 * (2 * tokens + height // 2) * columns + 2 * tokens * height,
        ),
    )(behind(places, replicas - 1, *after), left, left_far, *rights)


def sum_plane(total):
    return lax.psum_scatter(total, "rep", scatter_dimension=0)


def sum_levels(plane):
    shards = lax.axis_size("shard")
    pairs = [list(range(core, shards, 2)) for core in range(2)]
    return lax.psum_scatter(plane, "shard", scatter_dimension=0, axis_index_groups=pairs)


def tie_kernel(block, other, out):
    del block, other, out


def tied(block, other):
    any_space = pl.BlockSpec(memory_space=pl.ANY)
    return pl.pallas_call(
        tie_kernel,
        out_shape=jax.ShapeDtypeStruct(block.shape, block.dtype),
        in_specs=[any_space] * 2,
        out_specs=any_space,
        input_output_aliases={0: 0},
        compiler_params=pltpu.CompilerParams(has_side_effects=True),
    )(block, other)


def add_slabs(target, *terms):
    rows = target.shape[0]
    slab = min(32, rows)

    @pl.loop(0, rows // slab)
    def _(n):
        at = pl.ds(pl.multiple_of(n * slab, slab), slab)
        target[at] = sum(term[at].astype(jnp.float32) for term in terms).astype(target.dtype)


def sum_kernel(levels, replicas, kinds, counts, *refs):
    bits = replicas.bit_length() - 1
    r, s = lax.axis_index("rep"), lax.axis_index("shard")
    core, z = lax.rem(s, 2), lax.div(s, 2)
    other = {"shard": s + 1 - 2 * core}
    ring_to = {"shard": lax.rem(s + 2, 2 * levels)}
    ring_from = {"shard": lax.rem(s + 2 * levels - 2, 2 * levels)}
    rep_to = [{"rep": r ^ jnp.where(core == 0, 1 << bit_of(n, 0), 1 << bit_of(n, 1))} for n in range(bits)]
    lists = mask_lists()
    place = [jnp.where(core == 0, a, b) ^ r for a, b in zip(*lists)]
    ins, outs, scratch = [], [], []
    at = 0
    for kind in kinds:
        size = 2 if kind == "full" else 1
        ins.append(refs[at : at + size])
        at += size
    outs = refs[at : at + len(kinds)]
    at += len(kinds)
    for count in counts:
        scratch.append(refs[at : at + count])
        at += count
    crowd = []
    if "vectors" in kinds:
        crowd = [{"shard": s ^ (1 << n)} for n in range((2 * levels).bit_length() - 1)]
        crowd += [{"rep": r ^ (1 << n)} for n in range(bits)]
    barrier = pltpu.get_barrier_semaphore()
    partners = [ring_to, ring_from, other] + rep_to + crowd
    for partner in partners:
        pl.semaphore_signal(barrier, inc=1, device_id=partner, device_id_type=MESH_ID)
    pl.semaphore_wait(barrier, len(partners))

    level = [lax.rem(z + 2 * levels - 1 - i, levels) for i in range(levels)]
    sent = []

    def remote(source, target, sends, recvs, n, device):
        return pltpu.make_async_remote_copy(
            src_ref=source,
            dst_ref=target,
            send_sem=sends.at[n],
            recv_sem=recvs.at[n],
            device_id=device,
            device_id_type=MESH_ID,
        )

    def start(copy):
        copy.start()
        sent.append(copy)

    def offset(step):
        return replicas - (replicas >> step)

    class Job:
        def __init__(self, kind, ins, out, scratch):
            self.kind, self.ins, self.out = kind, ins, out
            self.held, self.came, self.ring = scratch[:3]
            self.load_sem, self.send_sem, self.recv_sem = scratch[3:6]
            self.ring_send, self.ring_recv, self.rep_send, self.rep_recv, self.own_sem = scratch[6:]

        def load(self, i, k=0):
            if self.kind == "pairs":
                source = self.ins[0].at[2 * level[i] + core]
            elif self.kind == "full":
                source = self.ins[0].at[k, level[i]]
            elif self.kind == "plane":
                source = self.ins[0].at[level[i]]
            else:
                source = self.ins[0].at[0]
            slots = self.held.shape[1]
            return pltpu.make_async_copy(source, self.held.at[i, k], self.load_sem.at[i * slots + k])

        def loads(self):
            return [(i, k) for i in range(self.held.shape[0]) for k in range(self.held.shape[1])]

        def exchange(self, i, step, k):
            n = i * self.came.shape[1] + offset(step) + k
            target = self.came.at[i, offset(step) + k]
            if self.kind == "pairs":
                source, device = self.ins[0].at[2 * level[i] + 1 - core], other
            else:
                device = rep_to[step]
                source = self.ins[1].at[k, level[i]] if step == 0 else self.held.at[i, (replicas >> (step + 1)) + k]
            return remote(source, target, self.send_sem, self.recv_sem, n, device)

        def ring_copy(self, i):
            return remote(self.held.at[i, 0], self.ring.at[i], self.ring_send, self.ring_recv, i, ring_to)

        def rep_copy(self, step, n):
            piece = self.out.at[place[n]]
            source = self.held.at[self.held.shape[0] - 1, 0] if n == 0 else piece
            return remote(source, piece, self.rep_send, self.rep_recv, (1 << step) + n, rep_to[step])

        def begin(self):
            for i, k in self.loads():
                self.load(i, k).start()
            if self.kind in ("pairs", "full"):
                slots = 1 if self.kind == "pairs" else replicas // 2
                for i in range(levels):
                    for k in range(slots):
                        start(self.exchange(i, 0, k))

        def halve(self, i, step):
            if self.kind != "full":
                return
            half = replicas >> (step + 1)
            if step == 0:
                for k in range(replicas // 2):
                    self.load(i, k).wait()
            for k in range(half):
                self.exchange(i, step, k).wait_recv()
            if step + 1 < bits:
                for k in range(half // 2, half):
                    held = self.held.at[i, k]
                    add_slabs(held, held, *[self.came.at[i, offset(n) + k] for n in range(step + 1)])
                    start(self.exchange(i, step + 1, k - half // 2))

        def forward(self, i):
            held = self.held.at[i, 0]
            terms = [held]
            if self.kind == "full":
                terms += [self.came.at[i, offset(n)] for n in range(bits)]
            else:
                self.load(i).wait()
            if self.kind == "pairs":
                self.exchange(i, 0, 0).wait_recv()
                terms.append(self.came.at[i, 0])
            if i > 0:
                self.ring_copy(i - 1).wait_recv()
                terms.append(self.ring.at[i - 1])
            if len(terms) > 1:
                add_slabs(held, *terms)
            if i < levels - 1:
                start(self.ring_copy(i))
            else:
                self.finish()

        def own_out(self):
            target = self.out if self.kind == "pairs" else self.out.at[r]
            final = self.held.at[self.held.shape[0] - 1, 0]
            return pltpu.make_async_copy(final, target, self.own_sem.at[0])

        def finish(self):
            self.own_out().start()
            if self.kind != "pairs":
                for step in range(bits):
                    start(self.rep_copy(step, 0))

        def spread(self, got):
            if self.kind == "pairs":
                return
            for n in range(1 << got):
                self.rep_copy(got, n).wait_recv()
                for step in range(got + 1, bits):
                    start(self.rep_copy(step, (1 << got) + n))

    class Vectors:
        def __init__(self, kind, ins, out, scratch):
            self.kind, self.out = kind, out
            self.held, self.came, self.load_sem, self.send_sem, self.recv_sem, own_sem = scratch
            self.first = pltpu.make_async_copy(ins[0], self.held.at[0], self.load_sem.at[0])
            self.final = pltpu.make_async_copy(self.held.at[len(crowd)], out, own_sem.at[0])
            self.done = 0

        def begin(self):
            self.first.start()

        def exchange(self, n):
            return remote(
                self.held.at[n], self.came.at[n], self.send_sem, self.recv_sem, n, crowd[n]
            )

        def go_on(self):
            n = self.done
            if n > len(crowd):
                return
            if n == 0:
                self.first.wait()
            else:
                self.exchange(n - 1).wait_recv()
                self.held[n] = self.held[n - 1] + self.came[n - 1]
            if n < len(crowd):
                start(self.exchange(n))
            else:
                self.final.start()
            self.done += 1

        def own_out(self):
            return self.final

    jobs = [
        (Vectors if parts[0] == "vectors" else Job)(*parts)
        for parts in zip(kinds, ins, outs, scratch)
    ]
    for job in jobs:
        job.begin()
    plain_jobs = [job for job in jobs if job.kind in ("pairs", "plane")]
    full_jobs = [job for job in jobs if job.kind == "full"]
    vector_jobs = [job for job in jobs if job.kind == "vectors"]
    spread_jobs = [job for job in jobs if job.kind == "spread"]
    for job in plain_jobs:
        job.forward(0)
    for job in spread_jobs:
        job.load(0).wait()
        job.finish()
    for i in range(levels):
        for job in vector_jobs:
            job.go_on()
        if i + 1 < levels:
            for job in plain_jobs:
                job.forward(i + 1)
        for job in full_jobs:
            job.halve(i, 0)
        if i > 0 and i <= bits:
            for job in spread_jobs:
                job.spread(i - 1)
        for step in range(1, bits):
            for job in full_jobs:
                job.halve(i, step)
        for job in full_jobs:
            job.forward(i)
    for got in range(bits):
        late = [job for job in spread_jobs if got >= levels - 1]
        for job in plain_jobs + full_jobs + late:
            job.spread(got)
        for job in vector_jobs:
            job.go_on()
    for job in vector_jobs:
        while job.done <= len(crowd):
            job.go_on()
    for copy in sent:
        copy.wait_send()
    for job in jobs:
        job.own_out().wait()


def sum_arrays(jobs, collective_id):
    replicas, shards = lax.axis_size("rep"), lax.axis_size("shard")
    levels = shards // 2
    dma = pltpu.SemaphoreType.DMA
    any_space = pl.BlockSpec(memory_space=pl.ANY)
    scratch, counts, out_shape, size, total = [], [], [], 0, 0
    exchanges = (shards * replicas).bit_length() - 1
    for kind, arrays in jobs:
        block = arrays[0].shape[-2:]
        dtype = arrays[0].dtype
        total += sum(array.size for array in arrays)
        if kind == "vectors":
            own = [
                pltpu.VMEM((exchanges + 1,) + block, dtype),
                pltpu.VMEM((exchanges,) + block, dtype),
                dma((1,)),
                dma((exchanges,)),
                dma((exchanges,)),
                dma((1,)),
            ]
            scratch += own
            counts.append(len(own))
            size += 4 * block[0] * block[1] * (2 * exchanges + 1)
            out_shape.append(jax.ShapeDtypeStruct(block, dtype))
            continue
        slots = replicas // 2 if kind == "full" else 1
        chunks = 1 if kind == "spread" else levels
        came = {"pairs": 1, "full": replicas - 1}.get(kind, 0)
        own = [
            pltpu.VMEM((chunks, slots) + block, dtype),
            pltpu.VMEM((levels, came) + block if came else (16, 128), dtype),
            pltpu.VMEM((levels - 1,) + block if kind != "spread" else (16, 128), dtype),
            dma((levels * slots,)),
            dma((levels * max(came, 1),)),
            dma((levels * max(came, 1),)),
            dma((levels,)),
            dma((levels,)),
            dma((replicas,)),
            dma((replicas,)),
            dma((1,)),
        ]
        scratch += own
        counts.append(len(own))
        size += 2 * block[0] * block[1] * (chunks * (slots + came) + chunks - 1)
        out_shape.append(jax.ShapeDtypeStruct(block if kind == "pairs" else (replicas,) + block, dtype))
    kinds = tuple(kind for kind, _ in jobs)
    operands = [array for _, arrays in jobs for array in arrays]
    return pl.pallas_call(
        functools.partial(sum_kernel, levels, replicas, kinds, tuple(counts)),
        out_shape=out_shape,
        in_specs=[any_space] * len(operands),
        out_specs=[any_space] * len(jobs),
        scratch_shapes=scratch,
        compiler_params=pltpu.CompilerParams(
            collective_id=collective_id, has_side_effects=True, vmem_limit_bytes=size + (4 << 20)
        ),
        cost_estimate=pl.CostEstimate(flops=total, transcendentals=0, bytes_accessed=20 * total),
    )(*operands)


def sum_along(block, axis):
    size = lax.axis_size(axis)
    step = 1
    while step < size:
        block = block + lax.ppermute(block, axis, [(n, n ^ step) for n in range(size)])
        step *= 2
    return block


def per_device(
    x_prompt,
    x_cont,
    teacher_prompt,
    teacher_cont,
    valid_mask,
    group_of,
    ln1_gain,
    ln1_bias,
    w_qkv,
    q_bias,
    v_bias,
    w_out,
    out_bias,
    ln2_gain,
    ln2_bias,
    w_up,
    up_bias,
    w_down,
    down_bias,
):
    shards = lax.axis_size("shard")
    replicas = lax.axis_size("rep")
    shard_index = lax.axis_index("shard")
    prompt_count, prompt_rows, width = x_prompt.shape
    cont_rows = x_cont.shape[0]
    cont_count, cont_len = valid_mask.shape
    prompt_len = prompt_rows * shards
    prompt_total = prompt_count * prompt_rows
    head_count = width // HEAD_DIM
    all_tokens = replicas * shards * (prompt_total + cont_rows)
    valid_local = jnp.sum(valid_mask.astype(jnp.float32)) + prompt_total
    vectors = (
        ln1_gain,
        ln1_bias,
        q_bias,
        v_bias,
        out_bias,
        ln2_gain,
        ln2_bias,
        up_bias,
        down_bias,
    )
    starts = [0]
    for vector in vectors:
        starts.append(starts[-1] + vector.shape[0])
    filled = -(starts[-1] + 1) % 1024
    joint = jnp.concatenate(
        [vector.astype(jnp.float32) for vector in vectors]
        + [valid_local[None], jnp.zeros((filled,), jnp.float32)]
    ).reshape(8, -1)
    levels = shards // 2
    steps = range(1, levels)
    ahead = (levels - 1) * 2 // 3
    first_units = [(m, j, True, True) for j in steps for m in (2, 0, 1)]
    first_units += [(3, j, True, False) for j in steps if j <= ahead]
    q_full, kv_full, joint, up_begun = gather_rows(
        [w_qkv[:, :width], w_qkv[:, width:], joint, w_up],
        (True, True, False, True),
        (True, True, True, False),
        first_units,
        0,
    )
    q_full, kv_full = plain(q_full), plain(kv_full)
    joint = joint.reshape(shards, -1)
    (
        gain_one,
        shift_one,
        bias_query,
        bias_value,
        bias_out,
        gain_two,
        shift_two,
        bias_up,
        bias_down,
    ) = [joint[:, begin:end].reshape(-1) for begin, end in zip(starts[:-1], starts[1:])]
    valid_group = jnp.broadcast_to(jnp.sum(joint[:, starts[-1]]), (8, 128))
    valid_all = sum_along(valid_group, "rep")[0, 0]
    loss_scale = all_tokens / valid_all
    inputs = jnp.concatenate([x_prompt.reshape(prompt_total, width), x_cont], axis=0).astype(
        jnp.float32
    )
    normed, unit_one, inverse_one = norm_forward(inputs, gain_one, shift_one)
    normed_low = normed.astype(jnp.bfloat16)
    queries = jnp.dot(normed_low, q_full, preferred_element_type=jnp.float32)
    queries = (queries + bias_query).astype(jnp.bfloat16)
    pair_bias = jnp.concatenate([jnp.zeros_like(bias_value), bias_value])
    pair_rows = jnp.dot(normed_low, kv_full, preferred_element_type=jnp.float32)
    pair_rows = (pair_rows + pair_bias).astype(jnp.bfloat16)
    local_pairs = pair_rows[:prompt_total].reshape(prompt_count, prompt_rows, 2 * width)
    own_pairs = pair_rows[prompt_total:]
    second_units = [(2, j, False, True) for j in steps if j <= ahead]
    for j in steps:
        second_units += [(1, j, True, True), (3, j, True, True)]
        if j > ahead:
            second_units.append((2, j, True, True))
        second_units.append((0, j, True, True))
    prompt_pairs, out_full, up_full, down_full = gather_rows(
        [local_pairs, w_out, w_up, w_down],
        (False, True, True, True),
        (True, True, True, True),
        second_units,
        1,
        {2: up_begun},
    )
    out_full, up_full, down_full = plain(out_full), plain(up_full), plain(down_full)
    sizes = (prompt_count, prompt_rows, cont_count, cont_len)
    places = jnp.concatenate([(shard_index * prompt_rows)[None], group_of]).astype(jnp.int32)
    joined_rows = (queries, own_pairs)
    attended, log_totals = attention_call(sizes, joined_rows, prompt_pairs, places)
    middle = inputs + jnp.dot(attended, out_full, preferred_element_type=jnp.float32) + bias_out
    normed_two, unit_two, inverse_two = norm_forward(middle, gain_two, shift_two)
    normed_two_low = normed_two.astype(jnp.bfloat16)
    upward = jnp.dot(normed_two_low, up_full, preferred_element_type=jnp.float32) + bias_up
    squared = upward * upward
    bend = jnp.tanh(gelu_coef * upward * (1.0 + 0.044715 * squared))
    half = 0.5 * (1.0 + bend)
    active_low = (upward * half).astype(jnp.bfloat16)
    rise = gelu_coef * (1.0 + 3.0 * 0.044715 * squared)
    gelu_slope = (half + 0.5 * upward * (1.0 - bend * bend) * rise).astype(jnp.bfloat16)
    result = middle + jnp.dot(active_low, down_full, preferred_element_type=jnp.float32) + bias_down
    out_prompt = (
        result[:prompt_total].reshape(prompt_count, prompt_rows, width).astype(jnp.bfloat16)
    )
    out_cont = result[prompt_total:].astype(jnp.bfloat16)
    targets = jnp.concatenate(
        [teacher_prompt.reshape(prompt_total, width), teacher_cont], axis=0
    ).astype(jnp.float32)
    weight_rows = jnp.concatenate(
        [jnp.ones((prompt_total,), jnp.float32), valid_mask.reshape(cont_rows).astype(jnp.float32)]
    )
    out_grad = (loss_scale * weight_rows)[:, None] * (result - targets)
    mlp_grad = out_grad.astype(jnp.bfloat16)
    grad_bias_down = jnp.sum(mlp_grad, axis=0, dtype=jnp.float32)
    down_total = chip_gradient(active_low, [mlp_grad[None]], halves=False)
    down_plane = sum_plane(down_total)
    active_grad = back_product(kept_behind(mlp_grad, down_total), down_full)
    upward_grad = (active_grad * gelu_slope.astype(jnp.float32)).astype(jnp.bfloat16)
    grad_bias_up = jnp.sum(upward_grad, axis=0, dtype=jnp.float32)
    up_total = chip_gradient(normed_two_low, [upward_grad[None]], halves=False)
    up_plane = sum_plane(up_total)
    normed_two_grad = back_product(upward_grad, up_full)
    middle_step, grad_gain_two, grad_shift_two = norm_backward(
        normed_two_grad, unit_two, inverse_two, gain_two
    )
    middle_grad = out_grad + middle_step
    branch_grad = middle_grad.astype(jnp.bfloat16)
    grad_bias_out = jnp.sum(branch_grad, axis=0, dtype=jnp.float32)
    attended_grad = back_product(branch_grad, out_full).astype(jnp.bfloat16)
    later_places = places
    query_part, pair_grad, own_grad = attention_call(
        sizes, joined_rows, prompt_pairs, later_places, (log_totals, attended_grad)
    )
    down_owned = sum_levels(tied(down_plane, query_part))
    out_total = chip_gradient(attended, [branch_grad[None]])
    q_total = chip_gradient(normed_low, [query_part[None]], after=[up_total])
    near_grad = back_product(query_part, q_full)
    cont_grad = near_grad[prompt_total:]
    for n in range(2):
        cont_grad = cont_grad + back_product(own_grad[n], kv_full[:, n * width : (n + 1) * width])
    cont_step, cont_gain, cont_shift = norm_backward(
        cont_grad, unit_one[prompt_total:], inverse_one[prompt_total:], gain_one
    )
    grad_cont = middle_grad[prompt_total:] + cont_step
    pair_sums = tied(pair_grad.reshape(shards, -1, width), grad_cont)
    owned_pairs, out_parts, q_parts = sum_arrays(
        [
            ("pairs", [pair_sums]),
            ("full", out_total),
            ("full", q_total),
        ],
        2,
    )
    owned_grad = owned_pairs.reshape(2, prompt_total, width)
    pair_total = chip_gradient(normed_low, [owned_grad, own_grad])
    grad_bias_query = jnp.sum(query_part, axis=0, dtype=jnp.float32)
    grad_bias_value = jnp.sum(owned_grad[1], axis=0, dtype=jnp.float32)
    grad_bias_value = grad_bias_value + jnp.sum(own_grad[1], axis=0, dtype=jnp.float32)
    prompt_grad = near_grad[:prompt_total]
    for n in range(2):
        prompt_grad = prompt_grad + back_product(
            owned_grad[n], kv_full[:, n * width : (n + 1) * width]
        )
    prompt_step, prompt_gain, prompt_shift = norm_backward(
        prompt_grad, unit_one[:prompt_total], inverse_one[:prompt_total], gain_one
    )
    grad_gain_one, grad_shift_one = prompt_gain + cont_gain, prompt_shift + cont_shift
    grad_prompt = middle_grad[:prompt_total] + prompt_step
    grad_prompt = grad_prompt.reshape(prompt_count, prompt_rows, width)
    vector_grads = (
        grad_gain_one,
        grad_shift_one,
        grad_bias_query,
        grad_bias_value,
        grad_bias_out,
        grad_gain_two,
        grad_shift_two,
        grad_bias_up,
        grad_bias_down,
    )
    joint_grads = jnp.concatenate([vector.reshape(shards, -1) for vector in vector_grads], axis=1)
    pair_parts, down_parts, up_parts, joint_sums = sum_arrays(
        [
            ("full", pair_total),
            ("spread", [down_owned[None]]),
            ("plane", [up_plane]),
            ("vectors", [joint_grads]),
        ],
        3,
    )
    summed_down, summed_up, summed_out = [
        plain(parts).astype(jnp.float32) for parts in (down_parts, up_parts, out_parts)
    ]
    summed_qkv = jnp.concatenate([plain(q_parts), plain(pair_parts)], axis=1).astype(jnp.float32)
    own_sums = lax.dynamic_index_in_dim(joint_sums, shard_index, 0, keepdims=False)
    owned_vectors = [own_sums[begin:end] for begin, end in zip(starts[:-1], starts[1:])]
    return (
        out_prompt,
        out_cont,
        grad_prompt,
        grad_cont,
        owned_vectors[0],
        owned_vectors[1],
        summed_qkv,
        owned_vectors[2],
        owned_vectors[3],
        summed_out,
        owned_vectors[4],
        owned_vectors[5],
        owned_vectors[6],
        summed_up,
        owned_vectors[7],
        summed_down,
        owned_vectors[8],
    )


def solution(mesh):
    in_specs = (
        P("rep", "shard", None),
        P(("rep", "shard"), None),
        P("rep", "shard", None),
        P(("rep", "shard"), None),
        P(("rep", "shard"), None),
        P(("rep", "shard")),
        P("shard"),
        P("shard"),
        P("shard", None),
        P("shard"),
        P("shard"),
        P("shard", None),
        P("shard"),
        P("shard"),
        P("shard"),
        P("shard", None),
        P("shard"),
        P("shard", None),
        P("shard"),
    )
    out_specs = (
        P("rep", "shard", None),
        P(("rep", "shard"), None),
        P("rep", "shard", None),
        P(("rep", "shard"), None),
        P("shard"),
        P("shard"),
        P("shard", None),
        P("shard"),
        P("shard"),
        P("shard", None),
        P("shard"),
        P("shard"),
        P("shard"),
        P("shard", None),
        P("shard"),
        P("shard", None),
        P("shard"),
    )
    return jax.shard_map(
        per_device, mesh=mesh, in_specs=in_specs, out_specs=out_specs, check_vma=False
    )
```

```python
import functools

import jax
import jax.numpy as jnp
from jax import lax
from jax.experimental import pallas as pl
from jax.experimental.pallas import tpu as pltpu
from jax.sharding import PartitionSpec as P

HEAD_DIM = 128
AXES = ("rep", "shard")


epsilon = 1e-05
gelu_coef = 0.7978845608028654


def norm_forward(inputs, norm_gain, norm_shift):
    centered = inputs - jnp.mean(inputs, axis=-1, keepdims=True)
    variance = jnp.mean(centered * centered, axis=-1, keepdims=True)
    inverse = lax.rsqrt(variance + epsilon)
    unit_rows = centered * inverse
    return (unit_rows * norm_gain + norm_shift, unit_rows, inverse)


def norm_backward(upstream, unit_rows, inverse, norm_gain):
    scaled = upstream * norm_gain
    centered = (
        scaled
        - jnp.mean(scaled, axis=-1, keepdims=True)
        - unit_rows * jnp.mean(scaled * unit_rows, axis=-1, keepdims=True)
    )
    return (centered * inverse, jnp.sum(upstream * unit_rows, axis=0), jnp.sum(upstream, axis=0))


def cross(left, right):
    return lax.dot_general(
        left, right, (((0,), (0,)), ((), ())), preferred_element_type=jnp.float32
    )


def back_product(left, right):
    return lax.dot_general(
        left, right, (((1,), (1,)), ((), ())), preferred_element_type=jnp.float32
    )


def dot_last(left, right):
    return back_product(left, right)


def causal_scores(queries, keys, factor, slope, key_start, query_start, masked):
    scores = dot_last(queries, keys) * factor
    key_pos = key_start + lax.broadcasted_iota(jnp.int32, (1, keys.shape[0]), 1)
    scores = scores + slope * (key_pos - query_start).astype(jnp.float32)
    if masked:
        query_pos = query_start + lax.broadcasted_iota(jnp.int32, (queries.shape[0], 1), 0)
        scores = jnp.where(key_pos <= query_pos, scores, -1e30)
    return scores


def all_rows(ref, prompt):
    return ref[:, prompt].reshape(-1, ref.shape[-1])


def forward_kernel(sizes, places, slopes, q_ref, k_ref, v_ref, own_k_ref, own_v_ref, out_ref, lse_ref):
    prompt_count, prompt_rows, cont_count, cont_len = sizes
    prompt_total = prompt_count * prompt_rows
    prompt_len = k_ref.shape[0] * prompt_rows
    slope = slopes[pl.program_id(0)]
    factor = q_ref.shape[1] ** (-0.5)
    for p in range(prompt_count):
        rows = slice(p * prompt_rows, (p + 1) * prompt_rows)
        scores = causal_scores(q_ref[rows], all_rows(k_ref, p), factor, slope, 0, places[0], True)
        largest = jnp.max(scores, axis=-1, keepdims=True)
        terms = jnp.exp(scores - largest)
        total = jnp.sum(terms, axis=-1, keepdims=True)
        probs = (terms / total).astype(jnp.bfloat16)
        mixed = jnp.dot(probs, all_rows(v_ref, p), preferred_element_type=jnp.float32)
        out_ref[rows] = mixed.astype(out_ref.dtype)
        lse_ref[0, rows] = largest + jnp.log(total)
    for c in range(cont_count):
        own = slice(c * cont_len, (c + 1) * cont_len)
        rows = slice(prompt_total + c * cont_len, prompt_total + (c + 1) * cont_len)
        group = places[1 + c]
        far = causal_scores(q_ref[rows], all_rows(k_ref, group), factor, slope, 0, prompt_len, False)
        near = causal_scores(q_ref[rows], own_k_ref[own], factor, slope, prompt_len, prompt_len, True)
        largest = jnp.maximum(
            jnp.max(far, axis=-1, keepdims=True), jnp.max(near, axis=-1, keepdims=True)
        )
        far, near = jnp.exp(far - largest), jnp.exp(near - largest)
        total = jnp.sum(far, axis=-1, keepdims=True) + jnp.sum(near, axis=-1, keepdims=True)
        mixed = jnp.dot(
            (far / total).astype(jnp.bfloat16), all_rows(v_ref, group), preferred_element_type=jnp.float32
        ) + jnp.dot(
            (near / total).astype(jnp.bfloat16), own_v_ref[own], preferred_element_type=jnp.float32
        )
        out_ref[rows] = mixed.astype(out_ref.dtype)
        lse_ref[0, rows] = largest + jnp.log(total)


def backward_kernel(
    sizes, places, slopes, q_ref, k_ref, v_ref, own_k_ref, own_v_ref, lse_ref, grad_ref,
    q_grad_ref, pair_grad_ref, own_grad_ref, k_sum, v_sum,
):
    prompt_count, prompt_rows, cont_count, cont_len = sizes
    prompt_total = prompt_count * prompt_rows
    prompt_len = k_ref.shape[0] * prompt_rows
    slope = slopes[pl.program_id(0)]
    factor = q_ref.shape[1] ** (-0.5)
    for p in range(prompt_count):
        rows = slice(p * prompt_rows, (p + 1) * prompt_rows)
        queries, grads = q_ref[rows], grad_ref[rows]
        scores = causal_scores(queries, all_rows(k_ref, p), factor, slope, 0, places[0], True)
        probs = jnp.exp(scores - lse_ref[0, rows])
        prob_grad = dot_last(grads, all_rows(v_ref, p))
        inner = jnp.sum(probs * prob_grad, axis=-1, keepdims=True)
        score_grad = (probs * (prob_grad - inner)).astype(jnp.bfloat16)
        q_grad = jnp.dot(score_grad, all_rows(k_ref, p), preferred_element_type=jnp.float32) * factor
        q_grad_ref[rows] = q_grad.astype(q_grad_ref.dtype)
        k_sum[p] = cross(score_grad, queries) * factor
        v_sum[p] = cross(probs.astype(jnp.bfloat16), grads)
    for c in range(cont_count):
        own = slice(c * cont_len, (c + 1) * cont_len)
        rows = slice(prompt_total + c * cont_len, prompt_total + (c + 1) * cont_len)
        group = places[1 + c]
        queries, grads = q_ref[rows], grad_ref[rows]
        far_keys, near_keys = all_rows(k_ref, group), own_k_ref[own]
        far = causal_scores(queries, far_keys, factor, slope, 0, prompt_len, False)
        near = causal_scores(queries, near_keys, factor, slope, prompt_len, prompt_len, True)
        far, near = jnp.exp(far - lse_ref[0, rows]), jnp.exp(near - lse_ref[0, rows])
        far_grad, near_grad = dot_last(grads, all_rows(v_ref, group)), dot_last(grads, own_v_ref[own])
        inner = jnp.sum(far * far_grad, axis=-1, keepdims=True)
        inner = inner + jnp.sum(near * near_grad, axis=-1, keepdims=True)
        far_grad = (far * (far_grad - inner)).astype(jnp.bfloat16)
        near_grad = (near * (near_grad - inner)).astype(jnp.bfloat16)
        q_grad = jnp.dot(far_grad, far_keys, preferred_element_type=jnp.float32)
        q_grad = q_grad + jnp.dot(near_grad, near_keys, preferred_element_type=jnp.float32)
        q_grad_ref[rows] = (q_grad * factor).astype(q_grad_ref.dtype)
        k_sum[group] = k_sum[group] + cross(far_grad, queries) * factor
        v_sum[group] = v_sum[group] + cross(far.astype(jnp.bfloat16), grads)
        own_grad_ref[0, own] = (cross(near_grad, queries) * factor).astype(own_grad_ref.dtype)
        own_grad_ref[1, own] = cross(near.astype(jnp.bfloat16), grads).astype(own_grad_ref.dtype)
    for p in range(prompt_count):
        for piece in range(prompt_len // prompt_rows):
            rows = slice(piece * prompt_rows, (piece + 1) * prompt_rows)
            pair_grad_ref[piece, 0, p] = k_sum[p, rows].astype(pair_grad_ref.dtype)
            pair_grad_ref[piece, 1, p] = v_sum[p, rows].astype(pair_grad_ref.dtype)


def attention_call(sizes, joined_rows, pairs, places, more=None):
    prompt_count, prompt_rows, cont_count, cont_len = sizes
    tokens, width = joined_rows[0].shape
    prompt_len = pairs.shape[0] * prompt_rows
    heads = width // HEAD_DIM
    cont_rows = cont_count * cont_len
    slopes = 2.0 ** (-8.0 * (jnp.arange(heads, dtype=jnp.float32) + 1.0) / heads)
    by_head = pl.BlockSpec((tokens, HEAD_DIM), lambda h, *_: (0, h))
    own_head = pl.BlockSpec((cont_rows, HEAD_DIM), lambda h, *_: (0, h))
    pair_block = pairs.shape[:3] + (HEAD_DIM,)
    keys = pl.BlockSpec(pair_block, lambda h, *_: (0, 0, 0, h))
    values = pl.BlockSpec(pair_block, lambda h, *_: (0, 0, 0, heads + h))
    stats = pl.BlockSpec((1, tokens, 1), lambda h, *_: (h, 0, 0))
    stats_shape = jax.ShapeDtypeStruct((heads, tokens, 1), jnp.float32)
    rows_shape = jax.ShapeDtypeStruct((tokens, width), jnp.bfloat16)
    own_shape = jax.ShapeDtypeStruct((2, cont_rows, width), jnp.bfloat16)
    queries, own_pairs = joined_rows
    own_values = pl.BlockSpec((cont_rows, HEAD_DIM), lambda h, *_: (0, heads + h))
    inputs = (queries, pairs, pairs, own_pairs, own_pairs)
    in_specs = [by_head, keys, values, own_head, own_values]
    pieces = prompt_len // prompt_rows
    scores = tokens * (prompt_len + cont_len) * heads
    if more is None:
        kernel, scratch, products = forward_kernel, [], 2
        out_shape, out_specs = (rows_shape, stats_shape), (by_head, stats)
    else:
        kernel, products = backward_kernel, 5
        scratch = [pltpu.VMEM((prompt_count, prompt_len, HEAD_DIM), jnp.float32)] * 2
        inputs += more
        in_specs += [stats, by_head]
        piece_shape = jax.ShapeDtypeStruct(
            (pieces, 2, prompt_count, prompt_rows, width), jnp.bfloat16
        )
        piece = pl.BlockSpec(
            (pieces, 2, prompt_count, prompt_rows, HEAD_DIM), lambda h, *_: (0, 0, 0, 0, h)
        )
        own_grad = pl.BlockSpec((2, cont_rows, HEAD_DIM), lambda h, *_: (0, 0, h))
        out_shape = (rows_shape, piece_shape, own_shape)
        out_specs = (by_head, piece, own_grad)
    return pl.pallas_call(
        functools.partial(kernel, sizes),
        out_shape=out_shape,
        grid_spec=pltpu.PrefetchScalarGridSpec(
            num_scalar_prefetch=2,
            grid=(heads,),
            in_specs=in_specs,
            out_specs=out_specs,
            scratch_shapes=scratch,
        ),
        compiler_params=pltpu.CompilerParams(vmem_limit_bytes=40 << 20),
        cost_estimate=pl.CostEstimate(
            flops=2 * products * scores * HEAD_DIM,
            transcendentals=scores,
            bytes_accessed=8 * prompt_count * prompt_len * width,
        ),
    )(places, slopes, *inputs)


def send(block, target):
    replicas, shards = lax.axis_size("rep"), lax.axis_size("shard")
    pairs = []
    for r in range(replicas):
        for s in range(shards):
            r_to, z_to, c_to = target(r, s // 2, s % 2)
            pairs.append((r * shards + s, r_to * shards + 2 * z_to + c_to))
    return lax.ppermute(block, AXES, pairs)


def swap_core(block):
    return send(block, lambda r, z, c: (r, z, 1 - c))


def bit_of(step, core):
    bits = lax.axis_size("rep").bit_length() - 1
    return step if core == 0 else bits - 1 - step


def mask_lists():
    bits = lax.axis_size("rep").bit_length() - 1
    lists = []
    for core in range(2):
        masks = [0]
        for step in range(bits):
            masks += [m ^ (1 << bit_of(step, core)) for m in masks]
        lists.append(masks)
    return lists


MESH_ID = pl.DeviceIdType.MESH


def gather_kernel(levels, replicas, spread, placed, begun, units, *refs):
    count = len(spread)
    owns, fulls = refs[:count], refs[count + begun : 2 * count + begun]
    staged = refs[2 * count + begun : 3 * count + begun]
    own_sem, ring_send, ring_recv, rep_send, rep_recv, core_send, core_recv = refs[3 * count + begun :]
    bits = replicas.bit_length() - 1
    r, s = lax.axis_index("rep"), lax.axis_index("shard")
    core, z = lax.rem(s, 2), lax.div(s, 2)
    other = {"shard": s + 1 - 2 * core}
    ring_to = {"shard": lax.rem(s + 2, 2 * levels)}
    ring_from = {"shard": lax.rem(s + 2 * levels - 2, 2 * levels)}
    rep_to = [{"rep": r ^ jnp.where(core == 0, 1 << bit_of(n, 0), 1 << bit_of(n, 1))} for n in range(bits)]
    barrier = pltpu.get_barrier_semaphore()
    partners = [ring_to, ring_from, other] + rep_to
    for partner in partners:
        pl.semaphore_signal(barrier, inc=1, device_id=partner, device_id_type=MESH_ID)
    pl.semaphore_wait(barrier, len(partners))
    lists = mask_lists()
    place = [jnp.where(core == 0, a, b) ^ r for a, b in zip(*lists)]

    def piece_of(m, j, n):
        block = fulls[m].at[2 * lax.rem(z - j + levels, levels) + core]
        return block.at[place[n]] if spread[m] else block

    def remote(source, target, sends, recvs, n, device):
        return pltpu.make_async_remote_copy(
            src_ref=source,
            dst_ref=target,
            send_sem=sends.at[n],
            recv_sem=recvs.at[n],
            device_id=device,
            device_id_type=MESH_ID,
        )

    def ring_copy(t):
        m, j = units[t][:2]
        target = piece_of(m, j - 1, 0)
        own = owns[m].at[r] if spread[m] else owns[m]
        return remote(own if j == 1 else target, target, ring_send, ring_recv, t, ring_to)

    def rep_copy(t, step, n):
        piece = piece_of(*units[t][:2], n)
        return remote(piece, piece, rep_send, rep_recv, t * replicas + (1 << step) + n, rep_to[step])

    def core_copy(t, n):
        piece = piece_of(*units[t][:2], n)
        return remote(piece, piece, core_send, core_recv, t * replicas + n, other)

    last = len(units)
    goes = [t for t in range(last) if units[t][2]]
    ready = {}
    for n, t in enumerate(goes):
        m, j = units[t][:2]
        needs = [goes[n - 3]] if n >= 3 else []
        needs += [e for e in goes[:n] if units[e][:2] == (m, j - 1)]
        ready.setdefault(max(needs, default=-1), []).append(t)
    started = []

    def start(copy):
        copy.start()
        started.append(copy)

    rings = {t: ring_copy(t) for t in goes}
    reps = {}
    for t in ready.get(-1, []):
        start(rings[t])
    own_ins, own_outs, own_cores = {}, {}, {}
    for m in range(count):
        if placed[m]:
            own_ins[m] = pltpu.make_async_copy(owns[m], staged[m], own_sem.at[2 * m])
            own_outs[m] = pltpu.make_async_copy(staged[m], fulls[m].at[s], own_sem.at[2 * m + 1])
            own_cores[m] = remote(
                staged[m], fulls[m].at[s], core_send, core_recv, last * replicas + m, other
            )
            own_ins[m].start()
    for m in own_ins:
        own_ins[m].wait()
        own_outs[m].start()
        start(own_cores[m])
    for tick in range(last + bits):
        t = tick
        if t < last:
            if units[t][2]:
                rings[t].wait_recv()
                for later in ready.get(t, []):
                    start(rings[later])
            if units[t][3]:
                if spread[units[t][0]]:
                    for step in range(bits):
                        reps[t, step, 0] = rep_copy(t, step, 0)
                        start(reps[t, step, 0])
                start(core_copy(t, 0))
        for lag in range(1, bits + 1):
            t = tick - lag
            if not 0 <= t < last or not units[t][3] or not spread[units[t][0]]:
                continue
            got = lag - 1
            for n in range(1 << got):
                reps[t, got, n].wait_recv()
                arrived = (1 << got) + n
                for step in range(got + 1, bits):
                    reps[t, step, arrived] = rep_copy(t, step, arrived)
                    start(reps[t, step, arrived])
                start(core_copy(t, arrived))
    for copy in started:
        copy.wait_send()
    for t in range(last):
        if units[t][3]:
            for n in range(replicas if spread[units[t][0]] else 1):
                core_copy(t, n).wait_recv()
    for m in own_outs:
        own_outs[m].wait()
        own_cores[m].wait_recv()


def gather_rows(arrays, spread, placed, units, collective_id, begun=None):
    begun = begun or {}
    replicas, shards = lax.axis_size("rep"), lax.axis_size("shard")
    levels = shards // 2
    count = len(arrays)
    owns = [
        w.reshape((replicas, w.shape[0] // replicas) + w.shape[1:]) if wide else w
        for w, wide in zip(arrays, spread)
    ]
    slots = len(units) * replicas
    any_space = pl.BlockSpec(memory_space=pl.ANY)
    dma = pltpu.SemaphoreType.DMA
    size = sum(w.size * w.dtype.itemsize for w in arrays)
    staging = [
        pltpu.VMEM(w.shape if put else (8, 128), w.dtype if put else jnp.float32)
        for w, put in zip(owns, placed)
    ]
    return pl.pallas_call(
        functools.partial(gather_kernel, levels, replicas, spread, placed, len(begun), tuple(units)),
        out_shape=[jax.ShapeDtypeStruct((shards,) + w.shape, w.dtype) for w in owns],
        in_specs=[any_space] * (count + len(begun)),
        out_specs=[any_space] * count,
        scratch_shapes=staging
        + [
            dma((2 * count,)),
            dma((len(units),)),
            dma((len(units),)),
            dma((slots,)),
            dma((slots,)),
            dma((slots + count,)),
            dma((slots + count,)),
        ],
        input_output_aliases={count + n: m for n, m in enumerate(begun)},
        compiler_params=pltpu.CompilerParams(
            collective_id=collective_id, has_side_effects=True, vmem_limit_bytes=size + (1 << 20)
        ),
        cost_estimate=pl.CostEstimate(flops=0, transcendentals=0, bytes_accessed=30 * size),
    )(*owns, *begun.values())


def kept_behind(block, array):
    first = lax.slice(array, (0,) * array.ndim, (1,) * array.ndim).reshape(())
    return jnp.where(first == first, block, jnp.zeros_like(block))


def plain(full):
    return full.reshape(-1, full.shape[-1])


def behind(numbers, top, *arrays):
    for array in arrays:
        first = lax.slice(array, (0,) * array.ndim, (1,) * array.ndim).reshape(())
        numbers = numbers + (first != first).astype(jnp.int32)
    return jnp.clip(numbers, 0, top)


def token_products(left, left_far, rights):
    sums, half = None, len(rights) // 2
    for source, blocks in ((left, rights[:half]), (left_far, rights[half:])):
        begin = 0
        for block in blocks:
            rows = block.shape[1]
            term = cross(source[begin : begin + rows], block[0])
            sums = term if sums is None else sums + term
            begin += rows
    return sums


def gradient_kernel(count, places, left, left_far, *refs):
    rights, (keep, leave, total) = refs[:count], refs[count:]
    sums = token_products(left, left_far, rights)
    parts, part = total.shape[0], total.shape[1]
    for q in range(parts):
        total[q] = sums[q * part : (q + 1) * part].astype(total.dtype)
    half = parts // 2
    for slot in range(half):
        keep[slot, 0] = total[places[1 + slot]]
        leave[slot, 0] = total[places[1 + half + slot]]


def whole_kernel(count, places, left, left_far, *refs):
    rights, out = refs[:count], refs[count]
    sums = token_products(left, left_far, rights)
    part = out.shape[2]
    for q in range(out.shape[0]):
        out[q, 0] = sums[q * part : (q + 1) * part].astype(out.dtype)


def slot_parts():
    bits = lax.axis_size("rep").bit_length() - 1
    r = lax.axis_index("rep")
    core = lax.rem(lax.axis_index("shard"), 2)
    lists = []
    for c in range(2):
        masks = [0]
        for step in reversed(range(bits)):
            masks = masks + [m ^ (1 << bit_of(step, c)) for m in masks]
        lists.append(masks)
    return [jnp.where(core == 0, a, b) ^ r for a, b in zip(*lists)]


def chip_gradient(left, rights, halves=True, after=()):
    replicas, shards = lax.axis_size("rep"), lax.axis_size("shard")
    levels = shards // 2
    core = lax.rem(lax.axis_index("shard"), 2)
    tokens, height = left.shape
    blocks, _, width = rights[0].shape
    columns = blocks * width
    rows = height // shards
    part = rows // replicas
    even, odd = [
        jnp.concatenate(
            [left[:, (2 * z + c) * rows : (2 * z + c + 1) * rows] for z in range(levels)], axis=1
        )
        for c in range(2)
    ]
    left_far = swap_core(jnp.where(core == 0, odd, even))
    rights = list(rights) + [swap_core(right) for right in rights]
    wide = min(width, max((1 << 18) // rows, 512))
    each = width // wide
    places = jnp.stack([core] + slot_parts()).astype(jnp.int32)
    slots = replicas // 2 if halves else replicas
    out_shape = jax.ShapeDtypeStruct((slots, levels, part, columns), jnp.bfloat16)
    out_spec = pl.BlockSpec((slots, 1, part, wide), lambda n, z, places: (0, z, 0, n))
    kernel = gradient_kernel if halves else whole_kernel
    return pl.pallas_call(
        functools.partial(kernel, len(rights)),
        out_shape=[out_shape] * 2 if halves else out_shape,
        grid_spec=pltpu.PrefetchScalarGridSpec(
            num_scalar_prefetch=1,
            grid=(columns // wide, levels),
            in_specs=[
                pl.BlockSpec((tokens, rows), lambda n, z, places: (0, 2 * z + places[0])),
                pl.BlockSpec((tokens, rows), lambda n, z, places: (0, z)),
            ]
            + [
                pl.BlockSpec((1, right.shape[1], wide), lambda n, z, places: (n // each, 0, n % each))
                for right in rights
            ],
            out_specs=[out_spec] * 2 if halves else out_spec,
            scratch_shapes=[pltpu.VMEM((replicas, part, wide), jnp.bfloat16)] if halves else [],
        ),
        compiler_params=pltpu.CompilerParams(vmem_limit_bytes=40 << 20),
        cost_estimate=pl.CostEstimate(
            flops=2 * tokens * height * columns,
            transcendentals=0,
            bytes_accessed=2 * (2 * tokens + height // 2) * columns + 2 * tokens * height,
        ),
    )(behind(places, replicas - 1, *after), left, left_far, *rights)


def sum_plane(total):
    return lax.psum_scatter(total, "rep", scatter_dimension=0)


def sum_levels(plane):
    shards = lax.axis_size("shard")
    pairs = [list(range(core, shards, 2)) for core in range(2)]
    return lax.psum_scatter(plane, "shard", scatter_dimension=0, axis_index_groups=pairs)


def tie_kernel(block, other, out):
    del block, other, out


def tied(block, other):
    any_space = pl.BlockSpec(memory_space=pl.ANY)
    return pl.pallas_call(
        tie_kernel,
        out_shape=jax.ShapeDtypeStruct(block.shape, block.dtype),
        in_specs=[any_space] * 2,
        out_specs=any_space,
        input_output_aliases={0: 0},
        compiler_params=pltpu.CompilerParams(has_side_effects=True),
    )(block, other)


def add_slabs(target, *terms):
    rows = target.shape[0]
    slab = min(32, rows)

    @pl.loop(0, rows // slab)
    def _(n):
        at = pl.ds(pl.multiple_of(n * slab, slab), slab)
        target[at] = sum(term[at].astype(jnp.float32) for term in terms).astype(target.dtype)


def sum_kernel(levels, replicas, kinds, counts, *refs):
    bits = replicas.bit_length() - 1
    r, s = lax.axis_index("rep"), lax.axis_index("shard")
    core, z = lax.rem(s, 2), lax.div(s, 2)
    other = {"shard": s + 1 - 2 * core}
    ring_to = {"shard": lax.rem(s + 2, 2 * levels)}
    ring_from = {"shard": lax.rem(s + 2 * levels - 2, 2 * levels)}
    rep_to = [{"rep": r ^ jnp.where(core == 0, 1 << bit_of(n, 0), 1 << bit_of(n, 1))} for n in range(bits)]
    lists = mask_lists()
    place = [jnp.where(core == 0, a, b) ^ r for a, b in zip(*lists)]
    ins, outs, scratch = [], [], []
    at = 0
    for kind in kinds:
        size = 2 if kind == "full" else 1
        ins.append(refs[at : at + size])
        at += size
    outs = refs[at : at + len(kinds)]
    at += len(kinds)
    for count in counts:
        scratch.append(refs[at : at + count])
        at += count
    crowd = []
    if "vectors" in kinds:
        crowd = [{"shard": s ^ (1 << n)} for n in range((2 * levels).bit_length() - 1)]
        crowd += [{"rep": r ^ (1 << n)} for n in range(bits)]
    barrier = pltpu.get_barrier_semaphore()
    partners = [ring_to, ring_from, other] + rep_to + crowd
    for partner in partners:
        pl.semaphore_signal(barrier, inc=1, device_id=partner, device_id_type=MESH_ID)
    pl.semaphore_wait(barrier, len(partners))

    level = [lax.rem(z + 2 * levels - 1 - i, levels) for i in range(levels)]
    sent = []

    def remote(source, target, sends, recvs, n, device):
        return pltpu.make_async_remote_copy(
            src_ref=source,
            dst_ref=target,
            send_sem=sends.at[n],
            recv_sem=recvs.at[n],
            device_id=device,
            device_id_type=MESH_ID,
        )

    def start(copy):
        copy.start()
        sent.append(copy)

    def offset(step):
        return replicas - (replicas >> step)

    class Job:
        def __init__(self, kind, ins, out, scratch):
            self.kind, self.ins, self.out = kind, ins, out
            self.held, self.came, self.ring = scratch[:3]
            self.load_sem, self.send_sem, self.recv_sem = scratch[3:6]
            self.ring_send, self.ring_recv, self.rep_send, self.rep_recv, self.own_sem = scratch[6:]

        def load(self, i, k=0):
            if self.kind == "pairs":
                source = self.ins[0].at[2 * level[i] + core]
            elif self.kind == "full":
                source = self.ins[0].at[k, level[i]]
            elif self.kind == "plane":
                source = self.ins[0].at[level[i]]
            else:
                source = self.ins[0].at[0]
            slots = self.held.shape[1]
            return pltpu.make_async_copy(source, self.held.at[i, k], self.load_sem.at[i * slots + k])

        def loads(self):
            return [(i, k) for i in range(self.held.shape[0]) for k in range(self.held.shape[1])]

        def exchange(self, i, step, k):
            n = i * self.came.shape[1] + offset(step) + k
            target = self.came.at[i, offset(step) + k]
            if self.kind == "pairs":
                source, device = self.ins[0].at[2 * level[i] + 1 - core], other
            else:
                device = rep_to[step]
                source = self.ins[1].at[k, level[i]] if step == 0 else self.held.at[i, (replicas >> (step + 1)) + k]
            return remote(source, target, self.send_sem, self.recv_sem, n, device)

        def ring_copy(self, i):
            return remote(self.held.at[i, 0], self.ring.at[i], self.ring_send, self.ring_recv, i, ring_to)

        def rep_copy(self, step, n):
            piece = self.out.at[place[n]]
            source = self.held.at[self.held.shape[0] - 1, 0] if n == 0 else piece
            return remote(source, piece, self.rep_send, self.rep_recv, (1 << step) + n, rep_to[step])

        def begin(self):
            for i, k in self.loads():
                self.load(i, k).start()
            if self.kind in ("pairs", "full"):
                slots = 1 if self.kind == "pairs" else replicas // 2
                for i in range(levels):
                    for k in range(slots):
                        start(self.exchange(i, 0, k))

        def halve(self, i, step):
            if self.kind != "full":
                return
            half = replicas >> (step + 1)
            if step == 0:
                for k in range(replicas // 2):
                    self.load(i, k).wait()
            for k in range(half):
                self.exchange(i, step, k).wait_recv()
            if step + 1 < bits:
                for k in range(half // 2, half):
                    held = self.held.at[i, k]
                    add_slabs(held, held, *[self.came.at[i, offset(n) + k] for n in range(step + 1)])
                    start(self.exchange(i, step + 1, k - half // 2))

        def forward(self, i):
            held = self.held.at[i, 0]
            terms = [held]
            if self.kind == "full":
                terms += [self.came.at[i, offset(n)] for n in range(bits)]
            else:
                self.load(i).wait()
            if self.kind == "pairs":
                self.exchange(i, 0, 0).wait_recv()
                terms.append(self.came.at[i, 0])
            if i > 0:
                self.ring_copy(i - 1).wait_recv()
                terms.append(self.ring.at[i - 1])
            if len(terms) > 1:
                add_slabs(held, *terms)
            if i < levels - 1:
                start(self.ring_copy(i))
            else:
                self.finish()

        def own_out(self):
            target = self.out if self.kind == "pairs" else self.out.at[r]
            final = self.held.at[self.held.shape[0] - 1, 0]
            return pltpu.make_async_copy(final, target, self.own_sem.at[0])

        def finish(self):
            self.own_out().start()
            if self.kind != "pairs":
                for step in range(bits):
                    start(self.rep_copy(step, 0))

        def spread(self, got):
            if self.kind == "pairs":
                return
            for n in range(1 << got):
                self.rep_copy(got, n).wait_recv()
                for step in range(got + 1, bits):
                    start(self.rep_copy(step, (1 << got) + n))

    class Vectors:
        def __init__(self, kind, ins, out, scratch):
            self.kind, self.out = kind, out
            self.held, self.came, self.load_sem, self.send_sem, self.recv_sem, own_sem = scratch
            self.first = pltpu.make_async_copy(ins[0], self.held.at[0], self.load_sem.at[0])
            self.final = pltpu.make_async_copy(self.held.at[len(crowd)], out, own_sem.at[0])
            self.done = 0

        def begin(self):
            self.first.start()

        def exchange(self, n):
            return remote(
                self.held.at[n], self.came.at[n], self.send_sem, self.recv_sem, n, crowd[n]
            )

        def go_on(self):
            n = self.done
            if n > len(crowd):
                return
            if n == 0:
                self.first.wait()
            else:
                self.exchange(n - 1).wait_recv()
                self.held[n] = self.held[n - 1] + self.came[n - 1]
            if n < len(crowd):
                start(self.exchange(n))
            else:
                self.final.start()
            self.done += 1

        def own_out(self):
            return self.final

    jobs = [
        (Vectors if parts[0] == "vectors" else Job)(*parts)
        for parts in zip(kinds, ins, outs, scratch)
    ]
    for job in jobs:
        job.begin()
    plain_jobs = [job for job in jobs if job.kind in ("pairs", "plane")]
    full_jobs = [job for job in jobs if job.kind == "full"]
    vector_jobs = [job for job in jobs if job.kind == "vectors"]
    spread_jobs = [job for job in jobs if job.kind == "spread"]
    for job in plain_jobs:
        job.forward(0)
    for job in spread_jobs:
        job.load(0).wait()
        job.finish()
    for i in range(levels):
        for job in vector_jobs:
            job.go_on()
        if i + 1 < levels:
            for job in plain_jobs:
                job.forward(i + 1)
        for job in full_jobs:
            job.halve(i, 0)
        if i > 0 and i <= bits:
            for job in spread_jobs:
                job.spread(i - 1)
        for step in range(1, bits):
            for job in full_jobs:
                job.halve(i, step)
        for job in full_jobs:
            job.forward(i)
    for got in range(bits):
        late = [job for job in spread_jobs if got >= levels - 1]
        for job in plain_jobs + full_jobs + late:
            job.spread(got)
        for job in vector_jobs:
            job.go_on()
    for job in vector_jobs:
        while job.done <= len(crowd):
            job.go_on()
    for copy in sent:
        copy.wait_send()
    for job in jobs:
        job.own_out().wait()


def sum_arrays(jobs, collective_id):
    replicas, shards = lax.axis_size("rep"), lax.axis_size("shard")
    levels = shards // 2
    dma = pltpu.SemaphoreType.DMA
    any_space = pl.BlockSpec(memory_space=pl.ANY)
    scratch, counts, out_shape, size, total = [], [], [], 0, 0
    exchanges = (shards * replicas).bit_length() - 1
    for kind, arrays in jobs:
        block = arrays[0].shape[-2:]
        dtype = arrays[0].dtype
        total += sum(array.size for array in arrays)
        if kind == "vectors":
            own = [
                pltpu.VMEM((exchanges + 1,) + block, dtype),
                pltpu.VMEM((exchanges,) + block, dtype),
                dma((1,)),
                dma((exchanges,)),
                dma((exchanges,)),
                dma((1,)),
            ]
            scratch += own
            counts.append(len(own))
            size += 4 * block[0] * block[1] * (2 * exchanges + 1)
            out_shape.append(jax.ShapeDtypeStruct(block, dtype))
            continue
        slots = replicas // 2 if kind == "full" else 1
        chunks = 1 if kind == "spread" else levels
        came = {"pairs": 1, "full": replicas - 1}.get(kind, 0)
        own = [
            pltpu.VMEM((chunks, slots) + block, dtype),
            pltpu.VMEM((levels, came) + block if came else (16, 128), dtype),
            pltpu.VMEM((levels - 1,) + block if kind != "spread" else (16, 128), dtype),
            dma((levels * slots,)),
            dma((levels * max(came, 1),)),
            dma((levels * max(came, 1),)),
            dma((levels,)),
            dma((levels,)),
            dma((replicas,)),
            dma((replicas,)),
            dma((1,)),
        ]
        scratch += own
        counts.append(len(own))
        size += 2 * block[0] * block[1] * (chunks * (slots + came) + chunks - 1)
        out_shape.append(jax.ShapeDtypeStruct(block if kind == "pairs" else (replicas,) + block, dtype))
    kinds = tuple(kind for kind, _ in jobs)
    operands = [array for _, arrays in jobs for array in arrays]
    return pl.pallas_call(
        functools.partial(sum_kernel, levels, replicas, kinds, tuple(counts)),
        out_shape=out_shape,
        in_specs=[any_space] * len(operands),
        out_specs=[any_space] * len(jobs),
        scratch_shapes=scratch,
        compiler_params=pltpu.CompilerParams(
            collective_id=collective_id, has_side_effects=True, vmem_limit_bytes=size + (4 << 20)
        ),
        cost_estimate=pl.CostEstimate(flops=total, transcendentals=0, bytes_accessed=20 * total),
    )(*operands)


def sum_along(block, axis):
    size = lax.axis_size(axis)
    step = 1
    while step < size:
        block = block + lax.ppermute(block, axis, [(n, n ^ step) for n in range(size)])
        step *= 2
    return block


def per_device(
    x_prompt,
    x_cont,
    teacher_prompt,
    teacher_cont,
    valid_mask,
    group_of,
    ln1_gain,
    ln1_bias,
    w_qkv,
    q_bias,
    v_bias,
    w_out,
    out_bias,
    ln2_gain,
    ln2_bias,
    w_up,
    up_bias,
    w_down,
    down_bias,
):
    shards = lax.axis_size("shard")
    replicas = lax.axis_size("rep")
    shard_index = lax.axis_index("shard")
    prompt_count, prompt_rows, width = x_prompt.shape
    cont_rows = x_cont.shape[0]
    cont_count, cont_len = valid_mask.shape
    prompt_len = prompt_rows * shards
    prompt_total = prompt_count * prompt_rows
    head_count = width // HEAD_DIM
    all_tokens = replicas * shards * (prompt_total + cont_rows)
    valid_local = jnp.sum(valid_mask.astype(jnp.float32)) + prompt_total
    vectors = (
        ln1_gain,
        ln1_bias,
        q_bias,
        v_bias,
        out_bias,
        ln2_gain,
        ln2_bias,
        up_bias,
        down_bias,
    )
    starts = [0]
    for vector in vectors:
        starts.append(starts[-1] + vector.shape[0])
    filled = -(starts[-1] + 1) % 1024
    joint = jnp.concatenate(
        [vector.astype(jnp.float32) for vector in vectors]
        + [valid_local[None], jnp.zeros((filled,), jnp.float32)]
    ).reshape(8, -1)
    levels = shards // 2
    steps = range(1, levels)
    ahead = (levels - 1) * 2 // 3
    first_units = [(m, j, True, True) for j in steps for m in (2, 0, 1)]
    first_units += [(3, j, True, False) for j in steps if j <= ahead]
    q_full, kv_full, joint, up_begun = gather_rows(
        [w_qkv[:, :width], w_qkv[:, width:], joint, w_up],
        (True, True, False, True),
        (True, True, True, False),
        first_units,
        0,
    )
    q_full, kv_full = plain(q_full), plain(kv_full)
    joint = joint.reshape(shards, -1)
    (
        gain_one,
        shift_one,
        bias_query,
        bias_value,
        bias_out,
        gain_two,
        shift_two,
        bias_up,
        bias_down,
    ) = [joint[:, begin:end].reshape(-1) for begin, end in zip(starts[:-1], starts[1:])]
    valid_group = jnp.broadcast_to(jnp.sum(joint[:, starts[-1]]), (8, 128))
    valid_all = sum_along(valid_group, "rep")[0, 0]
    loss_scale = all_tokens / valid_all
    inputs = jnp.concatenate([x_prompt.reshape(prompt_total, width), x_cont], axis=0).astype(
        jnp.float32
    )
    normed, unit_one, inverse_one = norm_forward(inputs, gain_one, shift_one)
    normed_low = normed.astype(jnp.bfloat16)
    queries = jnp.dot(normed_low, q_full, preferred_element_type=jnp.float32)
    queries = (queries + bias_query).astype(jnp.bfloat16)
    pair_bias = jnp.concatenate([jnp.zeros_like(bias_value), bias_value])
    pair_rows = jnp.dot(normed_low, kv_full, preferred_element_type=jnp.float32)
    pair_rows = (pair_rows + pair_bias).astype(jnp.bfloat16)
    local_pairs = pair_rows[:prompt_total].reshape(prompt_count, prompt_rows, 2 * width)
    own_pairs = pair_rows[prompt_total:]
    second_units = [(2, j, False, True) for j in steps if j <= ahead]
    for j in steps:
        second_units += [(1, j, True, True), (3, j, True, True)]
        if j > ahead:
            second_units.append((2, j, True, True))
        second_units.append((0, j, True, True))
    prompt_pairs, out_full, up_full, down_full = gather_rows(
        [local_pairs, w_out, w_up, w_down],
        (False, True, True, True),
        (True, True, True, True),
        second_units,
        1,
        {2: up_begun},
    )
    out_full, up_full, down_full = plain(out_full), plain(up_full), plain(down_full)
    sizes = (prompt_count, prompt_rows, cont_count, cont_len)
    places = jnp.concatenate([(shard_index * prompt_rows)[None], group_of]).astype(jnp.int32)
    joined_rows = (queries, own_pairs)
    attended, log_totals = attention_call(sizes, joined_rows, prompt_pairs, places)
    middle = inputs + jnp.dot(attended, out_full, preferred_element_type=jnp.float32) + bias_out
    normed_two, unit_two, inverse_two = norm_forward(middle, gain_two, shift_two)
    normed_two_low = normed_two.astype(jnp.bfloat16)
    upward = jnp.dot(normed_two_low, up_full, preferred_element_type=jnp.float32) + bias_up
    squared = upward * upward
    bend = jnp.tanh(gelu_coef * upward * (1.0 + 0.044715 * squared))
    half = 0.5 * (1.0 + bend)
    active_low = (upward * half).astype(jnp.bfloat16)
    rise = gelu_coef * (1.0 + 3.0 * 0.044715 * squared)
    gelu_slope = (half + 0.5 * upward * (1.0 - bend * bend) * rise).astype(jnp.bfloat16)
    result = middle + jnp.dot(active_low, down_full, preferred_element_type=jnp.float32) + bias_down
    out_prompt = (
        result[:prompt_total].reshape(prompt_count, prompt_rows, width).astype(jnp.bfloat16)
    )
    out_cont = result[prompt_total:].astype(jnp.bfloat16)
    targets = jnp.concatenate(
        [teacher_prompt.reshape(prompt_total, width), teacher_cont], axis=0
    ).astype(jnp.float32)
    weight_rows = jnp.concatenate(
        [jnp.ones((prompt_total,), jnp.float32), valid_mask.reshape(cont_rows).astype(jnp.float32)]
    )
    out_grad = (loss_scale * weight_rows)[:, None] * (result - targets)
    mlp_grad = out_grad.astype(jnp.bfloat16)
    grad_bias_down = jnp.sum(mlp_grad, axis=0, dtype=jnp.float32)
    down_total = chip_gradient(active_low, [mlp_grad[None]], halves=False)
    down_plane = sum_plane(down_total)
    active_grad = back_product(kept_behind(mlp_grad, down_total), down_full)
    upward_grad = (active_grad * gelu_slope.astype(jnp.float32)).astype(jnp.bfloat16)
    grad_bias_up = jnp.sum(upward_grad, axis=0, dtype=jnp.float32)
    up_total = chip_gradient(normed_two_low, [upward_grad[None]], halves=False)
    up_plane = sum_plane(up_total)
    normed_two_grad = back_product(upward_grad, up_full)
    middle_step, grad_gain_two, grad_shift_two = norm_backward(
        normed_two_grad, unit_two, inverse_two, gain_two
    )
    middle_grad = out_grad + middle_step
    branch_grad = middle_grad.astype(jnp.bfloat16)
    grad_bias_out = jnp.sum(branch_grad, axis=0, dtype=jnp.float32)
    attended_grad = back_product(branch_grad, out_full).astype(jnp.bfloat16)
    later_places = places
    query_part, pair_grad, own_grad = attention_call(
        sizes, joined_rows, prompt_pairs, later_places, (log_totals, attended_grad)
    )
    down_owned = sum_levels(tied(down_plane, query_part))
    out_total = chip_gradient(attended, [branch_grad[None]])
    q_total = chip_gradient(normed_low, [query_part[None]], after=[up_total])
    near_grad = back_product(query_part, q_full)
    cont_grad = near_grad[prompt_total:]
    for n in range(2):
        cont_grad = cont_grad + back_product(own_grad[n], kv_full[:, n * width : (n + 1) * width])
    cont_step, cont_gain, cont_shift = norm_backward(
        cont_grad, unit_one[prompt_total:], inverse_one[prompt_total:], gain_one
    )
    grad_cont = middle_grad[prompt_total:] + cont_step
    pair_sums = tied(pair_grad.reshape(shards, -1, width), grad_cont)
    owned_pairs, out_parts, q_parts = sum_arrays(
        [
            ("pairs", [pair_sums]),
            ("full", out_total),
            ("full", q_total),
        ],
        2,
    )
    owned_grad = owned_pairs.reshape(2, prompt_total, width)
    pair_total = chip_gradient(normed_low, [owned_grad, own_grad])
    grad_bias_query = jnp.sum(query_part, axis=0, dtype=jnp.float32)
    grad_bias_value = jnp.sum(owned_grad[1], axis=0, dtype=jnp.float32)
    grad_bias_value = grad_bias_value + jnp.sum(own_grad[1], axis=0, dtype=jnp.float32)
    prompt_grad = near_grad[:prompt_total]
    for n in range(2):
        prompt_grad = prompt_grad + back_product(
            owned_grad[n], kv_full[:, n * width : (n + 1) * width]
        )
    prompt_step, prompt_gain, prompt_shift = norm_backward(
        prompt_grad, unit_one[:prompt_total], inverse_one[:prompt_total], gain_one
    )
    grad_gain_one, grad_shift_one = prompt_gain + cont_gain, prompt_shift + cont_shift
    grad_prompt = middle_grad[:prompt_total] + prompt_step
    grad_prompt = grad_prompt.reshape(prompt_count, prompt_rows, width)
    vector_grads = (
        grad_gain_one,
        grad_shift_one,
        grad_bias_query,
        grad_bias_value,
        grad_bias_out,
        grad_gain_two,
        grad_shift_two,
        grad_bias_up,
        grad_bias_down,
    )
    joint_grads = jnp.concatenate([vector.reshape(shards, -1) for vector in vector_grads], axis=1)
    pair_parts, down_parts, up_parts, joint_sums = sum_arrays(
        [
            ("full", pair_total),
            ("spread", [down_owned[None]]),
            ("plane", [up_plane]),
            ("vectors", [joint_grads]),
        ],
        3,
    )
    summed_down, summed_up, summed_out = [
        plain(parts).astype(jnp.float32) for parts in (down_parts, up_parts, out_parts)
    ]
    summed_qkv = jnp.concatenate([plain(q_parts), plain(pair_parts)], axis=1).astype(jnp.float32)
    own_sums = lax.dynamic_index_in_dim(joint_sums, shard_index, 0, keepdims=False)
    owned_vectors = [own_sums[begin:end] for begin, end in zip(starts[:-1], starts[1:])]
    return (
        out_prompt,
        out_cont,
        grad_prompt,
        grad_cont,
        owned_vectors[0],
        owned_vectors[1],
        summed_qkv,
        owned_vectors[2],
        owned_vectors[3],
        summed_out,
        owned_vectors[4],
        owned_vectors[5],
        owned_vectors[6],
        summed_up,
        owned_vectors[7],
        summed_down,
        owned_vectors[8],
    )


def solution(mesh):
    in_specs = (
        P("rep", "shard", None),
        P(("rep", "shard"), None),
        P("rep", "shard", None),
        P(("rep", "shard"), None),
        P(("rep", "shard"), None),
        P(("rep", "shard")),
        P("shard"),
        P("shard"),
        P("shard", None),
        P("shard"),
        P("shard"),
        P("shard", None),
        P("shard"),
        P("shard"),
        P("shard"),
        P("shard", None),
        P("shard"),
        P("shard", None),
        P("shard"),
    )
    out_specs = (
        P("rep", "shard", None),
        P(("rep", "shard"), None),
        P("rep", "shard", None),
        P(("rep", "shard"), None),
        P("shard"),
        P("shard"),
        P("shard", None),
        P("shard"),
        P("shard"),
        P("shard", None),
        P("shard"),
        P("shard"),
        P("shard"),
        P("shard", None),
        P("shard"),
        P("shard", None),
        P("shard"),
    )
    return jax.shard_map(
        per_device, mesh=mesh, in_specs=in_specs, out_specs=out_specs, check_vma=False
    )
```
